32 devices in a mesh: dp: 16 (over z, x, core), tensor: 2 (over y).
Axes of the slice: x: 2, y: 2, z: 4, core: 2. Of those that a mesh axis runs over, the one named last changes fastest.
Arguments:
- tokens: bfloat16 [8192, 1536], P(('dp', 'tensor')), may hold values from -16 to 16
- w_query: bfloat16 [1536, 1536], P('dp', 'tensor'), may hold values from -0.15625 to 0.15625
- key_weight: bfloat16 [1536, 256], P('dp', 'tensor'), may hold values from -0.15625 to 0.15625
- value_weight: bfloat16 [1536, 256], P('dp', 'tensor'), may hold values from -0.15625 to 0.15625
- b_query: bfloat16 [1536], P('tensor'), may hold values from -3 to 3
- key_bias: bfloat16 [256], P('tensor'), may hold values from -3 to 3
- value_bias: bfloat16 [256], P('tensor'), may hold values from -3 to 3
- w_out: bfloat16 [1536, 1536], P('tensor', 'dp'), may hold values from -1.75 to 1.75
- gain_attn: bfloat16 [1536], replicated, may hold values from 0.5 to 1.5
- gain_mlp: bfloat16 [1536], replicated, may hold values from 0.5 to 1.5
- w_gate: bfloat16 [1536, 8960], P('dp', 'tensor'), may hold values from -0.15625 to 0.15625
- w_up: bfloat16 [1536, 8960], P('dp', 'tensor'), may hold values from -0.15625 to 0.15625
- w_down: bfloat16 [8960, 1536], P('tensor', 'dp'), may hold values from -0.0625 to 0.0625
- cotangent: bfloat16 [8192, 1536], P(('dp', 'tensor')), may hold values from -6 to 6
Outputs:
- mixed: bfloat16 [8192, 1536], P(('dp', 'tensor'))
- grad_tokens: float32 [8192, 1536], P(('dp', 'tensor'))
- grad_w_query: float32 [1536, 1536], P('dp', 'tensor')
- grad_w_key: float32 [1536, 256], P('dp', 'tensor')
- grad_w_value: float32 [1536, 256], P('dp', 'tensor')
- grad_b_query: float32 [1536], P('tensor')
- grad_b_key: float32 [256], P('tensor')
- grad_b_value: float32 [256], P('tensor')
- grad_w_out: float32 [1536, 1536], P('tensor', 'dp')
- grad_gain_attn: float32 [1536], replicated
- grad_gain_mlp: float32 [1536], replicated
- grad_w_gate: float32 [1536, 8960], P('dp', 'tensor')
- grad_w_up: float32 [1536, 8960], P('dp', 'tensor')
- grad_w_down: float32 [8960, 1536], P('tensor', 'dp')
The draws below stay inside these ranges and needn't reach their ends.
All inputs are finite; a program needn't handle non-finite values.
Results may differ from the reference program's by a relative error of at most 0.018.
Values may be sent and summed in bfloat16 or wider, within the bound.
A program may use at most 192 MiB of HBM per device.

```python
import math
import jax
import jax.numpy as jnp
from jax import lax

MODEL_WIDTH = 1536
QUERY_HEADS = 12
KEY_VALUE_HEADS = 2
HEAD_SIZE = 128
FF = 8960
SEQUENCE_TOKENS = 512
SEQUENCE_COUNT = 1
TOK_DEV = 512
TOKENS = 8192
N_DP = 16


def draw_tokens(key, part):
    key = jax.random.fold_in(key, 11)
    row_key = jax.random.fold_in(key, 0)
    entry_key = jax.random.fold_in(key, 2)
    row_scale = jnp.exp(jax.random.uniform(row_key, (TOKENS, 1), jnp.float32, math.log(0.4), math.log(4.0)))
    entries = jnp.clip(jax.random.normal(entry_key, (TOKENS, MODEL_WIDTH), jnp.float32), -4.0, 4.0)
    return (entries * row_scale).astype(jnp.bfloat16)


def draw_cotangent(key, part):
    key = jax.random.fold_in(key, 23)
    ramp = 0.5 + jnp.arange(TOKENS, dtype=jnp.float32)[:, None] / (TOKENS - 1)
    return (jnp.clip(jax.random.normal(key, (TOKENS, MODEL_WIDTH), jnp.float32), -4.0, 4.0) * ramp).astype(jnp.bfloat16)


def block_scale(stream_key, dims, shards, smallest, top_value):
    factor_of = 1.0
    for position, blocks in shards:
        draws = jax.random.uniform(jax.random.fold_in(jax.random.fold_in(stream_key, 6), position), (blocks,), jnp.float32, smallest / len(shards), top_value / len(shards))
        factor_of = factor_of * jnp.repeat(jnp.exp(draws), dims[position] // blocks).reshape((-1,) + (1,) * (len(dims) - 1 - position))
    return factor_of


def scatter_about(stream_key, shape, width, bound, cuts=(), kind=jnp.bfloat16):
    values = jax.random.normal(stream_key, shape, jnp.float32) * width
    if len(cuts) > 0:
        values = block_scale(stream_key, shape, cuts, -0.22, 0.18) * values
    return jnp.clip(values, min=-bound, max=bound).astype(kind)


def setup_inputs(seed: int = 0) -> dict:
    arg_keys = jax.random.split(jax.random.key(seed), 15)
    tokens = draw_tokens(jax.random.fold_in(arg_keys[14], 71), 0)
    w_query = scatter_about(arg_keys[1], (MODEL_WIDTH, QUERY_HEADS * HEAD_SIZE), MODEL_WIDTH ** -0.5, 0.15625, ((0, 16), (1, 2)))
    key_weight = scatter_about(arg_keys[2], (MODEL_WIDTH, KEY_VALUE_HEADS * HEAD_SIZE), MODEL_WIDTH ** -0.5, 0.15625, ((0, 16), (1, 2)))
    value_weight = scatter_about(arg_keys[3], (MODEL_WIDTH, KEY_VALUE_HEADS * HEAD_SIZE), MODEL_WIDTH ** -0.5, 0.15625, ((0, 16), (1, 2)))
    b_query = scatter_about(arg_keys[4], (QUERY_HEADS * HEAD_SIZE,), 0.5, 3.0, ((0, 2),))
    key_bias = scatter_about(arg_keys[5], (KEY_VALUE_HEADS * HEAD_SIZE,), 0.5, 3.0, ((0, 2),))
    value_bias = scatter_about(arg_keys[6], (KEY_VALUE_HEADS * HEAD_SIZE,), 0.5, 3.0, ((0, 2),))
    w_out = scatter_about(arg_keys[7], (QUERY_HEADS * HEAD_SIZE, MODEL_WIDTH), (QUERY_HEADS * HEAD_SIZE * 4 // SEQUENCE_TOKENS) ** -0.5, 1.75, ((0, 2), (1, 16)))
    gain_attn = jnp.clip(1.0 + 0.1 * jax.random.normal(arg_keys[8], (MODEL_WIDTH,), jnp.float32), 0.5, 1.5).astype(jnp.bfloat16)
    gain_mlp = jnp.clip(1.0 + 0.1 * jax.random.normal(arg_keys[9], (MODEL_WIDTH,), jnp.float32), 0.5, 1.5).astype(jnp.bfloat16)
    w_gate = scatter_about(arg_keys[10], (MODEL_WIDTH, FF), MODEL_WIDTH ** -0.5, 0.15625, ((0, 16), (1, 2)))
    w_up = scatter_about(arg_keys[11], (MODEL_WIDTH, FF), MODEL_WIDTH ** -0.5, 0.15625, ((0, 16), (1, 2)))
    w_down = scatter_about(arg_keys[12], (FF, MODEL_WIDTH), FF ** -0.5, 0.0625, ((0, 2), (1, 16)))
    cotangent = draw_cotangent(jax.random.fold_in(arg_keys[14], 71), 0)
    return dict(tokens=tokens, w_query=w_query, key_weight=key_weight, value_weight=value_weight, b_query=b_query, key_bias=key_bias, value_bias=value_bias, w_out=w_out, gain_attn=gain_attn, gain_mlp=gain_mlp, w_gate=w_gate, w_up=w_up, w_down=w_down, cotangent=cotangent)


norm_eps = 1e-06
rope_base = 1000000.0
highest = lax.Precision.HIGHEST

@jax.custom_vjp
def low(v):
    return lax.optimization_barrier(v.astype(jnp.bfloat16)).astype(jnp.float32)

@jax.custom_vjp
def lowered_backward(v):
    return v

def low_keep(v):
    return (low(v), None)

def low_pass(kept, grad):
    return (grad,)

def back_keep(v):
    return (v, None)

def back_low(kept, grad):
    return (low(grad),)
low.defvjp(low_keep, low_pass)
lowered_backward.defvjp(back_keep, back_low)

def rotate(values):
    midway = values.shape[-1] // 2
    return jnp.concatenate([-values[..., midway:], values[..., :midway]], axis=-1)

def rope_tables(length, columns):
    midway = columns // 2
    inverse = jnp.exp(jnp.arange(midway, dtype=jnp.float32) * (-2.0 * math.log(rope_base) / columns))
    angles = jnp.arange(length, dtype=jnp.float32)[:, None] * inverse[None, :]
    angles = jnp.concatenate([angles, angles], axis=-1)
    return (jnp.cos(angles)[None, :, None, :], jnp.sin(angles)[None, :, None, :])

def matrix_multiply(left, right):
    return jnp.dot(left, right, precision=highest, preferred_element_type=jnp.float32)

def rms_norm(values, gain):
    return values * lax.rsqrt(lax.optimization_barrier(jnp.mean(values * values, axis=-1, keepdims=True)) + norm_eps) * gain

def layer(params, inputs):
    w_query, key_weight, value_weight, b_query, key_bias, value_bias, w_out, gain_attn, gain_mlp, w_gate, w_up, w_down = params
    cosine, sine = rope_tables(SEQUENCE_TOKENS, HEAD_SIZE)
    factor = 1.0 / math.sqrt(HEAD_SIZE)
    normed_attention = low(rms_norm(inputs, gain_attn))
    query_lin = lowered_backward(matrix_multiply(normed_attention, w_query) + b_query).reshape(SEQUENCE_COUNT, SEQUENCE_TOKENS, QUERY_HEADS, HEAD_SIZE)
    key_linear = lowered_backward(matrix_multiply(normed_attention, key_weight) + key_bias).reshape(SEQUENCE_COUNT, SEQUENCE_TOKENS, KEY_VALUE_HEADS, HEAD_SIZE)
    value_linear = lowered_backward(matrix_multiply(normed_attention, value_weight) + value_bias).reshape(SEQUENCE_COUNT, SEQUENCE_TOKENS, KEY_VALUE_HEADS, HEAD_SIZE)
    query_matrix = low(query_lin * cosine + rotate(query_lin) * sine)
    keys = low(key_linear * cosine + rotate(key_linear) * sine)
    values = low(value_linear)
    grouped_heads = query_matrix.reshape(SEQUENCE_COUNT, SEQUENCE_TOKENS, KEY_VALUE_HEADS, QUERY_HEADS // KEY_VALUE_HEADS, HEAD_SIZE)
    scores = lowered_backward(jnp.einsum('bsjgd,btjd->bjgst', grouped_heads, keys, precision=highest) * factor)
    causal = jnp.arange(SEQUENCE_TOKENS)[:, None] >= jnp.arange(SEQUENCE_TOKENS)[None, :]
    scores = jnp.where(causal, scores, -1e+30)
    largest = lax.optimization_barrier(jnp.max(scores, axis=-1, keepdims=True))
    exponent = jnp.exp(scores - largest)
    probs = exponent / lax.optimization_barrier(jnp.sum(exponent, axis=-1, keepdims=True))
    mixed_heads = low(lowered_backward(jnp.einsum('bjgst,btjd->bsjgd', low(probs), values, precision=highest)))
    attended = matrix_multiply(mixed_heads.reshape(TOK_DEV, QUERY_HEADS * HEAD_SIZE), w_out)
    middle = inputs + lowered_backward(attended)
    normed_mlp = low(rms_norm(middle, gain_mlp))
    gate = lowered_backward(matrix_multiply(normed_mlp, w_gate))
    upper = lowered_backward(matrix_multiply(normed_mlp, w_up))
    hidden = low(jax.nn.silu(gate) * upper)
    return middle + lowered_backward(matrix_multiply(hidden, w_down))

def add_pair(first, second):
    return first + second

def reference(tokens, w_query, key_weight, value_weight, b_query, key_bias, value_bias, w_out, gain_attn, gain_mlp, w_gate, w_up, w_down, cotangent):
    params = tuple((weight.astype(jnp.float32) for weight in (w_query, key_weight, value_weight, b_query, key_bias, value_bias, w_out, gain_attn, gain_mlp, w_gate, w_up, w_down)))
    blocks = tokens.astype(jnp.float32).reshape(N_DP, TOK_DEV, MODEL_WIDTH)
    upstream = cotangent.astype(jnp.float32).reshape(N_DP, TOK_DEV, MODEL_WIDTH)
    totals = jax.tree.map(jnp.zeros_like, params)

    def step(carry, pair):
        inputs, grad_out = pair
        output, pullback = jax.vjp(layer, params, inputs)
        param_grads, input_grad = pullback(grad_out)
        return (jax.tree.map(add_pair, carry, param_grads), (output, input_grad))
    totals, (outputs, input_grads) = lax.scan(step, totals, (blocks, upstream))
    mixed = outputs.reshape(TOKENS, MODEL_WIDTH).astype(jnp.bfloat16)
    grad_tokens = input_grads.reshape(TOKENS, MODEL_WIDTH)
    return (mixed, grad_tokens, totals[0], totals[1], totals[2], totals[3], totals[4], totals[5], totals[6], totals[7], totals[8], totals[9], totals[10], totals[11])
```

```python
import math

import jax
import jax.numpy as jnp
from jax import lax
from jax.experimental import pallas as pl
from jax.experimental.pallas import tpu as pltpu
from jax.sharding import PartitionSpec as P

QUERY_HEADS = 12
KEY_VALUE_HEADS = 2
HEAD_SIZE = 128
SEQUENCE_TOKENS = 512

QUADS = 4
WIDE = 256

norm_eps = 1e-06
rope_base = 1000000.0
BF = jnp.bfloat16
F32 = jnp.float32
MESH = pl.DeviceIdType.MESH


def rotate(values):
    midway = values.shape[-1] // 2
    return jnp.concatenate([-values[..., midway:], values[..., :midway]], axis=-1)


def rope_tables(length, columns):
    midway = columns // 2
    inverse = jnp.exp(
        jnp.arange(midway, dtype=jnp.float32) * (-2.0 * math.log(rope_base) / columns)
    )
    angles = jnp.arange(length, dtype=jnp.float32)[:, None] * inverse[None, :]
    angles = jnp.concatenate([angles, angles], axis=-1)
    return (jnp.cos(angles)[None, :, None, :], jnp.sin(angles)[None, :, None, :])


def rms_scale(values):
    return lax.rsqrt(jnp.mean(values * values, axis=-1, keepdims=True) + norm_eps)


def norm_back(values, scale, gain, upstream):
    scaled = upstream * gain
    return scale * scaled - values * (scale * scale * scale) * jnp.mean(
        scaled * values, axis=-1, keepdims=True
    )


def dot_rows(left, right):
    return jnp.dot(left, right, preferred_element_type=F32)


def dot_left(left, right):
    return lax.dot_general(left, right, (((0,), (0,)), ((), ())), preferred_element_type=F32)


def dot_right(left, right):
    return lax.dot_general(left, right, (((1,), (1,)), ((), ())), preferred_element_type=F32)


def round_up(value, step):
    return (value + step - 1) // step * step


class Sizes:
    def __init__(self, dp, rows, hidden, tokens):
        self.dp = dp
        self.outer = dp // QUADS
        self.rows = rows
        self.pad = round_up(rows, 16)
        self.whole = rows % 16 == 0
        self.wide = dp * rows
        self.slice = round_up(-(-hidden // QUADS), 128)
        self.head = self.slice % WIDE or WIDE
        self.full = (self.slice - self.head) // WIDE
        self.tokens = tokens
        self.hidden = hidden
        self.scratch = 30 if self.whole else 32


def mlp_kernel(sz, *refs):
    (
        xn_ref, cot_ref, wh_ref, wf_ref,
        gh_ref, gf_ref, gn_ref, br_ref,
        wagh, wagf, ruph, rupf, rdnh, rdnf, pairbuf, chipbuf,
        xb, cb, nacc, wvh, wv, pbh, pb, hh, hf, gg, gu, nst, nsd, tk, rth, rtf, own,
        s_a2a, r_a2a, s_ag, r_ag, s_rs, r_rs, s_fin, r_fin, s_tok, r_tok, s_sum, r_sum, loc,
    ) = refs[:16] + refs[-sz.scratch :][:30]
    abh, abf, stage, joined = (None,) * 4 if sz.whole else refs[16:18] + refs[-2:]
    O, NF, T = sz.outer, sz.full, sz.tokens
    HK, W, R, RP = sz.head, sz.wide, sz.rows, sz.pad
    R4 = QUADS * R
    me = lax.axis_index("dp")
    y = lax.axis_index("tensor")
    o, q = me // QUADS, me % QUADS
    x, c = q // 2, q % 2

    def at(o_, q_, y_):
        return (o_ * QUADS + q_, y_)

    above, below = lax.rem(o + 1, O), lax.rem(o + O - 1, O)
    up, down = at(above, q, y), at(below, q, y)
    core = at(o, x * 2 + 1 - c, y)
    chips = [(1 - x, 1 - y), (1 - x, y), (x, 1 - y)]
    order = chips + [(x, y)]

    def remote(src, dst, ssem, rsem, dev):
        return pltpu.make_async_remote_copy(
            src_ref=src, dst_ref=dst, send_sem=ssem, recv_sem=rsem,
            device_id=dev, device_id_type=MESH,
        )

    def local(src, dst, sem):
        return pltpu.make_async_copy(src, dst, sem)

    bar = pltpu.get_barrier_semaphore()

    def greet(dev):
        pl.semaphore_signal(bar, inc=1, device_id=dev, device_id_type=MESH)

    for dq in range(QUADS):
        for yy in range(2):
            if dq or yy:
                greet(at(o, lax.rem(q + dq, QUADS), (y + yy) % 2))
    pl.when(o < O - 1)(lambda: greet(up))
    pl.when(o > 0)(lambda: greet(down))
    pl.semaphore_wait(bar, 2 * QUADS - 1 + lax.min(o, 1) + lax.min(O - 1 - o, 1))

    class Chunk:
        def __init__(self, kk):
            self.head = kk is None
            if self.head:
                self.i, self.fk = 0, HK
                self.src, self.wag, self.rup, self.rdn = wh_ref, wagh, ruph, rdnh
                self.pb, self.out, self.tmp, self.hid = pbh, gh_ref, rth, hh
                self.wv, self.lw, self.ab = wvh, loc.at[0], abh
            else:
                self.i, self.fk = kk + 1, WIDE
                self.src, self.wag, self.rup, self.rdn = (
                    wf_ref.at[kk], wagf.at[kk], rupf.at[kk], rdnf.at[kk],
                )
                self.pb, self.out, self.tmp, self.hid = pb.at[kk], gf_ref.at[kk], rtf, hf.at[kk]
                self.wv, self.lw = wv.at[lax.rem(kk, 2)], loc.at[1 + lax.rem(kk, 2)]
                self.ab = None if abf is None else abf.at[kk]

        def block(self, ref, b):
            return ref.at[:, pl.ds(pl.multiple_of(b * R4, R4), R4), :]

        def part(self, ref, b, q_):
            return ref.at[:, pl.ds(pl.multiple_of((b * QUADS + q_) * R, R), R), :]

        def mine(self):
            return self.part(self.wag, o, q) if sz.whole else self.ab.at[q]

        def a2a(self, dq):
            to = lax.rem(q + dq, QUADS)
            return remote(
                self.src.at[to], self.mine(),
                s_a2a.at[self.i, dq - 1], r_a2a.at[self.i, dq - 1], at(o, to, y),
            )

        def a2a_own(self):
            return local(self.src.at[q], self.mine(), loc.at[3])

        def a2a_start(self):
            for dq in range(1, QUADS):
                self.a2a(dq).start()
            self.a2a_own().start()
            self.a2a_own().wait()

        def join(self):
            move = local(self.ab, stage.at[:, :, :, pl.ds(0, self.fk)], loc.at[3])
            move.start()
            move.wait()
            for m in range(3):
                rows = [stage[i, m, :, : self.fk].astype(F32)[:R] for i in range(QUADS)]
                joined[m, :, : self.fk] = jnp.concatenate(rows, axis=0).astype(BF)
            move = local(joined.at[:, :, pl.ds(0, self.fk)], self.block(self.wag, o), loc.at[3])
            move.start()
            move.wait()

        def ag(self, way, step, b):
            return remote(
                self.block(self.wag, b), self.block(self.wag, b),
                s_ag.at[self.i, way, step], r_ag.at[self.i, way, step], (up, down)[way],
            )

        def ag_own(self):
            for dq in range(1, QUADS):
                self.a2a(dq).wait_recv()
            if not sz.whole:
                self.join()
            pl.when(o < O - 1)(lambda: self.ag(0, 0, o).start())
            pl.when(o > 0)(lambda: self.ag(1, 0, o).start())

        def ag_pass(self, s):
            @pl.when(o - 1 - s >= 0)
            def _():
                self.ag(0, s, lax.max(o - 1 - s, 0)).wait_recv()
                if s + 1 < O - 1:
                    pl.when(o < O - 1)(lambda: self.ag(0, s + 1, lax.max(o - 1 - s, 0)).start())

            @pl.when(o + 1 + s <= O - 1)
            def _():
                self.ag(1, s, lax.min(o + 1 + s, O - 1)).wait_recv()
                if s + 1 < O - 1:
                    pl.when(o > 0)(lambda: self.ag(1, s + 1, lax.min(o + 1 + s, O - 1)).start())

        def ag_sent(self):
            for s in range(O - 1):

                @pl.when((o - s >= 0) & (o < O - 1))
                def _():
                    self.ag(0, s, lax.max(o - s, 0)).wait_send()

                @pl.when((o + s <= O - 1) & (o > 0))
                def _():
                    self.ag(1, s, lax.min(o + s, O - 1)).wait_send()

        def load(self):
            return local(self.wag, self.wv, self.lw)

        def rs(self, way, s):
            d = (O - 1 - s, s)[way]
            return remote(
                self.block(self.pb, d), self.block((self.rup, self.rdn)[way], d),
                s_rs.at[self.i, way, s], r_rs.at[self.i, way, s], (up, down)[way],
            )

        def fetch(self, way, d):
            return local(self.block((self.rup, self.rdn)[way], d), self.tmp.at[way], loc.at[4 + way])

        def add(self, way, d):
            ref = self.block(self.pb, d)
            for m in range(3):
                ref[m] = (ref[m].astype(F32) + self.tmp[way, m].astype(F32)).astype(BF)

        def rs_first(self):
            for s in range(O - 1):
                pl.when(o == 0)(lambda: self.rs(0, s).start())
                pl.when(o == O - 1)(lambda: self.rs(1, s).start())

        def rs_pass(self, s):
            d_up, d_down = O - 1 - s, s

            @pl.when((o > 0) & (d_up > o))
            def _():
                self.rs(0, s).wait_recv()
                self.fetch(0, d_up).start()
                self.fetch(0, d_up).wait()
                self.add(0, d_up)
                self.rs(0, s).start()

            @pl.when((o < O - 1) & (d_down < o))
            def _():
                self.rs(1, s).wait_recv()
                self.fetch(1, d_down).start()
                self.fetch(1, d_down).wait()
                self.add(1, d_down)
                self.rs(1, s).start()

        def result(self, q_):
            if sz.whole:
                return self.part(self.pb, o, q_)
            return self.ab.at[q_]

        def fin(self, dq):
            to = lax.rem(q + dq, QUADS)
            return remote(
                self.result(to), self.out.at[q],
                s_fin.at[self.i, dq - 1], r_fin.at[self.i, dq - 1], at(o, to, y),
            )

        def fin_own(self):
            return local(self.result(q), self.out.at[q], loc.at[3])

        def split(self):
            for m in range(3):
                rows = self.block(self.pb, o)[m].astype(F32)
                for i in range(QUADS):
                    part = rows[i * R : (i + 1) * R]
                    part = jnp.concatenate([part, jnp.zeros((RP - R, self.fk), F32)], axis=0)
                    stage[i, m, :, : self.fk] = part.astype(BF)
            move = local(stage.at[:, :, :, pl.ds(0, self.fk)], self.ab, loc.at[3])
            move.start()
            move.wait()

        def rs_last(self):
            @pl.when(o > 0)
            def _():
                self.rs(0, O - 1 - o).wait_recv()
                self.fetch(0, o).start()

            @pl.when(o < O - 1)
            def _():
                self.rs(1, o).wait_recv()
                self.fetch(1, o).start()

            @pl.when(o > 0)
            def _():
                self.fetch(0, o).wait()
                self.add(0, o)

            @pl.when(o < O - 1)
            def _():
                self.fetch(1, o).wait()
                self.add(1, o)

            if not sz.whole:
                self.split()
            for dq in range(1, QUADS):
                self.fin(dq).start()
            self.fin_own().start()
            self.fin_own().wait()

        def finished(self):
            for dq in range(1, QUADS):
                self.a2a(dq).wait_send()
                self.fin(dq).wait()
            self.ag_sent()
            for s in range(O):
                pl.when((o < O - 1) & (O - 1 - s > o))(lambda: self.rs(0, s).wait_send())
                pl.when((o > 0) & (s < o))(lambda: self.rs(1, s).wait_send())

    def chip_rows(xx, yy):
        return pl.ds(pl.multiple_of((xx * 2 + yy) * (2 * T), 2 * T), 2 * T)

    def rows_of(xx, yy, cc):
        return pl.ds(pl.multiple_of(((xx * 2 + yy) * 2 + cc) * T, T), T)

    def tok(src, buf, which, n):
        if n == 3:
            return remote(
                src, buf.at[rows_of(x, y, c), :],
                s_tok.at[which, n], r_tok.at[which, n], core,
            )
        xx, yy = chips[n]
        return remote(
            src, buf.at[rows_of(x, y, c), :],
            s_tok.at[which, n], r_tok.at[which, n], at(o, xx * 2 + c, yy),
        )

    def tok_pass(buf, which, n):
        xx, yy = chips[n]
        rows = rows_of(xx, yy, c)
        return remote(
            buf.at[rows, :], buf.at[rows, :],
            s_tok.at[which, 4 + n], r_tok.at[which, 4 + n], core,
        )

    def tok_start(src, buf, which):
        for n in (3, 2, 1, 0):
            tok(src, buf, which, n).start()
        local(src, buf.at[rows_of(x, y, c), :], loc.at[6]).start()
        local(src, buf.at[rows_of(x, y, c), :], loc.at[6]).wait()

    def tok_take(src, buf, which, n):
        tok(src, buf, which, n).wait_recv()
        if n < 3:
            tok_pass(buf, which, n).start()
            tok_pass(buf, which, n).wait_recv()

    def tok_sent(src, buf, which):
        for n in range(4):
            tok(src, buf, which, n).wait_send()
        for n in range(3):
            tok_pass(buf, which, n).wait_send()

    def sum_pair(n, stage, which):
        return remote(
            stage, pairbuf.at[which, n],
            s_sum.at[which, n], r_sum.at[which, n], core,
        )

    def sum_chip(n, stage, which):
        xx, yy = chips[n]
        return remote(
            stage, chipbuf.at[which, n],
            s_sum.at[which, 4 + n], r_sum.at[which, 4 + n], at(o, xx * 2 + c, yy),
        )

    def sum_open(n, which, stage):
        xx, yy = order[n]
        stage[...] = nacc[rows_of(xx, yy, 1 - c), :].astype(BF)
        sum_pair(n, stage, which).start()

    def take(src):
        cp = local(src, tk, loc.at[7])
        cp.start()
        cp.wait()
        return tk[...].astype(F32)

    def sum_mid(n, which, stage, onward):
        xx, yy = order[n]
        sum_pair(n, stage, which).wait_recv()
        total = nacc[rows_of(xx, yy, c), :] + take(pairbuf.at[which, n])
        if n < 3:
            onward[...] = total.astype(BF)
            sum_chip(n, onward, which).start()
        else:
            own[...] = total

    def sum_close(which, stages, onwards, out_ref):
        for n in range(3):
            sum_chip(n, onwards[n], which).wait_recv()
            own[...] = own[...] + take(chipbuf.at[which, n])
        cp = local(own, out_ref, loc.at[7])
        cp.start()
        cp.wait()
        for n in range(3):
            sum_chip(n, onwards[n], which).wait_send()
        for n in range(4):
            sum_pair(n, stages[n], which).wait_send()

    head = Chunk(None)
    head.a2a_start()
    tok_start(xn_ref, xb, 0)
    tok_start(cot_ref, cb, 1)
    Chunk(0).a2a_start()
    head.ag_own()
    for n in (2, 1, 0):
        tok_take(cot_ref, cb, 1, n)
    tok_take(cot_ref, cb, 1, 3)
    Chunk(0).ag_own()
    for s in range(O - 1):
        head.ag_pass(s)
    for kk in range(1, NF):
        Chunk(kk).a2a_start()
    head.load().start()
    if NF > 1:
        Chunk(1).ag_own()

    def tile(ch, rows, first):
        fk = ch.fk
        xv, cv = xb[rows, :], cb[rows, :]
        gate = dot_rows(xv, ch.wv[0])
        upper = dot_rows(xv, ch.wv[1])
        back = dot_rows(cv, ch.wv[2])
        sigma = jax.nn.sigmoid(gate)
        silu = gate * sigma
        ch.hid[rows, :] = (silu * upper).astype(BF)
        gg_t = (back * upper * (sigma * (1.0 + gate * (1.0 - sigma)))).astype(BF)
        gu_t = (back * silu).astype(BF)
        gg[rows, pl.ds(0, fk)] = gg_t
        gu[rows, pl.ds(0, fk)] = gu_t
        total = dot_right(gg_t, ch.wv[0]) + dot_right(gu_t, ch.wv[1])
        if first:
            nacc[rows, :] = total
        else:
            nacc[rows, :] = nacc[rows, :] + total

    TD = 512 if W % 512 == 0 else 256

    def products(ch, m):
        src, right = (
            (xb, lambda: gg[:, pl.ds(0, ch.fk)]),
            (xb, lambda: gu[:, pl.ds(0, ch.fk)]),
            (cb, lambda: ch.hid[...]),
        )[m]

        def step(i, carry):
            cols = pl.ds(pl.multiple_of(i * TD, TD), TD)
            ch.pb[m, cols, :] = dot_left(src[:, cols], right()).astype(BF)
            return carry

        lax.fori_loop(0, W // TD, step, 0)

    def ag_span(point):
        return range((O - 1) * point // 3, (O - 1) * (point + 1) // 3)

    head.load().wait()
    tok_take(xn_ref, xb, 0, 3)
    near_first = [3, 2, 1, 0]

    for p, n in enumerate(near_first):
        if n < 3:
            tok_take(xn_ref, xb, 0, n)
        xx, yy = order[n]
        tile(head, chip_rows(xx, yy), True)
        if p < 3 and NF > 0:
            for s in ag_span(p):
                Chunk(0).ag_pass(s)
    if NF > 0:
        Chunk(0).load().start()
    for m in range(3):
        products(head, m)
    head.rs_first()
    if NF > 2:
        Chunk(2).ag_own()

    def rs_at(i):
        def run():
            kk = i // O
            Chunk(kk).rs_pass(i % O)

        pl.when((i >= 0) & (i < NF * O))(run)

    per = (3 * O) // 4

    def body(kk, carry):
        ch, nxt = Chunk(kk), Chunk(lax.min(kk + 1, NF - 1))
        last = kk == NF - 1
        ch.load().wait()

        def visit(p, carry2):
            xx = jnp.where(p < 2, 1 - x, x)
            yy = jnp.where(p % 2 == 0, 1 - y, y)
            tile(ch, chip_rows(xx, yy), False)

            @pl.when(last)
            def _():
                for n in range(4):
                    pl.when(p == n)(lambda: sum_open(n, 0, nst.at[n]))
                for n in range(3):
                    pl.when(p == n + 1)(lambda: sum_mid(n, 0, nst.at[n], nsd.at[n]))

            @pl.when(kk < NF - 1)
            def _():
                for point in range(3):

                    @pl.when(p == point)
                    def _():
                        for s in ag_span(point):
                            nxt.ag_pass(s)

            @pl.when(kk == 0)
            def _():
                for s in range(O):
                    pl.when(p == s * 4 // O)(lambda: head.rs_pass(s))

            @pl.when((kk > 0) & (p < 3))
            def _():
                for e in range(-(-per // 3)):
                    pl.when(p * (-(-per // 3)) + e < per)(
                        lambda: rs_at((kk - 1) * per + p * (-(-per // 3)) + e)
                    )

            return carry2

        lax.fori_loop(0, 4, visit, 0)
        pl.when(kk < NF - 1)(lambda: nxt.load().start())
        pl.when(last)(lambda: sum_mid(3, 0, nst.at[3], None))
        for m in range(3):
            products(ch, m)
        ch.rs_first()
        pl.when(kk + 3 < NF)(lambda: Chunk(lax.min(kk + 3, NF - 1)).ag_own())
        return carry

    lax.fori_loop(0, NF, body, 0)

    done = (NF - 1) * per
    rs_total = NF * O
    sum_close(0, [nst.at[n] for n in range(4)], [nsd.at[n] for n in range(3)], gn_ref)

    mst = [cb.at[pl.ds(n * T, T), :] for n in range(4)]
    msd = [cb.at[pl.ds((4 + n) * T, T), :] for n in range(3)]

    def m_first(p, carry):
        rows = pl.ds(pl.multiple_of(p * 2 * T, 2 * T), 2 * T)
        nacc[rows, :] = dot_right(hh[rows, :], wvh[2])
        return carry

    lax.fori_loop(0, 4, m_first, 0)

    def m_chunk(kk, carry):
        cp = local(wagf.at[kk, 2], wv.at[0, 2], loc.at[8])
        cp.start()
        cp.wait()

        def m_tile(p, carry2):
            rows = pl.ds(pl.multiple_of(p * 2 * T, 2 * T), 2 * T)
            nacc[rows, :] = nacc[rows, :] + dot_right(hf[kk, rows, :], wv[0, 2])
            return carry2

        lax.fori_loop(0, 4, m_tile, 0)
        rs_at(done + kk)
        return carry

    lax.fori_loop(0, NF, m_chunk, 0)
    tok_sent(cot_ref, cb, 1)
    for n in range(4):
        sum_open(n, 1, mst[n])
    for n in range(4):
        sum_mid(n, 1, mst[n], msd[n] if n < 3 else None)
    head.rs_last()

    def rest(i, carry):
        rs_at(i)
        return carry

    lax.fori_loop(done + NF, rs_total, rest, 0)

    def lasts(kk, carry):
        Chunk(kk).rs_last()
        return carry

    lax.fori_loop(0, NF, lasts, 0)
    sum_close(1, mst, msd, br_ref)
    tok_sent(xn_ref, xb, 0)
    head.finished()

    def ends(kk, carry):
        Chunk(kk).finished()
        return carry

    lax.fori_loop(0, NF, ends, 0)


def feed_forward(sz, normed, cotangent, wh, wf):
    O, NF, T = sz.outer, sz.full, sz.tokens
    HK, W, R, RP = sz.head, sz.wide, sz.rows, sz.pad
    R4 = QUADS * R
    PT = 2 * QUADS * T
    out = jax.ShapeDtypeStruct
    any_spec = pl.BlockSpec(memory_space=pl.ANY)
    outs = [
        out((QUADS, 3, RP, HK), BF),
        out((NF, QUADS, 3, RP, WIDE), BF),
        out((T, W), F32),
        out((T, W), F32),
        out((3, W, HK), BF),
        out((NF, 3, W, WIDE), BF),
        out((3, W, HK), BF),
        out((NF, 3, W, WIDE), BF),
        out((3, W, HK), BF),
        out((NF, 3, W, WIDE), BF),
        out((2, 4, T, W), BF),
        out((2, 3, T, W), BF),
    ]
    if not sz.whole:
        outs += [out((QUADS, 3, RP, HK), BF), out((NF, QUADS, 3, RP, WIDE), BF)]
    dma = pltpu.SemaphoreType.DMA
    vm = pltpu.VMEM
    scratch = [
        vm((PT, W), BF),
        vm((PT, W), BF),
        vm((PT, W), F32),
        vm((3, W, HK), BF),
        vm((2, 3, W, WIDE), BF),
        vm((3, W, HK), BF),
        vm((NF, 3, W, WIDE), BF),
        vm((PT, HK), BF),
        vm((NF, PT, WIDE), BF),
        vm((PT, WIDE), BF),
        vm((PT, WIDE), BF),
        vm((4, T, W), BF),
        vm((3, T, W), BF),
        vm((T, W), BF),
        vm((2, 3, R4, HK), BF),
        vm((2, 3, R4, WIDE), BF),
        vm((T, W), F32),
        dma((NF + 1, 3)),
        dma((NF + 1, 3)),
        dma((NF + 1, 2, O - 1)),
        dma((NF + 1, 2, O - 1)),
        dma((NF + 1, 2, O)),
        dma((NF + 1, 2, O)),
        dma((NF + 1, 3)),
        dma((NF + 1, 3)),
        dma((2, 7)),
        dma((2, 7)),
        dma((2, 7)),
        dma((2, 7)),
        dma((9,)),
    ]
    if not sz.whole:
        scratch += [
            vm((QUADS, 3, RP, WIDE), BF),
            vm((3, R4, WIDE), BF),
        ]
    results = pl.pallas_call(
        lambda *refs: mlp_kernel(sz, *refs),
        out_shape=outs,
        in_specs=[any_spec] * 4,
        out_specs=[any_spec] * len(outs),
        scratch_shapes=scratch,
        compiler_params=pltpu.CompilerParams(
            collective_id=0, has_side_effects=True, vmem_limit_bytes=63 << 20
        ),
        name="feed_forward",
    )(normed, cotangent, wh, wf)
    return results[:4]


def per_device(
    sz,
    tokens,
    w_query,
    key_weight,
    value_weight,
    b_query,
    key_bias,
    value_bias,
    w_out,
    gain_attn,
    gain_mlp,
    w_gate,
    w_up,
    w_down,
    cotangent,
):
    rows, hidden_units = w_gate.shape
    w3 = jnp.stack([w_gate, w_up, w_down.T])
    w3 = jnp.pad(
        w3, ((0, 0), (0, sz.pad - sz.rows), (0, QUADS * sz.slice - hidden_units))
    ).reshape(3, sz.pad, QUADS, sz.slice)
    wh = w3[..., : sz.head].transpose(2, 0, 1, 3)
    wf = w3[..., sz.head :].reshape(3, sz.pad, QUADS, sz.full, WIDE).transpose(3, 2, 0, 1, 4)

    query_width, key_width = w_query.shape[1], key_weight.shape[1]
    packed = jnp.concatenate([w_query, key_weight, value_weight, w_out.T], axis=1)
    packed = lax.all_gather(packed, "dp", axis=0, tiled=True)
    cuts = (query_width, query_width + key_width, query_width + 2 * key_width)
    query_full, key_full, value_full, out_t = jnp.split(packed, cuts, axis=1)

    local_heads = query_width // HEAD_SIZE
    local_groups = key_width // HEAD_SIZE
    share = local_heads // local_groups
    factor = 1.0 / math.sqrt(HEAD_SIZE)
    cosine, sine = rope_tables(SEQUENCE_TOKENS, HEAD_SIZE)
    causal = jnp.arange(SEQUENCE_TOKENS)[:, None] >= jnp.arange(SEQUENCE_TOKENS)[None, :]
    inputs = tokens.astype(F32)
    scale_attn = rms_scale(inputs)
    normed_attention = (inputs * scale_attn * gain_attn).astype(BF)
    normed_all = lax.all_gather(normed_attention, "tensor", axis=0, tiled=True)
    total_rows = normed_all.shape[0]
    sequences = total_rows // SEQUENCE_TOKENS
    query_lin = (dot_rows(normed_all, query_full) + b_query).reshape(
        sequences, SEQUENCE_TOKENS, local_heads, HEAD_SIZE
    )
    key_linear = (dot_rows(normed_all, key_full) + key_bias).reshape(
        sequences, SEQUENCE_TOKENS, local_groups, HEAD_SIZE
    )
    value_linear = dot_rows(normed_all, value_full) + value_bias
    queries = (query_lin * cosine + rotate(query_lin) * sine).astype(BF)
    queries = queries.reshape(sequences, SEQUENCE_TOKENS, local_groups, share, HEAD_SIZE)
    keys = (key_linear * cosine + rotate(key_linear) * sine).astype(BF)
    values = value_linear.astype(BF).reshape(sequences, SEQUENCE_TOKENS, local_groups, HEAD_SIZE)

    scores = jnp.einsum("bsjgd,btjd->bjgst", queries, keys, preferred_element_type=F32) * factor
    scores = jnp.where(causal, scores, -1e30)
    largest = jnp.max(scores, axis=-1, keepdims=True)
    exponent = jnp.exp(scores - largest)
    row_totals = jnp.sum(exponent, axis=-1, keepdims=True)
    probs_low = (exponent / row_totals).astype(BF)
    mixed_heads = jnp.einsum(
        "bjgst,btjd->bsjgd", probs_low, values, preferred_element_type=F32
    ).astype(BF)
    logsum = largest + jnp.log(row_totals)
    mixed_all = mixed_heads.reshape(total_rows, query_width)
    attended = lax.psum_scatter(
        dot_right(mixed_all, out_t), "tensor", scatter_dimension=0, tiled=True
    )
    middle = inputs + attended
    scale_mlp = rms_scale(middle)
    normed_mlp = (middle * scale_mlp * gain_mlp).astype(BF)

    grad_head, grad_full, grad_normed_mlp, branch = feed_forward(
        sz, normed_mlp, cotangent, wh, wf
    )
    mixed = (middle + branch).astype(BF)
    grads = jnp.concatenate(
        [
            grad_head.transpose(1, 2, 0, 3),
            grad_full.transpose(2, 3, 1, 0, 4).reshape(3, sz.pad, QUADS, sz.full * WIDE),
        ],
        axis=-1,
    ).reshape(3, sz.pad, QUADS * sz.slice)[:, :rows, :hidden_units]
    grads = grads.astype(F32)
    grad_w_gate, grad_w_up, grad_w_down = grads[0], grads[1], grads[2].T

    upstream = cotangent.astype(F32)
    grad_middle = upstream + norm_back(middle, scale_mlp, gain_mlp, grad_normed_mlp)
    gain_mlp_term = jnp.sum(grad_normed_mlp * middle * scale_mlp, axis=0)
    grad_attended = grad_middle.astype(BF)
    grad_att_all = lax.all_gather(grad_attended, "tensor", axis=0, tiled=True)
    grad_mixed = dot_rows(grad_att_all, out_t).astype(BF)
    grad_out_part = dot_left(grad_att_all, mixed_all)
    grad_block = grad_mixed.reshape(sequences, SEQUENCE_TOKENS, local_groups, share, HEAD_SIZE)

    probs = jnp.exp(scores - logsum)
    grad_values = jnp.einsum(
        "bjgst,bsjgd->btjd", probs.astype(BF), grad_block, preferred_element_type=F32
    )
    grad_probs = jnp.einsum(
        "bsjgd,btjd->bjgst", grad_block, values, preferred_element_type=F32
    )
    inner = jnp.sum(grad_probs * probs, axis=-1, keepdims=True)
    grad_scores = (probs * (grad_probs - inner)).astype(BF)
    grad_queries = (
        jnp.einsum("bjgst,btjd->bsjgd", grad_scores, keys, preferred_element_type=F32) * factor
    )
    grad_keys = (
        jnp.einsum("bjgst,bsjgd->btjd", grad_scores, queries, preferred_element_type=F32) * factor
    )
    grad_queries = grad_queries.reshape(sequences, SEQUENCE_TOKENS, local_heads, HEAD_SIZE)
    grad_query_lin = (grad_queries * cosine - rotate(grad_queries * sine)).astype(BF)
    grad_query_lin = grad_query_lin.reshape(total_rows, query_width)
    grad_key_lin = (grad_keys * cosine - rotate(grad_keys * sine)).astype(BF)
    grad_key_lin = grad_key_lin.reshape(total_rows, key_width)
    grad_value_lin = grad_values.astype(BF).reshape(total_rows, key_width)
    grad_lin = jnp.concatenate([grad_query_lin, grad_key_lin, grad_value_lin], axis=1)
    grad_part = dot_left(normed_all, grad_lin)
    grad_normed_attn = lax.psum_scatter(
        dot_right(grad_lin, packed[:, : cuts[2]]).astype(BF),
        "tensor",
        scatter_dimension=0,
        tiled=True,
    ).astype(F32)
    grad_packed = lax.psum_scatter(
        jnp.concatenate([grad_part, grad_out_part], axis=1).astype(BF),
        "dp",
        scatter_dimension=0,
        tiled=True,
    ).astype(F32)
    grad_w_query, grad_w_key, grad_w_value, grad_w_out = jnp.split(grad_packed, cuts, axis=1)
    grad_w_out = grad_w_out.T
    grad_tokens = grad_middle + norm_back(inputs, scale_attn, gain_attn, grad_normed_attn)
    gain_attn_term = jnp.sum(grad_normed_attn * inputs * scale_attn, axis=0)
    position = lax.axis_index("tensor")

    def place(values, width):
        return lax.dynamic_update_slice(
            jnp.zeros((2 * width,), F32), values, (position * width,)
        )

    grad_gain_attn, grad_gain_mlp, query_sums, key_sums, value_sums = lax.psum(
        (
            gain_attn_term,
            gain_mlp_term,
            place(jnp.sum(grad_query_lin, axis=0, dtype=F32), query_width),
            place(jnp.sum(grad_key_lin, axis=0, dtype=F32), key_width),
            place(jnp.sum(grad_value_lin, axis=0, dtype=F32), key_width),
        ),
        ("dp", "tensor"),
    )
    grad_b_query = lax.dynamic_slice_in_dim(query_sums, position * query_width, query_width, 0)
    grad_b_key = lax.dynamic_slice_in_dim(key_sums, position * key_width, key_width, 0)
    grad_b_value = lax.dynamic_slice_in_dim(value_sums, position * key_width, key_width, 0)
    return (
        mixed,
        grad_tokens,
        grad_w_query,
        grad_w_key,
        grad_w_value,
        grad_b_query,
        grad_b_key,
        grad_b_value,
        grad_w_out,
        grad_gain_attn,
        grad_gain_mlp,
        grad_w_gate,
        grad_w_up,
        grad_w_down,
    )


def solution(mesh):
    dp = mesh.shape["dp"]

    def whole(*args):
        def shard(*blocks):
            w_gate, tokens = blocks[10], blocks[0]
            sz = Sizes(dp, w_gate.shape[0], w_gate.shape[1], tokens.shape[0])
            return per_device(sz, *blocks)

        return jax.shard_map(
            shard, mesh=mesh, in_specs=in_specs, out_specs=out_specs, check_vma=False
        )(*args)

    in_specs = (
        P(("dp", "tensor"), None),
        P("dp", "tensor"),
        P("dp", "tensor"),
        P("dp", "tensor"),
        P("tensor"),
        P("tensor"),
        P("tensor"),
        P("tensor", "dp"),
        P(),
        P(),
        P("dp", "tensor"),
        P("dp", "tensor"),
        P("tensor", "dp"),
        P(("dp", "tensor"), None),
    )
    out_specs = (
        P(("dp", "tensor"), None),
        P(("dp", "tensor"), None),
        P("dp", "tensor"),
        P("dp", "tensor"),
        P("dp", "tensor"),
        P("tensor"),
        P("tensor"),
        P("tensor"),
        P("tensor", "dp"),
        P(),
        P(),
        P("dp", "tensor"),
        P("dp", "tensor"),
        P("tensor", "dp"),
    )
    return whole
```

```python
import math

import jax
import jax.numpy as jnp
from jax import lax
from jax.experimental import pallas as pl
from jax.experimental.pallas import tpu as pltpu
from jax.sharding import PartitionSpec as P

QUERY_HEADS = 12
KEY_VALUE_HEADS = 2
HEAD_SIZE = 128
SEQUENCE_TOKENS = 512

QUADS = 4
WIDE = 256

norm_eps = 1e-06
rope_base = 1000000.0
BF = jnp.bfloat16
F32 = jnp.float32
MESH = pl.DeviceIdType.MESH


def rope_tables(length, columns):
    midway = columns // 2
    inverse = jnp.exp(
        jnp.arange(midway, dtype=jnp.float32) * (-2.0 * math.log(rope_base) / columns)
    )
    angles = jnp.arange(length, dtype=jnp.float32)[:, None] * inverse[None, :]
    angles = jnp.concatenate([angles, angles], axis=-1)
    return (jnp.cos(angles)[None, :, None, :], jnp.sin(angles)[None, :, None, :])


def dot_rows(left, right):
    return jnp.dot(left, right, preferred_element_type=F32)


def dot_left(left, right):
    return lax.dot_general(left, right, (((0,), (0,)), ((), ())), preferred_element_type=F32)


def dot_right(left, right):
    return lax.dot_general(left, right, (((1,), (1,)), ((), ())), preferred_element_type=F32)


def round_up(value, step):
    return (value + step - 1) // step * step


class Sizes:
    def __init__(self, dp, gate_shape, tokens, query, key):
        self.dp = dp
        self.outer = dp // QUADS
        self.rows, self.hidden = gate_shape
        self.pad = round_up(self.rows, 16)
        self.whole = self.pad == self.rows
        self.wide = dp * self.rows
        self.slice = round_up(-(-self.hidden // QUADS), 128)
        self.head = self.slice % WIDE or WIDE
        self.full = (self.slice - self.head) // WIDE
        self.tokens, self.query, self.key = tokens, query, key


def layer_kernel(sz, *refs):
    refs = iter(refs)

    def some(n):
        return [next(refs) for _ in range(n)]

    tok_ref, cot_ref, wq_ref, wo_ref, wh_ref, wf_ref, vec, rope = some(8)
    gh_ref, gf_ref, gaq_ref, gao_ref, mixed_ref, gtok_ref, sums_ref = some(7)
    wagh, wagf, colh, colf, nearh, nearf, outh, outf = some(8)
    pairbuf, chipbuf, gq, go = some(4)
    rcq, rco, rxq, rxo, colq, colo, nearq, nearo, outq, outo = some(10)
    abh, abf = (None, None) if sz.whole else some(2)
    xb, cb, nacc, wv, pbh, pb, hh, hf, gu, nsd, tk, rt, own = some(13)
    xa, qkv, mh, ar, st, mid, ga, sv, svr, svz = some(10)
    s_a2a, r_a2a, s_own, r_own, s_far, r_far, s_fwd, r_fwd = some(8)
    s_col, r_col, s_nr, r_nr, s_out, r_out, s_fin, r_fin = some(8)
    s_tok, r_tok, s_sum, r_sum, s_y, r_y, s_gz, r_gz, s_gx, r_gx, s_gc, r_gc = some(12)
    s_pc, r_pc, s_px, r_px, s_v, r_v, s_vz, r_vz, loc = some(9)
    stage, joined = (None, None) if sz.whole else some(2)

    O, NF, T = sz.outer, sz.full, sz.tokens
    H = O // 2
    HK, W, R, RP = sz.head, sz.wide, sz.rows, sz.pad
    R4, LR = QUADS * R, O * RP
    QW = sz.query
    GW = sz.query + 2 * sz.key
    HEADS = QW // HEAD_SIZE
    FACTOR = 1.0 / math.sqrt(HEAD_SIZE)
    me = lax.axis_index("dp")
    y = lax.axis_index("tensor")
    o, q = me // QUADS, me % QUADS
    x, c = q // 2, q % 2
    half, pos = o // H, o % H
    base, far = half * H, (1 - half) * H
    middle_pos = (1 - half) * (H - 1)
    is_middle = pos == middle_pos

    def at(o_, q_, y_):
        return (o_ * QUADS + q_, y_)

    mid_dev = at(base + middle_pos, q, y)
    far_mid = at(far + half * (H - 1), q, y)
    core = at(o, x * 2 + 1 - c, y)
    over_x = at(o, (1 - x) * 2 + c, y)
    over_y = at(o, q, 1 - y)
    chips = [(1 - x, 1 - y), (1 - x, y), (x, 1 - y)]
    order = chips + [(x, y)]

    def remote(src, dst, ssem, rsem, dev):
        return pltpu.make_async_remote_copy(
            src_ref=src, dst_ref=dst, send_sem=ssem, recv_sem=rsem,
            device_id=dev, device_id_type=MESH,
        )

    def local(src, dst, sem):
        return pltpu.make_async_copy(src, dst, sem)

    def move(src, dst, sem):
        local(src, dst, sem).start()
        local(src, dst, sem).wait()

    def span(start, size, unit):
        return pl.ds(pl.multiple_of(start, unit), size)

    def loop(n, step):
        def run(i, carry):
            step(i)
            return carry

        lax.fori_loop(0, n, run, 0)

    bar = pltpu.get_barrier_semaphore()

    def greet(dev):
        pl.semaphore_signal(bar, inc=1, device_id=dev, device_id_type=MESH)

    for dq in range(QUADS):
        for yy in range(2):
            if dq or yy:
                greet(at(o, lax.rem(q + dq, QUADS), (y + yy) % 2))
    for step in range(1, O):
        greet(at(lax.rem(o + step, O), q, y))
    pl.semaphore_wait(bar, 2 * QUADS - 1 + O - 1)

    def add_into(dst, src, n):
        rows = 32

        def step(i):
            here = span(i * rows, rows, rows)
            dst[here, :] = (dst[here, :].astype(F32) + src[here, :].astype(F32)).astype(BF)

        loop(n // rows, step)

    class Line:
        def __init__(self, i, rows, pieces, col, near, out, temps):
            self.i, self.rows, self.pieces = i, rows, pieces
            self.col, self.near_, self.out, self.temps = col, near, out, temps

        def block(self, k, b, n=1):
            return self.pieces[k].at[span(b * self.rows, n * self.rows, self.rows), :]

        def temp(self, k, start, n):
            return self.temps[k].at[pl.ds(start * self.rows, n * self.rows), :]

        def to_middle(self, k, t):
            return remote(
                self.block(k, far, H), self.col[k].at[t],
                s_col.at[self.i + k], r_col.at[self.i + k, t], mid_dev,
            )

        def near(self, k, to, t):
            return remote(
                self.block(k, base + to), self.near_[k].at[t],
                s_nr.at[self.i + k, to], r_nr.at[self.i + k, t], at(base + to, q, y),
            )

        def cross(self, k, to):
            return remote(
                self.block(k, far + to), self.out[k],
                s_out.at[self.i + k, to], r_out.at[self.i + k], at(far + to, q, y),
            )

        def first(self):
            for k in range(len(self.pieces)):
                pl.when(jnp.logical_not(is_middle))(lambda: self.to_middle(k, pos).start())
                for t in range(H):
                    pl.when(pos != t)(lambda: self.near(k, t, pos).start())

        def middle(self):
            ks = range(len(self.pieces))

            @pl.when(is_middle)
            def _():
                for t in range(H):

                    @pl.when(pos != t)
                    def _():
                        for k in ks:
                            self.to_middle(k, t).wait_recv()
                            local(self.col[k].at[t], self.temp(k, 0, H), loc.at[4 + k]).start()
                        for k in ks:
                            local(self.col[k].at[t], self.temp(k, 0, H), loc.at[4 + k]).wait()
                            add_into(self.block(k, far, H), self.temp(k, 0, H), H * self.rows)

                for k in ks:
                    for t in range(H):
                        self.cross(k, t).start()

        def last(self):
            ks = range(len(self.pieces))
            for t in range(H):

                @pl.when(pos != t)
                def _():
                    for k in ks:
                        self.near(k, pos, t).wait_recv()
                        local(self.near_[k].at[t], self.temp(k, 0, 1), loc.at[4 + k]).start()
                    for k in ks:
                        local(self.near_[k].at[t], self.temp(k, 0, 1), loc.at[4 + k]).wait()
                        add_into(self.block(k, o), self.temp(k, 0, 1), self.rows)

            for k in ks:
                self.cross(k, pos).wait_recv()
                local(self.out[k], self.temp(k, 1, 1), loc.at[4 + k]).start()
            for k in ks:
                local(self.out[k], self.temp(k, 1, 1), loc.at[4 + k]).wait()
                add_into(self.block(k, o), self.temp(k, 1, 1), self.rows)

        def sent(self):
            for k in range(len(self.pieces)):
                pl.when(jnp.logical_not(is_middle))(lambda: self.to_middle(k, pos).wait_send())
                for t in range(H):
                    pl.when(pos != t)(lambda: self.near(k, t, pos).wait_send())
                    pl.when(is_middle)(lambda: self.cross(k, t).wait_send())

    class Chunk:
        def __init__(self, kk):
            self.head = kk is None
            if self.head:
                self.i, self.fk = 0, HK
                self.src, self.wag, self.pb, self.out = wh_ref, wagh, pbh, gh_ref
                self.hid, self.ab = hh, abh
                col, near, out = colh, nearh, outh
            else:
                self.i, self.fk = kk + 1, WIDE
                self.src, self.wag, self.pb, self.out = (
                    wf_ref.at[kk], wagf.at[kk], pb.at[kk], gf_ref.at[kk],
                )
                self.hid, self.ab = hf.at[kk], None if abf is None else abf.at[kk]
                col, near, out = colf.at[kk], nearf.at[kk], outf.at[kk]
            self.cols = pl.ds(0, 3 * self.fk)
            self.wv = wv.at[:, self.cols]
            self.line = Line(self.i, R4, [self.pb], [col], [near], [out], [rt.at[:, self.cols]])

        def block(self, ref, b, n=1):
            return ref.at[span(b * R4, n * R4, R4), :]

        def part(self, ref, b, q_):
            return ref.at[span((b * QUADS + q_) * R, R, R), :]

        def mine(self):
            return self.part(self.wag, o, q) if sz.whole else self.ab.at[q]

        def a2a(self, dq):
            to = lax.rem(q + dq, QUADS)
            return remote(
                self.src.at[to], self.mine(),
                s_a2a.at[self.i, dq - 1], r_a2a.at[self.i, dq - 1], at(o, to, y),
            )

        def a2a_own(self):
            return local(self.src.at[q], self.mine(), s_a2a.at[self.i, 3])

        def a2a_start(self):
            self.a2a_own().start()
            for dq in (1, 2, 3):
                self.a2a(dq).start()

        def join(self):
            for i in range(QUADS):
                move(self.ab.at[i], stage.at[pl.ds(i * RP, RP), self.cols], loc.at[3])
            rows = [stage[i * RP : i * RP + RP, self.cols].astype(F32)[:R] for i in range(QUADS)]
            joined[:, self.cols] = jnp.concatenate(rows, axis=0).astype(BF)
            move(joined.at[:, self.cols], self.block(self.wag, o), loc.at[3])

        def own_to(self, to, t):
            return remote(
                self.block(self.wag, base + t), self.block(self.wag, base + t),
                s_own.at[self.i, to], r_own.at[self.i, t], at(base + to, q, y),
            )

        def own_far(self, half_, t):
            b = half_ * H + t
            return remote(
                self.block(self.wag, b), self.block(self.wag, b),
                s_far.at[self.i], r_far.at[self.i, t], far_mid,
            )

        def forward(self, half_, to):
            rows = self.block(self.wag, half_ * H, H)
            return remote(
                rows, rows, s_fwd.at[self.i, to], r_fwd.at[self.i], at(base + to, q, y),
            )

        def gather_own(self):
            self.a2a_own().wait()
            for dq in (1, 2, 3):
                self.a2a(dq).wait_recv()
            if not sz.whole:
                self.join()
            self.own_far(half, pos).start()
            for t in range(H):
                pl.when(pos != t)(lambda: self.own_to(t, pos).start())

        def gather_middle(self):
            @pl.when(is_middle)
            def _():
                for t in range(H):
                    self.own_far(1 - half, t).wait_recv()
                for t in range(H):
                    pl.when(pos != t)(lambda: self.forward(1 - half, t).start())

        def gather_wait(self):
            for t in range(H):
                pl.when(pos != t)(lambda: self.own_to(pos, t).wait_recv())
            pl.when(jnp.logical_not(is_middle))(lambda: self.forward(1 - half, pos).wait_recv())

        def gather_sent(self):
            for dq in (1, 2, 3):
                self.a2a(dq).wait_send()
            self.own_far(half, pos).wait_send()
            for t in range(H):

                @pl.when(pos != t)
                def _():
                    self.own_to(t, pos).wait_send()
                    pl.when(is_middle)(lambda: self.forward(1 - half, t).wait_send())

        def load(self):
            return local(self.wag, self.wv, loc.at[0])

        def result(self, q_):
            return self.part(self.pb, o, q_) if sz.whole else self.ab.at[q_]

        def give(self, dq):
            to = lax.rem(q + dq, QUADS)
            return remote(
                self.result(to), self.out.at[q],
                s_fin.at[self.i, dq - 1], r_fin.at[self.i, dq - 1], at(o, to, y),
            )

        def give_own(self):
            return local(self.result(q), self.out.at[q], s_fin.at[self.i, 3])

        def split(self):
            rows = self.block(self.pb, o)[...].astype(F32)
            for i in range(QUADS):
                part = rows[i * R : (i + 1) * R]
                part = jnp.concatenate([part, jnp.zeros((RP - R, 3 * self.fk), F32)], axis=0)
                stage[i * RP : i * RP + RP, self.cols] = part.astype(BF)
            for i in range(QUADS):
                move(stage.at[pl.ds(i * RP, RP), self.cols], self.ab.at[i], loc.at[3])

        def finish(self):
            self.line.last()
            if not sz.whole:
                self.split()
            self.give_own().start()
            for dq in (1, 2, 3):
                self.give(dq).start()

        def finished(self):
            self.give_own().wait()
            for dq in (1, 2, 3):
                self.give(dq).wait()
            self.gather_sent()
            self.line.sent()

    def chip_rows(xx, yy):
        return span((xx * 2 + yy) * (2 * T), 2 * T, 2 * T)

    def rows_of(xx, yy, cc):
        return span(((xx * 2 + yy) * 2 + cc) * T, T, T)

    mine = rows_of(x, y, c)

    def tok(src, buf, which, n):
        dev = core if n == 3 else at(o, chips[n][0] * 2 + c, chips[n][1])
        return remote(src, buf.at[mine, :], s_tok.at[which, n], r_tok.at[which, n], dev)

    def tok_pass(buf, which, n):
        rows = rows_of(*chips[n], c)
        return remote(
            buf.at[rows, :], buf.at[rows, :],
            s_tok.at[which, 4 + n], r_tok.at[which, 4 + n], core,
        )

    def tok_start(src, buf, which):
        for n in (3, 2, 1, 0):
            tok(src, buf, which, n).start()

    def tok_take(src, buf, which, n):
        tok(src, buf, which, n).wait_recv()
        if n < 3:
            tok_pass(buf, which, n).start()
            tok_pass(buf, which, n).wait_recv()

    def tok_sent(src, buf, which):
        for n in range(4):
            tok(src, buf, which, n).wait_send()
        for n in range(3):
            tok_pass(buf, which, n).wait_send()

    def sum_pair(n, which):
        return remote(
            nacc.at[rows_of(*order[n], 1 - c), :], pairbuf.at[which, n],
            s_sum.at[which, n], r_sum.at[which, n], core,
        )

    def sum_chip(n, which):
        xx, yy = chips[n]
        return remote(
            nsd.at[n], chipbuf.at[which, n],
            s_sum.at[which, 4 + n], r_sum.at[which, 4 + n], at(o, xx * 2 + c, yy),
        )

    def sum_mid(n, which):
        here, spare = nacc.at[rows_of(*order[n], c), :], nacc.at[rows_of(*order[n], 1 - c), :]
        sum_pair(n, which).wait()
        move(pairbuf.at[which, n], spare, loc.at[7])

        def step(i):
            a = span(i * 32, 32, 32)
            total = here[a, :] + spare[a, :]
            if n < 3:
                nsd[n, a, :] = total.astype(BF)
            else:
                here[a, :] = total

        loop(T // 32, step)
        if n < 3:
            sum_chip(n, which).start()

    def sum_close(which, finish):
        here = nacc.at[mine, :]
        for n in range(3):
            sum_chip(n, which).wait_recv()
            move(chipbuf.at[which, n], tk, loc.at[7])

            def step(i):
                a = span(i * 32, 32, 32)
                total = here[a, :] + tk[a, :].astype(F32)
                if n < 2:
                    here[a, :] = total
                else:
                    finish(a, total)

            loop(T // 32, step)
        for n in range(3):
            sum_chip(n, which).wait_send()

    class Gather:
        def __init__(self, i, src, buf):
            self.i, self.src, self.buf = i, src, buf

        def rows(self, o_, x_, c_):
            return self.buf.at[span(((o_ * 2 + x_) * 2 + c_) * RP, RP, RP), :]

        def place(self, step):
            return lax.rem(o - step + O, O)

        def send(self, step):
            return remote(
                self.src, self.rows(o, x, c), s_gz.at[self.i, step], r_gz.at[self.i, step],
                at(lax.rem(o + step, O), q, y),
            )

        def over(self, step):
            rows = self.rows(self.place(step), x, c)
            src = self.src if step == 0 else rows
            return remote(src, rows, s_gx.at[self.i, step], r_gx.at[self.i, step], over_x)

        def across(self, step, far_x):
            rows = self.rows(self.place(step), (1 - x) if far_x else x, c)
            src = self.src if step == 0 and not far_x else rows
            return remote(
                src, rows, s_gc.at[self.i, far_x, step], r_gc.at[self.i, far_x, step], core,
            )

        def own(self):
            return local(self.src, self.rows(o, x, c), s_gz.at[self.i, 0])

        def start(self):
            for step in range(1, O):
                self.send(step).start()
            self.over(0).start()
            self.across(0, 0).start()
            self.own().start()

        def pass_on(self):
            for step in range(1, O):
                self.send(step).wait_recv()
                self.over(step).start()
                self.across(step, 0).start()

        def pass_over(self):
            for step in range(O):
                self.over(step).wait_recv()
                self.across(step, 1).start()

        def wait(self):
            for far_x in range(2):
                for step in range(O):
                    self.across(step, far_x).wait_recv()
            self.own().wait()

        def sent(self):
            for step in range(1, O):
                self.send(step).wait_send()
            for step in range(O):
                self.over(step).wait_send()
                self.across(step, 0).wait_send()
                self.across(step, 1).wait_send()

    def fetch(parts, sem):
        if sz.whole:
            copies = [local(buf.at[:, cols], dst, loc.at[sem + i]) for i, (buf, cols, dst) in enumerate(parts)]
            for copy in copies:
                copy.start()

            def wait():
                for copy in copies:
                    copy.wait()

            return wait
        for buf, cols, dst in parts:
            n = dst.shape[-1]

            def step(b):
                rows = span(b * QUADS * RP, QUADS * RP, QUADS * RP)
                move(buf.at[rows, cols], stage.at[:, pl.ds(0, n)], loc.at[sem])
                part = [stage[i * RP : i * RP + RP, :n].astype(F32)[:R] for i in range(QUADS)]
                dst[span(b * R4, R4, R4), :] = jnp.concatenate(part, axis=0).astype(BF)

            loop(O, step)
        return lambda: None

    def y_copy(src, dst, i):
        return remote(src, dst, s_y.at[i], r_y.at[i], over_y)

    QUERY, KEY, VALUE = pl.ds(0, QW), pl.ds(QW, sz.key), pl.ds(QW + sz.key, sz.key)
    REST = pl.ds(QW, 2 * sz.key)
    TT = 2 * T
    seq = TT // 2

    def head_cols(h):
        return pl.ds(h * HEAD_SIZE, HEAD_SIZE)

    def turn(u, sign, rows):
        return u * rope[0, rows, :] + sign * pltpu.roll(u, HEAD_SIZE // 2, 1) * rope[1, rows, :]

    gather_q = Gather(0, wq_ref, gq)
    gather_o = Gather(1, wo_ref, go)
    head = Chunk(None)

    gather_q.start()
    local(tok_ref, tk, loc.at[1]).start()
    gather_o.start()
    local(tok_ref, tk, loc.at[1]).wait()

    def norm_first(i):
        a = span(i * 32, 32, 32)
        values = tk[a, :].astype(F32)
        scale = lax.rsqrt(jnp.mean(values * values, axis=-1, keepdims=True) + norm_eps)
        xa[span(y * T + i * 32, 32, 32), :] = (values * scale * vec[0:1, :]).astype(BF)

    loop(T // 32, norm_first)
    own_half, other_half = span(y * T, T, T), span((1 - y) * T, T, T)
    y_copy(xa.at[own_half, :], xa.at[own_half, :], 0).start()
    sv[...] = jnp.zeros_like(sv)
    gather_q.pass_on()
    gather_q.pass_over()
    gather_q.wait()
    wq_v, wr_v, wo_v = pb.at[0], pb.at[1, :, pl.ds(0, 2 * sz.key)], pb.at[2]
    ready = fetch([(gq, QUERY, wq_v), (gq, REST, wr_v)], 1)
    head.a2a_start()
    if NF > 0:
        Chunk(0).a2a_start()
    y_copy(xa.at[own_half, :], xa.at[other_half, :], 0).wait_recv()
    ready()

    def project(i):
        rows = span(i * seq, seq, seq)
        lin = dot_rows(xa[rows, :], wq_v[...]) + vec[2:3, :QW]
        for h in range(HEADS):
            qkv[rows, head_cols(h)] = turn(lin[:, h * HEAD_SIZE : (h + 1) * HEAD_SIZE], 1.0, rows).astype(BF)
        lin = dot_rows(xa[rows, :], wr_v[...]) + vec[2:3, QW:GW]
        for h in range(sz.key // HEAD_SIZE):
            cut = slice(h * HEAD_SIZE, (h + 1) * HEAD_SIZE)
            qkv[rows, head_cols(HEADS + h)] = turn(lin[:, cut], 1.0, rows).astype(BF)
        qkv[rows, VALUE] = lin[:, sz.key :].astype(BF)

    loop(2, project)
    gather_o.pass_on()
    head.gather_own()
    SHARE = QW // sz.key

    def chances(h, part, queries):
        keys = slice(0, (part + 1) * seq)
        kcol = span(QW + (h // SHARE) * HEAD_SIZE, HEAD_SIZE, HEAD_SIZE)
        scores = dot_right(queries, qkv[keys, kcol]) * FACTOR
        row = lax.broadcasted_iota(jnp.int32, scores.shape, 0) + part * seq
        col = lax.broadcasted_iota(jnp.int32, scores.shape, 1)
        scores = jnp.where(row >= col, scores, -1e30)
        exponent = jnp.exp(scores - jnp.max(scores, axis=-1, keepdims=True))
        return exponent / jnp.sum(exponent, axis=-1, keepdims=True)

    def attend(h):
        qcol = span(h * HEAD_SIZE, HEAD_SIZE, HEAD_SIZE)
        vcol = span(QW + sz.key + (h // SHARE) * HEAD_SIZE, HEAD_SIZE, HEAD_SIZE)
        for part in range(2):
            rows = slice(part * seq, (part + 1) * seq)
            probs = chances(h, part, qkv[rows, qcol]).astype(BF)
            mh[rows, qcol] = dot_rows(probs, qkv[0 : (part + 1) * seq, vcol]).astype(BF)

    loop(HEADS, attend)
    gather_o.pass_over()
    gather_o.wait()
    ready = fetch([(go, pl.ds(0, QW), wo_v)], 1)
    if NF > 0:
        Chunk(0).gather_own()
    ready()
    st[...] = dot_right(mh[other_half, :], wo_v[...]).astype(BF)
    y_copy(st, ar.at[0], 1).start()
    tok_start(cot_ref, cb, 1)
    local(cot_ref, cb.at[mine, :], loc.at[1]).start()
    mid[...] = dot_right(mh[own_half, :], wo_v[...]) + tk[...].astype(F32)
    for kk in range(1, NF):
        Chunk(kk).a2a_start()
    head.gather_middle()
    y_copy(st, ar.at[0], 1).wait_recv()

    def norm_second(i):
        a = span(i * 32, 32, 32)
        values = mid[a, :] + ar[0, a, :].astype(F32)
        mid[a, :] = values
        scale = lax.rsqrt(jnp.mean(values * values, axis=-1, keepdims=True) + norm_eps)
        xb[span(((x * 2 + y) * 2 + c) * T + i * 32, 32, 32), :] = (values * scale * vec[1:2, :]).astype(BF)

    loop(T // 32, norm_second)

    xsrc = xb.at[mine, :]
    tok_start(xsrc, xb, 0)
    local(cot_ref, cb.at[mine, :], loc.at[1]).wait()
    for n in (3, 2, 1, 0):
        tok_take(cot_ref, cb, 1, n)
    if NF > 1:
        Chunk(1).gather_own()
    head.gather_wait()
    head.load().start()
    if NF > 0:
        Chunk(0).gather_middle()
    head.load().wait()

    def tile(ch, rows, first):
        fk = ch.fk
        both = dot_rows(xb[rows, :], ch.wv[:, : 2 * fk])
        back = dot_rows(cb[rows, :], ch.wv[:, 2 * fk :])
        gate, upper = both[:, :fk], both[:, fk:]
        sigma = jax.nn.sigmoid(gate)
        silu = gate * sigma
        ch.hid[rows, :] = (silu * upper).astype(BF)
        gu[rows, :fk] = (back * upper * (sigma * (1.0 + gate * (1.0 - sigma)))).astype(BF)
        gu[rows, fk : 2 * fk] = (back * silu).astype(BF)
        for j in range(0, W, 512):
            cols = slice(j, j + 512)
            total = dot_right(gu[rows, : 2 * fk], ch.wv[cols, : 2 * fk])
            if first:
                nacc[rows, cols] = total
            else:
                nacc[rows, cols] = nacc[rows, cols] + total

    TD = 512 if W % 512 == 0 else 256

    def products(ch):
        fk = ch.fk

        def step(i):
            cols = span(i * TD, TD, TD)
            ch.pb[cols, : 2 * fk] = dot_left(xb[:, cols], gu[:, : 2 * fk]).astype(BF)
            ch.pb[cols, 2 * fk :] = dot_left(cb[:, cols], ch.hid[...]).astype(BF)

        loop(W // TD, step)

    for n in (3, 2, 1, 0):
        tok_take(xsrc, xb, 0, n)
        tile(head, chip_rows(*order[n]), True)
    if NF > 0:
        Chunk(0).gather_wait()
        Chunk(0).load().start()
    products(head)
    head.line.first()

    def body(kk):
        ch, nxt = Chunk(kk), Chunk(lax.min(kk + 1, NF - 1))
        before, two = Chunk(lax.max(kk - 1, 0)), Chunk(lax.max(kk - 2, 0))
        last = kk == NF - 1
        pl.when(kk + 2 < NF)(lambda: Chunk(lax.min(kk + 2, NF - 1)).gather_own())
        ch.load().wait()

        def visit(p):
            xx = jnp.where(p < 2, 1 - x, x)
            yy = jnp.where(p % 2 == 0, 1 - y, y)
            tile(ch, chip_rows(xx, yy), False)

            @pl.when(last)
            def _():
                for n in range(4):
                    pl.when(p == n)(lambda: sum_pair(n, 0).start())
                for n in range(3):
                    pl.when(p == n + 1)(lambda: sum_mid(n, 0))

        loop(4, visit)
        pl.when(last)(lambda: sum_mid(3, 0))
        pl.when(kk < NF - 1)(lambda: nxt.gather_middle())
        products(ch)
        ch.line.first()
        pl.when(kk == 0)(lambda: head.line.middle())
        pl.when(kk == 1)(lambda: head.finish())
        pl.when((kk >= 1) & (kk < NF - 1))(lambda: before.line.middle())
        pl.when((kk >= 2) & (kk < NF - 1))(lambda: two.finish())

        @pl.when(kk < NF - 1)
        def _():
            nxt.gather_wait()
            nxt.load().start()

    loop(NF, body)

    y_copy(st, ar.at[0], 1).wait_send()
    local(cot_ref, st, loc.at[1]).start()
    wo_b, wq_b = cb.at[pl.ds(0, W), pl.ds(0, QW)], xb.at[pl.ds(0, W), pl.ds(0, GW)]
    tok_sent(cot_ref, cb, 1)
    tok_sent(xsrc, xb, 0)
    ready = fetch([(go, pl.ds(0, QW), wo_b), (gq, pl.ds(0, GW), wq_b)], 2)
    local(cot_ref, st, loc.at[1]).wait()

    def back_second(a, grad):
        values = mid[a, :]
        scale = lax.rsqrt(jnp.mean(values * values, axis=-1, keepdims=True) + norm_eps)
        scaled = grad * vec[1:2, :]
        mean = jnp.mean(scaled * values, axis=-1, keepdims=True)
        total = st[a, :].astype(F32) + (scale * scaled - values * (scale * scale * scale) * mean)
        own[a, :] = total
        tk[a, :] = total.astype(BF)
        sv[1:2, :] = sv[1:2, :] + jnp.sum(grad * values * scale, axis=0, keepdims=True)

    sum_close(0, back_second)
    ga[own_half, :] = tk[...]
    y_copy(ga.at[own_half, :], ga.at[own_half, :], 2).start()
    if NF > 1:
        Chunk(NF - 2).line.middle()

    def m_load(kk):
        return local(
            wagf.at[kk, :, pl.ds(2 * WIDE, WIDE)], wv.at[:, span(lax.rem(kk, 2) * WIDE, WIDE, WIDE)], loc.at[8],
        )

    local(wagh.at[:, pl.ds(2 * HK, HK)], wv.at[:, pl.ds(2 * WIDE, HK)], loc.at[0]).start()
    local(wagh.at[:, pl.ds(2 * HK, HK)], wv.at[:, pl.ds(2 * WIDE, HK)], loc.at[0]).wait()
    m_load(0).start()

    def m_first(p):
        rows = span(p * TT, TT, TT)
        nacc[rows, :] = dot_right(hh[rows, :], wv[:, 2 * WIDE : 2 * WIDE + HK])

    loop(4, m_first)

    def m_chunk(kk):
        m_load(kk).wait()
        pl.when(kk + 1 < NF)(lambda: m_load(lax.min(kk + 1, NF - 1)).start())
        cut = span(lax.rem(kk, 2) * WIDE, WIDE, WIDE)

        def m_tile(p):
            rows = span(p * TT, TT, TT)
            for j in range(0, W, 512):
                cols = slice(j, j + 512)
                nacc[rows, cols] = nacc[rows, cols] + dot_right(hf[kk, rows, :], wv[cols, cut])

        loop(4, m_tile)

    loop(NF, m_chunk)
    for n in range(4):
        sum_pair(n, 1).start()
    for n in range(4):
        sum_mid(n, 1)
    ready()
    y_copy(ga.at[own_half, :], ga.at[other_half, :], 2).wait_recv()

    PER = 2 * WIDE // HEAD_SIZE

    def cell(h, level):
        return (level * 2 + h // PER) * TT, span(h % PER * HEAD_SIZE, HEAD_SIZE, HEAD_SIZE)

    grad_mixed = dot_rows(ga[...], wo_b[...]).astype(BF)
    for h in range(HEADS):
        row, cut = cell(h, 1)
        gu[pl.ds(row, TT), cut] = grad_mixed[:, h * HEAD_SIZE : (h + 1) * HEAD_SIZE]

    HR = 2 * LR
    tile_rows = R4 * 128 // math.gcd(R4, 128)
    quads = tile_rows // R4

    def spread_rows(i, values, store):
        for b in range(quads):
            for q_ in range(QUADS):
                rows = values[(b * QUADS + q_) * R : (b * QUADS + q_ + 1) * R]
                if not sz.whole:
                    rows = jnp.concatenate([rows, jnp.zeros((RP - R, rows.shape[1]), F32)], axis=0)
                where = ((q_ % 2) * 2 + q_ // 2) * O + i * quads + b
                store(span(where * RP, RP, RP), rows.astype(BF))

    out_cols = pl.ds(QW, QW)

    def out_products(i):
        cols = span(i * tile_rows, tile_rows, 128)
        values = dot_left(ga[:, cols], mh[...])

        def store(rows, part):
            cb[rows, out_cols] = part

        spread_rows(i, values, store)

    loop(W // tile_rows, out_products)

    class Part:
        def __init__(self, i, pieces, temps, cores, overs, col, near, out):
            self.i, self.pieces, self.temps, self.cores, self.overs = i, pieces, temps, cores, overs
            first = (c * 2 + x) * LR
            self.line = Line(
                NF + 1 + i, RP, [p.at[span(first, LR, RP), :] for p in pieces], col, near, out, temps
            )

        def to_core(self, k):
            rows = span((1 - c) * HR, HR, RP)
            return remote(
                self.pieces[k].at[rows, :], self.cores[k], s_pc.at[self.i + k], r_pc.at[self.i + k], core
            )

        def to_x(self, k):
            rows = span((c * 2 + 1 - x) * LR, LR, RP)
            return remote(
                self.pieces[k].at[rows, :], self.overs[k], s_px.at[self.i + k], r_px.at[self.i + k], over_x
            )

        def send_core(self):
            for k in range(len(self.pieces)):
                self.to_core(k).start()

        def take(self, copies, bufs, start, n):
            for k, p in enumerate(self.pieces):
                copies(k).wait_recv()
                local(bufs[k], self.temps[k].at[pl.ds(0, n), :], loc.at[4 + k]).start()
            for k, p in enumerate(self.pieces):
                local(bufs[k], self.temps[k].at[pl.ds(0, n), :], loc.at[4 + k]).wait()
                add_into(p.at[span(start, n, RP), :], self.temps[k], n)

        def send_x(self):
            self.take(self.to_core, self.cores, c * HR, HR)
            for k in range(len(self.pieces)):
                self.to_x(k).start()

        def send_along(self):
            self.take(self.to_x, self.overs, (c * 2 + x) * LR, LR)
            self.line.first()

        def sent(self):
            for k in range(len(self.pieces)):
                self.to_core(k).wait_send()
                self.to_x(k).wait_send()
            self.line.sent()

    NQ = GW // WIDE
    temp_q = [
        xb.at[pl.ds((k // 2) * HR, HR), pl.ds(GW + (k % 2) * WIDE, WIDE)] for k in range(NQ)
    ]
    part_q = Part(
        0, [hf.at[k] for k in range(NQ)], temp_q,
        [rcq.at[k] for k in range(NQ)], [rxq.at[k] for k in range(NQ)],
        [colq.at[k] for k in range(NQ)], [nearq.at[k] for k in range(NQ)],
        [outq.at[k] for k in range(NQ)],
    )
    part_o = Part(
        NQ, [cb.at[:, out_cols]], [rt.at[:, pl.ds(0, QW)]], [rco], [rxo], [colo], [nearo], [outo]
    )
    part_o.send_core()
    if NF > 2:
        Chunk(NF - 3).finish()

    kv_sums = nacc.at[rows_of(*order[1], c), :]
    kv_sums[:, : 4 * HEAD_SIZE] = jnp.zeros((T, 4 * HEAD_SIZE), F32)

    def attend_back(h):
        qcol = span(h * HEAD_SIZE, HEAD_SIZE, HEAD_SIZE)
        row, cut = cell(h, 1)
        to_row, to_cut = cell(h, 0)
        for part in range(2):
            rows = slice(part * seq, (part + 1) * seq)
            keys = slice(0, (part + 1) * seq)
            queries = qkv[rows, qcol]
            probs = chances(h, part, queries)
            upstream = gu[span(row + part * seq, seq, seq), cut]
            grad_probs = dot_right(upstream, qkv[keys, VALUE])
            inner = jnp.sum(grad_probs * probs, axis=-1, keepdims=True)
            grad_scores = (probs * (grad_probs - inner)).astype(BF)
            grad_queries = dot_rows(grad_scores, qkv[keys, KEY]) * FACTOR
            gu[span(to_row + part * seq, seq, seq), to_cut] = turn(grad_queries, -1.0, rows).astype(BF)
            grad_keys = dot_left(grad_scores, queries) * FACTOR
            grad_values = dot_left(probs.astype(BF), upstream)
            for i in range(part + 1):
                kcut, vcut = head_cols(i), head_cols(2 + i)
                piece = slice(i * seq, (i + 1) * seq)
                kv_sums[:, kcut] = kv_sums[:, kcut] + grad_keys[piece]
                kv_sums[:, vcut] = kv_sums[:, vcut] + grad_values[piece]

    loop(HEADS, attend_back)
    for i in range(2):
        rows = slice(i * seq, (i + 1) * seq)
        row, cut = cell(HEADS, 0)
        gu[pl.ds(row + i * seq, seq), cut] = turn(kv_sums[:, head_cols(i)], -1.0, rows).astype(BF)
        row, cut = cell(HEADS + 1, 0)
        gu[pl.ds(row + i * seq, seq), cut] = kv_sums[:, head_cols(2 + i)].astype(BF)

    half_cols = 2 * WIDE

    def lin_back(start):
        return dot_right(
            gu[span(start, T, T), :], wq_b[:, :half_cols]
        ) + dot_right(gu[span(TT + start, T, T), :], wq_b[:, half_cols:])

    st[...] = lin_back((1 - y) * T).astype(BF)
    y_copy(st, ar.at[1], 3).start()

    def lin_products(i):
        cols = span(i * tile_rows, tile_rows, 128)
        for side in range(2):
            values = dot_left(xa[:, cols], gu[side * TT : (side + 1) * TT, :])

            def store(rows, part):
                hf[2 * side, rows, :] = part[:, :WIDE]
                hf[2 * side + 1, rows, :] = part[:, WIDE:]

            spread_rows(i, values, store)

    loop(W // tile_rows, lin_products)
    part_q.send_core()
    part_o.send_x()
    grad_lin = nacc.at[rows_of(*order[0], c), :]
    grad_lin[...] = lin_back(y * T)
    for side in range(2):
        cut = slice(side * half_cols, (side + 1) * half_cols)
        sums = jnp.sum(gu[side * TT : (side + 1) * TT, :].astype(F32), axis=0, keepdims=True)
        sv[2:3, cut] = sums
    part_q.send_x()
    tokens_again = ga.at[other_half, :]
    y_copy(ga.at[own_half, :], ga.at[own_half, :], 2).wait_send()
    local(tok_ref, tokens_again, loc.at[1]).start()
    part_o.send_along()
    Chunk(NF - 1).line.middle()
    if NF > 1:
        Chunk(NF - 2).finish()
    part_q.send_along()
    local(tok_ref, tokens_again, loc.at[1]).wait()
    y_copy(st, ar.at[1], 3).wait()

    def back_first(i):
        a = span(i * 32, 32, 32)
        values = tokens_again[a, :].astype(F32)
        grad = grad_lin[a, :] + ar[1, a, :].astype(F32)
        scale = lax.rsqrt(jnp.mean(values * values, axis=-1, keepdims=True) + norm_eps)
        scaled = grad * vec[0:1, :]
        mean = jnp.mean(scaled * values, axis=-1, keepdims=True)
        own[a, :] = own[a, :] + (scale * scaled - values * (scale * scale * scale) * mean)
        sv[0:1, :] = sv[0:1, :] + jnp.sum(grad * values * scale, axis=0, keepdims=True)

    loop(T // 32, back_first)
    local(own, gtok_ref, loc.at[1]).start()

    def small(dq, dy):
        to_q, to_y = lax.rem(q + dq, QUADS), lax.rem(y + dy, 2)
        return remote(
            sv, svr.at[q * 2 + y], s_v.at[dq * 2 + dy], r_v.at[q * 2 + y], at(o, to_q, to_y)
        )

    def small_from(dq, dy):
        from_q, from_y = lax.rem(q + dq, QUADS), lax.rem(y + dy, 2)
        return remote(
            sv, svr.at[from_q * 2 + from_y], s_v.at[dq * 2 + dy],
            r_v.at[from_q * 2 + from_y], at(o, from_q, from_y),
        )

    def small_along(step):
        return remote(sv, svz.at[o], s_vz.at[step], r_vz.at[o], at(lax.rem(o + step, O), q, y))

    def small_along_from(step):
        place = lax.rem(o + step, O)
        return remote(sv, svz.at[place], s_vz.at[step], r_vz.at[place], at(place, q, y))

    peers = [(dq, dy) for dq in range(QUADS) for dy in range(2) if dq or dy]
    for dq, dy in peers:
        small(dq, dy).start()
    svr[q * 2 + y] = sv[...]

    part_o.line.middle()

    def layer_out(a, total):
        tk[a, :] = (mid[a, :] + total).astype(BF)

    sum_close(1, layer_out)
    local(tk, mixed_ref, loc.at[2]).start()
    for dq, dy in peers:
        small_from(dq, dy).wait_recv()
        small(dq, dy).wait_send()
    gains = svr[0]
    for i in range(1, 2 * QUADS):
        gains = gains + svr[i]
    biases = svr[y]
    for i in range(1, QUADS):
        biases = biases + svr[i * 2 + y]
    sv[...] = gains
    sv[2:3, :] = biases[2:3, :]
    for step in range(1, O):
        small_along(step).start()
    svz[o] = sv[...]
    part_q.line.middle()
    Chunk(NF - 1).finish()
    part_o.line.last()
    local(part_o.line.block(0, o), gao_ref, loc.at[3]).start()
    for step in range(1, O):
        small_along_from(step).wait_recv()
        small_along(step).wait_send()
    total = svz[0]
    for i in range(1, O):
        total = total + svz[i]
    sv[...] = total
    local(sv, sums_ref, loc.at[8]).start()
    part_q.line.last()
    for k in range(NQ):
        local(part_q.line.block(k, o), gaq_ref.at[k], loc.at[4 + k]).start()

    gather_q.sent()
    gather_o.sent()
    y_copy(xa.at[own_half, :], xa.at[own_half, :], 0).wait_send()
    part_o.sent()
    part_q.sent()
    head.finished()
    loop(NF, lambda kk: Chunk(kk).finished())
    local(own, gtok_ref, loc.at[1]).wait()
    local(tk, mixed_ref, loc.at[2]).wait()
    local(part_o.line.block(0, o), gao_ref, loc.at[3]).wait()
    local(sv, sums_ref, loc.at[8]).wait()
    for k in range(NQ):
        local(part_q.line.block(k, o), gaq_ref.at[k], loc.at[4 + k]).wait()


def layer(sz, tokens, cotangent, wq, wo, wh, wf, vec, rope):
    O, NF, T = sz.outer, sz.full, sz.tokens
    H = O // 2
    HK, W, RP = sz.head, sz.wide, sz.pad
    R4, LR = QUADS * sz.rows, O * sz.pad
    HR = 2 * LR
    QW, GW = sz.query, sz.query + 2 * sz.key
    NQ = GW // WIDE
    PT = 2 * QUADS * T
    NL = NF + 1 + NQ + 1
    A, B = 3 * HK, 3 * WIDE
    out = jax.ShapeDtypeStruct
    outs = [
        out((QUADS, RP, A), BF),
        out((NF, QUADS, RP, B), BF),
        out((NQ, RP, WIDE), BF),
        out((RP, QW), BF),
        out((T, W), BF),
        out((T, W), F32),
        out((8, W), F32),
        out((W, A), BF),
        out((NF, W, B), BF),
        out((H, H * R4, A), BF),
        out((NF, H, H * R4, B), BF),
        out((H, R4, A), BF),
        out((NF, H, R4, B), BF),
        out((R4, A), BF),
        out((NF, R4, B), BF),
        out((2, 4, T, W), F32),
        out((2, 3, T, W), BF),
        out((sz.dp * RP, GW), BF),
        out((sz.dp * RP, QW), BF),
        out((NQ, HR, WIDE), BF),
        out((HR, QW), BF),
        out((NQ, LR, WIDE), BF),
        out((LR, QW), BF),
        out((NQ, H, H * RP, WIDE), BF),
        out((H, H * RP, QW), BF),
        out((NQ, H, RP, WIDE), BF),
        out((H, RP, QW), BF),
        out((NQ, RP, WIDE), BF),
        out((RP, QW), BF),
    ]
    if not sz.whole:
        outs += [out((QUADS, RP, A), BF), out((NF, QUADS, RP, B), BF)]
    dma = pltpu.SemaphoreType.DMA
    vm = pltpu.VMEM
    scratch = [
        vm((PT, W), BF),
        vm((PT, W), BF),
        vm((PT, W), F32),
        vm((W, B), BF),
        vm((W, A), BF),
        vm((NF, W, B), BF),
        vm((PT, HK), BF),
        vm((NF, PT, WIDE), BF),
        vm((PT, 2 * WIDE), BF),
        vm((3, T, W), BF),
        vm((T, W), BF),
        vm((max(W // 2, HR), B), BF),
        vm((T, W), F32),
        vm((2 * T, W), BF),
        vm((2 * T, GW), BF),
        vm((2 * T, QW), BF),
        vm((2, T, W), BF),
        vm((T, W), BF),
        vm((T, W), F32),
        vm((2 * T, W), BF),
        vm((8, W), F32),
        vm((2 * QUADS, 8, W), F32),
        vm((O, 8, W), F32),
        dma((NF + 1, 4)),
        dma((NF + 1, 3)),
        dma((NF + 1, H)),
        dma((NF + 1, H)),
        dma((NF + 1,)),
        dma((NF + 1, H)),
        dma((NF + 1, H)),
        dma((NF + 1,)),
        dma((NL,)),
        dma((NL, H)),
        dma((NL, H)),
        dma((NL, H)),
        dma((NL, H)),
        dma((NL,)),
        dma((NF + 1, 4)),
        dma((NF + 1, 3)),
        dma((2, 7)),
        dma((2, 7)),
        dma((2, 7)),
        dma((2, 7)),
        dma((4,)),
        dma((4,)),
        dma((2, O)),
        dma((2, O)),
        dma((2, O)),
        dma((2, O)),
        dma((2, 2, O)),
        dma((2, 2, O)),
        dma((NQ + 1,)),
        dma((NQ + 1,)),
        dma((NQ + 1,)),
        dma((NQ + 1,)),
        dma((2 * QUADS,)),
        dma((2 * QUADS,)),
        dma((O,)),
        dma((O,)),
        dma((12,)),
    ]
    if not sz.whole:
        scratch += [vm((QUADS * RP, max(B, GW)), BF), vm((R4, B), BF)]
    any_spec = pl.BlockSpec(memory_space=pl.ANY)
    vmem_spec = pl.BlockSpec(memory_space=pltpu.VMEM)
    results = pl.pallas_call(
        lambda *refs: layer_kernel(sz, *refs),
        out_shape=outs,
        in_specs=[any_spec] * 6 + [vmem_spec] * 2,
        out_specs=[any_spec] * len(outs),
        scratch_shapes=scratch,
        compiler_params=pltpu.CompilerParams(
            collective_id=0, has_side_effects=True, vmem_limit_bytes=64 << 20
        ),
        name="layer",
    )(tokens, cotangent, wq, wo, wh, wf, vec, rope)
    return results[:7]


def per_device(
    sz,
    tokens,
    w_query,
    key_weight,
    value_weight,
    b_query,
    key_bias,
    value_bias,
    w_out,
    gain_attn,
    gain_mlp,
    w_gate,
    w_up,
    w_down,
    cotangent,
):
    rows, hidden_units = w_gate.shape
    more = sz.pad - sz.rows
    w3 = jnp.stack([w_gate, w_up, w_down.T])
    w3 = jnp.pad(w3, ((0, 0), (0, more), (0, QUADS * sz.slice - hidden_units)))
    w3 = w3.reshape(3, sz.pad, QUADS, sz.slice)
    wh = w3[..., : sz.head].transpose(2, 1, 0, 3).reshape(QUADS, sz.pad, 3 * sz.head)
    wf = w3[..., sz.head :].reshape(3, sz.pad, QUADS, sz.full, WIDE)
    wf = wf.transpose(3, 2, 1, 0, 4).reshape(sz.full, QUADS, sz.pad, 3 * WIDE)
    wq = jnp.concatenate([w_query, key_weight, value_weight], axis=1)
    wq = jnp.pad(wq, ((0, more), (0, 0)))
    wo = jnp.pad(w_out.T, ((0, more), (0, 0)))
    bias = jnp.concatenate([b_query, key_bias, value_bias]).astype(F32)
    bias = jnp.pad(bias, (0, sz.wide - bias.shape[0]))
    vec = jnp.stack([gain_attn.astype(F32), gain_mlp.astype(F32), bias])
    vec = jnp.pad(vec, ((0, 5), (0, 0)))
    cosine, sine = rope_tables(SEQUENCE_TOKENS, HEAD_SIZE)
    midway = HEAD_SIZE // 2
    signed = jnp.concatenate([-sine[..., :midway], sine[..., midway:]], axis=-1)
    rope = jnp.stack([cosine[0, :, 0, :], signed[0, :, 0, :]])

    grad_head, grad_full, grad_q, grad_o, mixed, grad_tokens, sums = layer(
        sz, tokens, cotangent, wq, wo, wh, wf, vec, rope
    )
    grad_head = grad_head.reshape(QUADS, sz.pad, 3, sz.head).transpose(2, 1, 0, 3)
    grad_full = grad_full.reshape(sz.full, QUADS, sz.pad, 3, WIDE).transpose(3, 2, 1, 0, 4)
    grad_full = grad_full.reshape(3, sz.pad, QUADS, sz.full * WIDE)
    grads = jnp.concatenate([grad_head, grad_full], axis=-1)
    grads = grads.reshape(3, sz.pad, QUADS * sz.slice)[:, :rows, :hidden_units].astype(F32)
    grad_q = grad_q.transpose(1, 0, 2).reshape(sz.pad, -1)[:rows].astype(F32)
    grad_o = grad_o[:rows].astype(F32)
    cuts = (sz.query, sz.query + sz.key, sz.query + 2 * sz.key)
    return (
        mixed,
        grad_tokens,
        grad_q[:, : cuts[0]],
        grad_q[:, cuts[0] : cuts[1]],
        grad_q[:, cuts[1] :],
        sums[2, : cuts[0]],
        sums[2, cuts[0] : cuts[1]],
        sums[2, cuts[1] : cuts[2]],
        grad_o.T,
        sums[0],
        sums[1],
        grads[0],
        grads[1],
        grads[2].T,
    )


def solution(mesh):
    dp = mesh.shape["dp"]

    def whole(*args):
        def shard(*blocks):
            tokens, w_query, key_weight, w_gate = blocks[0], blocks[1], blocks[2], blocks[10]
            sz = Sizes(dp, w_gate.shape, tokens.shape[0], w_query.shape[1], key_weight.shape[1])
            return per_device(sz, *blocks)

        return jax.shard_map(
            shard, mesh=mesh, in_specs=in_specs, out_specs=out_specs, check_vma=False
        )(*args)

    in_specs = (
        P(("dp", "tensor"), None),
        P("dp", "tensor"),
        P("dp", "tensor"),
        P("dp", "tensor"),
        P("tensor"),
        P("tensor"),
        P("tensor"),
        P("tensor", "dp"),
        P(),
        P(),
        P("dp", "tensor"),
        P("dp", "tensor"),
        P("tensor", "dp"),
        P(("dp", "tensor"), None),
    )
    out_specs = (
        P(("dp", "tensor"), None),
        P(("dp", "tensor"), None),
        P("dp", "tensor"),
        P("dp", "tensor"),
        P("dp", "tensor"),
        P("tensor"),
        P("tensor"),
        P("tensor"),
        P("tensor", "dp"),
        P(),
        P(),
        P("dp", "tensor"),
        P("dp", "tensor"),
        P("tensor", "dp"),
    )
    return whole
```

```python
import math

import jax
import jax.numpy as jnp
from jax import lax
from jax.experimental import pallas as pl
from jax.experimental.pallas import tpu as pltpu
from jax.sharding import PartitionSpec as P

QUERY_HEADS = 12
KEY_VALUE_HEADS = 2
HEAD_SIZE = 128
SEQUENCE_TOKENS = 512

QUADS = 4
WIDE = 256

norm_eps = 1e-06
rope_base = 1000000.0
BF = jnp.bfloat16
F32 = jnp.float32
MESH = pl.DeviceIdType.MESH


def rope_tables(length, columns):
    midway = columns // 2
    inverse = jnp.exp(
        jnp.arange(midway, dtype=jnp.float32) * (-2.0 * math.log(rope_base) / columns)
    )
    angles = jnp.arange(length, dtype=jnp.float32)[:, None] * inverse[None, :]
    angles = jnp.concatenate([angles, angles], axis=-1)
    return (jnp.cos(angles)[None, :, None, :], jnp.sin(angles)[None, :, None, :])


def dot_rows(left, right):
    return jnp.dot(left, right, preferred_element_type=F32)


def dot_left(left, right):
    return lax.dot_general(left, right, (((0,), (0,)), ((), ())), preferred_element_type=F32)


def dot_right(left, right):
    return lax.dot_general(left, right, (((1,), (1,)), ((), ())), preferred_element_type=F32)


def round_up(value, step):
    return (value + step - 1) // step * step


class Sizes:
    def __init__(self, dp, gate_shape, tokens, query, key):
        self.dp = dp
        self.outer = dp // QUADS
        self.rows, self.hidden = gate_shape
        self.pad = round_up(self.rows, 16)
        self.whole = self.pad == self.rows
        self.wide = dp * self.rows
        self.slice = round_up(-(-self.hidden // QUADS), 128)
        self.head = self.slice % WIDE or WIDE
        self.full = (self.slice - self.head) // WIDE
        self.tokens, self.query, self.key = tokens, query, key


def layer_kernel(sz, *refs):
    refs = iter(refs)

    def some(n):
        return [next(refs) for _ in range(n)]

    tok_ref, cot_ref, wq_ref, wo_ref, wh_ref, wf_ref, vec, rope = some(8)
    gh_ref, gf_ref, gaq_ref, gao_ref, mixed_ref, gtok_ref, sums_ref = some(7)
    wagh, wagf, colh, colf, nearh, nearf, outh, outf = some(8)
    pairbuf, chipbuf, gq, go = some(4)
    rcq, rco, rxq, rxo, colq, colo, nearq, nearo, outq, outo = some(10)
    abh, abf = (None, None) if sz.whole else some(2)
    xb, cb, nacc, wv, pbh, pb, hh, hf, gu, nsd, tk, rt, own = some(13)
    xa, qkv, mh, ar, st, mid, ga, sv, svr, svz = some(10)
    s_a2a, r_a2a, s_own, r_own, s_far, r_far, s_fwd, r_fwd = some(8)
    s_col, r_col, s_nr, r_nr, s_out, r_out, s_fin, r_fin = some(8)
    s_tok, r_tok, s_sum, r_sum, s_y, r_y, s_gz, r_gz, s_gx, r_gx, s_gc, r_gc = some(12)
    s_pc, r_pc, s_px, r_px, s_v, r_v, s_vz, r_vz, loc = some(9)
    stage, joined = (None, None) if sz.whole else some(2)

    O, NF, T = sz.outer, sz.full, sz.tokens
    H = O // 2
    HK, W, R, RP = sz.head, sz.wide, sz.rows, sz.pad
    R4, LR = QUADS * R, O * RP
    QW = sz.query
    GW = sz.query + 2 * sz.key
    HEADS = QW // HEAD_SIZE
    FACTOR = 1.0 / math.sqrt(HEAD_SIZE)
    me = lax.axis_index("dp")
    y = lax.axis_index("tensor")
    o, q = me // QUADS, me % QUADS
    x, c = q // 2, q % 2
    half, pos = o // H, o % H
    base, far = half * H, (1 - half) * H
    middle_pos = (1 - half) * (H - 1)
    is_middle = pos == middle_pos

    def at(o_, q_, y_):
        return (o_ * QUADS + q_, y_)

    mid_dev = at(base + middle_pos, q, y)
    far_mid = at(far + half * (H - 1), q, y)
    core = at(o, x * 2 + 1 - c, y)
    over_x = at(o, (1 - x) * 2 + c, y)
    over_y = at(o, q, 1 - y)
    chips = [(1 - x, 1 - y), (1 - x, y), (x, 1 - y)]
    order = chips + [(x, y)]

    def remote(src, dst, ssem, rsem, dev):
        return pltpu.make_async_remote_copy(
            src_ref=src, dst_ref=dst, send_sem=ssem, recv_sem=rsem,
            device_id=dev, device_id_type=MESH,
        )

    def local(src, dst, sem):
        return pltpu.make_async_copy(src, dst, sem)

    def move(src, dst, sem):
        local(src, dst, sem).start()
        local(src, dst, sem).wait()

    def span(start, size, unit):
        return pl.ds(pl.multiple_of(start, unit), size)

    def loop(n, step):
        def run(i, carry):
            step(i)
            return carry

        lax.fori_loop(0, n, run, 0)

    bar = pltpu.get_barrier_semaphore()

    def greet(dev):
        pl.semaphore_signal(bar, inc=1, device_id=dev, device_id_type=MESH)

    for dq in range(QUADS):
        for yy in range(2):
            if dq or yy:
                greet(at(o, lax.rem(q + dq, QUADS), (y + yy) % 2))
    for step in range(1, O):
        greet(at(lax.rem(o + step, O), q, y))
    pl.semaphore_wait(bar, 2 * QUADS - 1 + O - 1)

    def add_into(dst, src, n):
        rows = 32

        def step(i):
            here = span(i * rows, rows, rows)
            dst[here, :] = (dst[here, :].astype(F32) + src[here, :].astype(F32)).astype(BF)

        loop(n // rows, step)

    class Line:
        def __init__(self, i, rows, pieces, col, near, out, temps):
            self.i, self.rows, self.pieces = i, rows, pieces
            self.col, self.near_, self.out, self.temps = col, near, out, temps

        def block(self, k, b, n=1):
            return self.pieces[k].at[span(b * self.rows, n * self.rows, self.rows), :]

        def temp(self, k, start, n):
            return self.temps[k].at[pl.ds(start * self.rows, n * self.rows), :]

        def to_middle(self, k, t):
            return remote(
                self.block(k, far, H), self.col[k].at[t],
                s_col.at[self.i + k], r_col.at[self.i + k, t], mid_dev,
            )

        def near(self, k, to, t):
            return remote(
                self.block(k, base + to), self.near_[k].at[t],
                s_nr.at[self.i + k, to], r_nr.at[self.i + k, t], at(base + to, q, y),
            )

        def cross(self, k):
            return remote(
                self.block(k, far, H), self.out[k], s_out.at[self.i + k], r_out.at[self.i + k], far_mid
            )

        def first(self):
            @pl.when(jnp.logical_not(is_middle))
            def _():
                for k in range(len(self.pieces)):
                    self.to_middle(k, pos).start()
                for k in range(len(self.pieces)):
                    for t in range(H):
                        pl.when(pos != t)(lambda: self.near(k, t, pos).start())

        def far_copy(self, k, t):
            return local(self.col[k].at[t], self.temp(k, 0, H), loc.at[4 + k])

        def far_add(self, t):
            for k in range(len(self.pieces)):
                self.far_copy(k, t).wait()
                add_into(self.block(k, far, H), self.temp(k, 0, H), H * self.rows)

        def far_take(self):
            @pl.when(is_middle)
            def _():
                for i in range(H - 1):
                    t = jnp.where(half == 0, i, i + 1)
                    for k in range(len(self.pieces)):
                        self.to_middle(k, t).wait_recv()
                        self.far_copy(k, t).start()
                    if i < H - 2:
                        self.far_add(t)

        def far_give(self):
            @pl.when(is_middle)
            def _():
                self.far_add(jnp.where(half == 0, H - 2, H - 1))
                for k in range(len(self.pieces)):
                    self.cross(k).start()

        def out_copy(self, k):
            return local(self.out[k], self.temp(k, 0, H), loc.at[4 + k])

        def cross_take(self):
            @pl.when(is_middle)
            def _():
                for k in range(len(self.pieces)):
                    self.cross(k).wait_recv()
                    self.out_copy(k).start()

        def cross_give(self):
            @pl.when(is_middle)
            def _():
                for k in range(len(self.pieces)):
                    self.out_copy(k).wait()
                    add_into(self.block(k, base, H), self.temp(k, 0, H), H * self.rows)
                    for t in range(H):
                        pl.when(pos != t)(lambda: self.near(k, t, pos).start())

        def near_copy(self, k, t):
            return local(self.near_[k].at[t], self.temp(k, 0, 1), loc.at[4 + k])

        def near_add(self, t):
            for k in range(len(self.pieces)):
                self.near_copy(k, t).wait()
                add_into(self.block(k, o), self.temp(k, 0, 1), self.rows)

        def last_take(self):
            for i in range(H - 1):
                t = jnp.where(pos <= i, i + 1, i)
                for k in range(len(self.pieces)):
                    self.near(k, pos, t).wait_recv()
                    self.near_copy(k, t).start()
                if i < H - 2:
                    self.near_add(t)

        def last_give(self):
            self.near_add(jnp.where(pos <= H - 2, H - 1, H - 2))

        def sent(self):
            for k in range(len(self.pieces)):
                pl.when(jnp.logical_not(is_middle))(lambda: self.to_middle(k, pos).wait_send())
                pl.when(is_middle)(lambda: self.cross(k).wait_send())
                for t in range(H):
                    pl.when(pos != t)(lambda: self.near(k, t, pos).wait_send())

    class Chunk:
        def __init__(self, kk):
            self.head = kk is None
            if self.head:
                self.i, self.fk = 0, HK
                self.src, self.wag, self.pb, self.out = wh_ref, wagh, pbh, gh_ref
                self.hid, self.ab = hh, abh
                col, near, out = colh, nearh, outh
            else:
                self.i, self.fk = kk + 1, WIDE
                self.src, self.wag, self.pb, self.out = (
                    wf_ref.at[kk], wagf.at[kk], pb.at[kk], gf_ref.at[kk],
                )
                self.hid, self.ab = hf.at[kk], None if abf is None else abf.at[kk]
                col, near, out = colf.at[kk], nearf.at[kk], outf.at[kk]
            self.cols = pl.ds(0, 3 * self.fk)
            self.wv = wv.at[:, self.cols]
            self.line = Line(self.i, R4, [self.pb], [col], [near], [out], [rt.at[:, self.cols]])

        def block(self, ref, b, n=1):
            return ref.at[span(b * R4, n * R4, R4), :]

        def part(self, ref, b, q_):
            return ref.at[span((b * QUADS + q_) * R, R, R), :]

        def mine(self):
            return self.part(self.wag, o, q) if sz.whole else self.ab.at[q]

        def a2a(self, dq):
            to = lax.rem(q + dq, QUADS)
            return remote(
                self.src.at[to], self.mine(),
                s_a2a.at[self.i, dq - 1], r_a2a.at[self.i, dq - 1], at(o, to, y),
            )

        def a2a_own(self):
            return local(self.src.at[q], self.mine(), s_a2a.at[self.i, 3])

        def a2a_start(self):
            self.a2a_own().start()
            for dq in (1, 2, 3):
                self.a2a(dq).start()

        def join(self):
            for i in range(QUADS):
                move(self.ab.at[i], stage.at[pl.ds(i * RP, RP), self.cols], loc.at[3])
            rows = [stage[i * RP : i * RP + RP, self.cols].astype(F32)[:R] for i in range(QUADS)]
            joined[:, self.cols] = jnp.concatenate(rows, axis=0).astype(BF)
            move(joined.at[:, self.cols], self.block(self.wag, o), loc.at[3])

        def own_to(self, to, t):
            return remote(
                self.block(self.wag, base + t), self.block(self.wag, base + t),
                s_own.at[self.i, to], r_own.at[self.i, t], at(base + to, q, y),
            )

        def half_far(self, half_):
            rows = self.block(self.wag, half_ * H, H)
            return remote(rows, rows, s_far.at[self.i], r_far.at[self.i], far_mid)

        def forward(self, half_, to):
            rows = self.block(self.wag, half_ * H, H)
            return remote(
                rows, rows, s_fwd.at[self.i, to], r_fwd.at[self.i], at(base + to, q, y),
            )

        def gather_own(self):
            self.a2a_own().wait()
            for dq in (1, 2, 3):
                self.a2a(dq).wait_recv()
            if not sz.whole:
                self.join()
            for t in range(H):
                pl.when(pos != t)(lambda: self.own_to(t, pos).start())

        def gather_half(self):
            @pl.when(is_middle)
            def _():
                for t in range(H):
                    pl.when(pos != t)(lambda: self.own_to(pos, t).wait_recv())
                self.half_far(half).start()

        def gather_far(self):
            @pl.when(is_middle)
            def _():
                self.half_far(1 - half).wait_recv()
                for t in range(H):
                    pl.when(pos != t)(lambda: self.forward(1 - half, t).start())

        def gather_wait(self):
            @pl.when(jnp.logical_not(is_middle))
            def _():
                for t in range(H):
                    pl.when(pos != t)(lambda: self.own_to(pos, t).wait_recv())
                self.forward(1 - half, pos).wait_recv()

        def gather_sent(self):
            for dq in (1, 2, 3):
                self.a2a(dq).wait_send()
            pl.when(is_middle)(lambda: self.half_far(half).wait_send())
            for t in range(H):

                @pl.when(pos != t)
                def _():
                    self.own_to(t, pos).wait_send()
                    pl.when(is_middle)(lambda: self.forward(1 - half, t).wait_send())

        def load(self):
            return local(self.wag, self.wv, loc.at[0])

        def result(self, q_):
            return self.part(self.pb, o, q_) if sz.whole else self.ab.at[q_]

        def give(self, dq):
            to = lax.rem(q + dq, QUADS)
            return remote(
                self.result(to), self.out.at[q],
                s_fin.at[self.i, dq - 1], r_fin.at[self.i, dq - 1], at(o, to, y),
            )

        def give_own(self):
            return local(self.result(q), self.out.at[q], s_fin.at[self.i, 3])

        def split(self):
            rows = self.block(self.pb, o)[...].astype(F32)
            for i in range(QUADS):
                part = rows[i * R : (i + 1) * R]
                part = jnp.concatenate([part, jnp.zeros((RP - R, 3 * self.fk), F32)], axis=0)
                stage[i * RP : i * RP + RP, self.cols] = part.astype(BF)
            for i in range(QUADS):
                move(stage.at[pl.ds(i * RP, RP), self.cols], self.ab.at[i], loc.at[3])

        def finish(self):
            self.line.last_take()
            self.finish_give()

        def finish_give(self):
            self.line.last_give()
            if not sz.whole:
                self.split()
            self.give_own().start()
            for dq in (1, 2, 3):
                self.give(dq).start()

        def finished(self):
            self.give_own().wait()
            for dq in (1, 2, 3):
                self.give(dq).wait()
            self.gather_sent()
            self.line.sent()

    def chip_rows(xx, yy):
        return span((xx * 2 + yy) * (2 * T), 2 * T, 2 * T)

    def rows_of(xx, yy, cc):
        return span(((xx * 2 + yy) * 2 + cc) * T, T, T)

    mine = rows_of(x, y, c)

    def tok(src, buf, which, n):
        dev = core if n == 3 else (over_x, over_y)[n - 1]
        return remote(src, buf.at[mine, :], s_tok.at[which, n], r_tok.at[which, n], dev)

    def tok_half(buf, which, n):
        start = rows_of(*chips[n], c).start
        rows = span(start + (n - 1) * (T // 2), T // 2, T // 2)
        return remote(
            buf.at[rows, :], buf.at[rows, :],
            s_tok.at[which, 6 + n], r_tok.at[which, 6 + n], (over_y, over_x)[n - 1],
        )

    def tok_pass(buf, which, n):
        rows = rows_of(*chips[n], c)
        return remote(
            buf.at[rows, :], buf.at[rows, :],
            s_tok.at[which, 4 + n], r_tok.at[which, 4 + n], core,
        )

    def tok_start(src, buf, which):
        for n in (3, 2, 1):
            tok(src, buf, which, n).start()

    def tok_next(src, buf, which):
        for n in (2, 1):
            tok(src, buf, which, n).wait_recv()
            tok_half(buf, which, n).start()
            tok_pass(buf, which, n).start()

    def tok_across(buf, which):
        for n in (2, 1):
            tok_half(buf, which, n).wait_recv()
        tok_pass(buf, which, 0).start()

    def tok_sent(src, buf, which):
        for n in (1, 2, 3):
            tok(src, buf, which, n).wait_send()
        for n in (1, 2):
            tok_half(buf, which, n).wait_send()
        for n in range(3):
            tok_pass(buf, which, n).wait_send()

    def sum_pair(n, which):
        return remote(
            nacc.at[rows_of(*order[n], 1 - c), :], pairbuf.at[which, n],
            s_sum.at[which, n], r_sum.at[which, n], core,
        )

    def sum_chip(n, which):
        xx, yy = chips[n]
        return remote(
            nsd.at[n], chipbuf.at[which, n],
            s_sum.at[which, 4 + n], r_sum.at[which, 4 + n], at(o, xx * 2 + c, yy),
        )

    def sum_fetch(n, which):
        return local(pairbuf.at[which, n], nacc.at[rows_of(*order[n], 1 - c), :], loc.at[12 + n])

    def sum_take(n, which):
        sum_pair(n, which).wait()
        sum_fetch(n, which).start()

    def sum_give(n, which):
        here, spare = nacc.at[rows_of(*order[n], c), :], nacc.at[rows_of(*order[n], 1 - c), :]
        sum_fetch(n, which).wait()

        def step(i):
            a = span(i * 32, 32, 32)
            total = here[a, :] + spare[a, :]
            if n < 3:
                nsd[n, a, :] = total.astype(BF)
            else:
                here[a, :] = total

        loop(T // 32, step)
        if n < 3:
            sum_chip(n, which).start()

    def sum_close(which, finish):
        here = nacc.at[mine, :]
        for n in range(3):
            sum_chip(n, which).wait_recv()
            move(chipbuf.at[which, n], tk, loc.at[7])

            def step(i):
                a = span(i * 32, 32, 32)
                total = here[a, :] + tk[a, :].astype(F32)
                if n < 2:
                    here[a, :] = total
                else:
                    finish(a, total)

            loop(T // 32, step)
        for n in range(3):
            sum_chip(n, which).wait_send()

    class Gather:
        def __init__(self, i, src, buf):
            self.i, self.src, self.buf = i, src, buf

        def rows(self, o_, x_, c_):
            return self.buf.at[span(((o_ * 2 + x_) * 2 + c_) * RP, RP, RP), :]

        def place(self, step):
            return lax.rem(o - step + O, O)

        def send(self, step):
            return remote(
                self.src, self.rows(o, x, c), s_gz.at[self.i, step], r_gz.at[self.i, step],
                at(lax.rem(o + step, O), q, y),
            )

        def over(self, step):
            rows = self.rows(self.place(step), x, c)
            src = self.src if step == 0 else rows
            return remote(src, rows, s_gx.at[self.i, step], r_gx.at[self.i, step], over_x)

        def across(self, step, far_x):
            rows = self.rows(self.place(step), (1 - x) if far_x else x, c)
            src = self.src if step == 0 and not far_x else rows
            return remote(
                src, rows, s_gc.at[self.i, far_x, step], r_gc.at[self.i, far_x, step], core,
            )

        def own(self):
            return local(self.src, self.rows(o, x, c), s_gz.at[self.i, 0])

        def start(self):
            for step in range(1, O):
                self.send(step).start()
            self.over(0).start()
            self.across(0, 0).start()
            self.own().start()

        def pass_on(self):
            for step in range(1, O):
                self.send(step).wait_recv()
                self.over(step).start()
                self.across(step, 0).start()

        def pass_over(self):
            for step in range(O):
                self.over(step).wait_recv()
                self.across(step, 1).start()

        def wait(self):
            for far_x in range(2):
                for step in range(O):
                    self.across(step, far_x).wait_recv()
            self.own().wait()

        def sent(self):
            for step in range(1, O):
                self.send(step).wait_send()
            for step in range(O):
                self.over(step).wait_send()
                self.across(step, 0).wait_send()
                self.across(step, 1).wait_send()

    def fetch(parts, sem):
        if sz.whole:
            copies = [local(buf.at[:, cols], dst, loc.at[sem + i]) for i, (buf, cols, dst) in enumerate(parts)]
            for copy in copies:
                copy.start()

            def wait():
                for copy in copies:
                    copy.wait()

            return wait
        for buf, cols, dst in parts:
            n = dst.shape[-1]

            def step(b):
                rows = span(b * QUADS * RP, QUADS * RP, QUADS * RP)
                move(buf.at[rows, cols], stage.at[:, pl.ds(0, n)], loc.at[sem])
                part = [stage[i * RP : i * RP + RP, :n].astype(F32)[:R] for i in range(QUADS)]
                dst[span(b * R4, R4, R4), :] = jnp.concatenate(part, axis=0).astype(BF)

            loop(O, step)
        return lambda: None

    def y_copy(src, dst, i):
        return remote(src, dst, s_y.at[i], r_y.at[i], over_y)

    QUERY, KEY, VALUE = pl.ds(0, QW), pl.ds(QW, sz.key), pl.ds(QW + sz.key, sz.key)
    REST = pl.ds(QW, 2 * sz.key)
    TT = 2 * T
    seq = TT // 2

    def head_cols(h):
        return pl.ds(h * HEAD_SIZE, HEAD_SIZE)

    def turn(u, sign, rows):
        return u * rope[0, rows, :] + sign * pltpu.roll(u, HEAD_SIZE // 2, 1) * rope[1, rows, :]

    gather_q = Gather(0, wq_ref, gq)
    gather_o = Gather(1, wo_ref, go)
    head = Chunk(None)

    gather_q.start()
    local(tok_ref, tk, loc.at[1]).start()
    head.a2a_start()
    Chunk(0).a2a_start()
    local(tok_ref, tk, loc.at[1]).wait()

    def norm_first(i):
        a = span(i * 32, 32, 32)
        values = tk[a, :].astype(F32)
        scale = lax.rsqrt(jnp.mean(values * values, axis=-1, keepdims=True) + norm_eps)
        xa[span(y * T + i * 32, 32, 32), :] = (values * scale * vec[0:1, :]).astype(BF)

    loop(T // 32, norm_first)
    own_half, other_half = span(y * T, T, T), span((1 - y) * T, T, T)
    y_copy(xa.at[own_half, :], xa.at[own_half, :], 0).start()
    sv[...] = jnp.zeros_like(sv)
    head.gather_own()
    gather_q.pass_on()
    gather_o.start()
    head.gather_half()
    gather_q.pass_over()
    Chunk(0).gather_own()
    gather_q.wait()
    wq_v, wr_v, wo_v = pb.at[0], pb.at[1, :, pl.ds(0, 2 * sz.key)], pb.at[2]
    ready = fetch([(gq, QUERY, wq_v), (gq, REST, wr_v)], 1)
    Chunk(1).a2a_start()
    tok_start(cot_ref, cb, 1)
    local(cot_ref, cb.at[mine, :], loc.at[3]).start()
    y_copy(xa.at[own_half, :], xa.at[other_half, :], 0).wait_recv()
    ready()

    def project(i):
        rows = span(i * seq, seq, seq)
        lin = dot_rows(xa[rows, :], wq_v[...]) + vec[2:3, :QW]
        for h in range(HEADS):
            qkv[rows, head_cols(h)] = turn(lin[:, h * HEAD_SIZE : (h + 1) * HEAD_SIZE], 1.0, rows).astype(BF)
        lin = dot_rows(xa[rows, :], wr_v[...]) + vec[2:3, QW:GW]
        for h in range(sz.key // HEAD_SIZE):
            cut = slice(h * HEAD_SIZE, (h + 1) * HEAD_SIZE)
            qkv[rows, head_cols(HEADS + h)] = turn(lin[:, cut], 1.0, rows).astype(BF)
        qkv[rows, VALUE] = lin[:, sz.key :].astype(BF)

    loop(2, project)
    gather_o.pass_on()
    head.gather_far()
    Chunk(0).gather_half()
    SHARE = QW // sz.key

    def chances(h, part, queries):
        keys = slice(0, (part + 1) * seq)
        kcol = span(QW + (h // SHARE) * HEAD_SIZE, HEAD_SIZE, HEAD_SIZE)
        scores = dot_right(queries, qkv[keys, kcol]) * FACTOR
        row = lax.broadcasted_iota(jnp.int32, scores.shape, 0) + part * seq
        col = lax.broadcasted_iota(jnp.int32, scores.shape, 1)
        scores = jnp.where(row >= col, scores, -1e30)
        exponent = jnp.exp(scores - jnp.max(scores, axis=-1, keepdims=True))
        return exponent / jnp.sum(exponent, axis=-1, keepdims=True)

    def attend(h):
        qcol = span(h * HEAD_SIZE, HEAD_SIZE, HEAD_SIZE)
        vcol = span(QW + sz.key + (h // SHARE) * HEAD_SIZE, HEAD_SIZE, HEAD_SIZE)
        for part in range(2):
            rows = slice(part * seq, (part + 1) * seq)
            probs = chances(h, part, qkv[rows, qcol]).astype(BF)
            mh[rows, qcol] = dot_rows(probs, qkv[0 : (part + 1) * seq, vcol]).astype(BF)

    loop(HEADS, attend)
    gather_o.pass_over()
    Chunk(1).gather_own()
    gather_o.wait()
    ready = fetch([(go, pl.ds(0, QW), wo_v)], 1)
    tok_next(cot_ref, cb, 1)
    ready()
    st[...] = dot_right(mh[other_half, :], wo_v[...]).astype(BF)
    y_copy(st, ar.at[0], 1).start()
    mid[...] = dot_right(mh[own_half, :], wo_v[...]) + tk[...].astype(F32)
    Chunk(2).a2a_start()
    Chunk(0).gather_far()
    Chunk(1).gather_half()
    tok_across(cb, 1)
    y_copy(st, ar.at[0], 1).wait_recv()

    def norm_second(i):
        a = span(i * 32, 32, 32)
        values = mid[a, :] + ar[0, a, :].astype(F32)
        mid[a, :] = values
        scale = lax.rsqrt(jnp.mean(values * values, axis=-1, keepdims=True) + norm_eps)
        xb[span(((x * 2 + y) * 2 + c) * T + i * 32, 32, 32), :] = (values * scale * vec[1:2, :]).astype(BF)

    loop(T // 32, norm_second)

    xsrc = xb.at[mine, :]
    tok_start(xsrc, xb, 0)
    local(cot_ref, cb.at[mine, :], loc.at[3]).wait()
    tok(cot_ref, cb, 1, 3).wait_recv()
    for n in range(3):
        tok_pass(cb, 1, n).wait_recv()
    head.gather_wait()
    head.load().start()
    Chunk(2).gather_own()
    head.load().wait()

    def tile(ch, rows, first):
        fk = ch.fk
        both = dot_rows(xb[rows, :], ch.wv[:, : 2 * fk])
        back = dot_rows(cb[rows, :], ch.wv[:, 2 * fk :])
        gate, upper = both[:, :fk], both[:, fk:]
        sigma = jax.nn.sigmoid(gate)
        silu = gate * sigma
        ch.hid[rows, :] = (silu * upper).astype(BF)
        gu[rows, :fk] = (back * upper * (sigma * (1.0 + gate * (1.0 - sigma)))).astype(BF)
        gu[rows, fk : 2 * fk] = (back * silu).astype(BF)
        for j in range(0, W, 512):
            cols = slice(j, j + 512)
            total = dot_right(gu[rows, : 2 * fk], ch.wv[cols, : 2 * fk])
            if first:
                nacc[rows, cols] = total
            else:
                nacc[rows, cols] = nacc[rows, cols] + total

    TD = 512 if W % 512 == 0 else 256

    def products(ch):
        fk = ch.fk

        def step(i):
            cols = span(i * TD, TD, TD)
            ch.pb[cols, : 2 * fk] = dot_left(xb[:, cols], gu[:, : 2 * fk]).astype(BF)
            ch.pb[cols, 2 * fk :] = dot_left(cb[:, cols], ch.hid[...]).astype(BF)

        loop(W // TD, step)

    tok(xsrc, xb, 0, 3).wait_recv()
    tile(head, chip_rows(*order[3]), True)
    tok_next(xsrc, xb, 0)
    tok_pass(xb, 0, 2).wait_recv()
    tile(head, chip_rows(*order[2]), True)
    Chunk(1).gather_far()
    Chunk(2).gather_half()
    tok_pass(xb, 0, 1).wait_recv()
    tile(head, chip_rows(*order[1]), True)
    tok_across(xb, 0)
    for kk in range(3, NF):
        Chunk(kk).a2a_start()
    Chunk(0).gather_wait()
    tok_pass(xb, 0, 0).wait_recv()
    tile(head, chip_rows(*order[0]), True)
    Chunk(0).load().start()
    products(head)
    head.line.first()

    def body(kk):
        ch, nxt = Chunk(kk), Chunk(lax.min(kk + 1, NF - 1))
        two, three = Chunk(lax.max(kk - 2, 0)), Chunk(lax.max(kk - 3, 0))
        last = kk == NF - 1
        later = Chunk(lax.min(kk + 3, NF - 1))
        pl.when(kk + 3 < NF)(later.gather_own)
        ch.load().wait()

        def visit(p):
            for n in range(3):
                pl.when(last & (p == n + 1))(lambda: sum_take(n, 0))
            pl.when((kk == 1) & (p == 1))(head.line.far_take)
            pl.when((kk == 2) & (p == 0))(head.line.cross_take)
            pl.when((kk >= 2) & (kk < NF - 1) & (p == 2))(two.line.far_take)
            pl.when((kk == 3) & (p == 0))(head.line.last_take)
            xx = jnp.where(p < 2, 1 - x, x)
            yy = jnp.where(p % 2 == 0, 1 - y, y)
            tile(ch, chip_rows(xx, yy), False)
            for n in range(4):
                pl.when(last & (p == n))(lambda: sum_pair(n, 0).start())
            for n in range(3):
                pl.when(last & (p == n + 1))(lambda: sum_give(n, 0))

            pl.when((kk == 1) & (p == 1))(head.line.far_give)
            pl.when((kk == 2) & (p == 0))(head.line.cross_give)
            pl.when((kk >= 2) & (kk < NF - 1) & (p == 2))(two.line.far_give)
            pl.when((kk == 3) & (p == 0))(head.finish_give)
            pl.when((kk + 3 < NF) & (p == 2))(later.gather_half)

        loop(4, visit)
        pl.when(last)(lambda: sum_take(3, 0))

        @pl.when(kk < NF - 1)
        def _():
            pl.when(kk == 0)(Chunk(1).gather_wait)
            pl.when(kk > 1)(nxt.gather_far)
            pl.when(kk > 0)(nxt.gather_wait)
            nxt.load().start()

        pl.when(kk >= 3)(three.line.cross_take)
        products(ch)
        ch.line.first()
        pl.when(kk >= 3)(three.line.cross_give)
        pl.when(last)(lambda: sum_give(3, 0))
        pl.when(kk == 0)(Chunk(2).gather_far)

    loop(NF, body)

    y_copy(st, ar.at[0], 1).wait_send()
    local(cot_ref, st, loc.at[1]).start()
    wo_b, wq_b = cb.at[pl.ds(0, W), pl.ds(0, QW)], xb.at[pl.ds(0, W), pl.ds(0, GW)]
    tok_sent(cot_ref, cb, 1)
    tok_sent(xsrc, xb, 0)
    ready = fetch([(go, pl.ds(0, QW), wo_b), (gq, pl.ds(0, GW), wq_b)], 2)
    local(cot_ref, st, loc.at[1]).wait()

    def back_second(a, grad):
        values = mid[a, :]
        scale = lax.rsqrt(jnp.mean(values * values, axis=-1, keepdims=True) + norm_eps)
        scaled = grad * vec[1:2, :]
        mean = jnp.mean(scaled * values, axis=-1, keepdims=True)
        total = st[a, :].astype(F32) + (scale * scaled - values * (scale * scale * scale) * mean)
        own[a, :] = total
        tk[a, :] = total.astype(BF)
        sv[1:2, :] = sv[1:2, :] + jnp.sum(grad * values * scale, axis=0, keepdims=True)

    sum_close(0, back_second)
    ga[own_half, :] = tk[...]
    y_copy(ga.at[own_half, :], ga.at[own_half, :], 2).start()
    Chunk(NF - 3).line.far_take()

    def m_load(kk):
        return local(
            wagf.at[kk, :, pl.ds(2 * WIDE, WIDE)], wv.at[:, span(lax.rem(kk, 2) * WIDE, WIDE, WIDE)], loc.at[8],
        )

    move(wagh.at[:, pl.ds(2 * HK, HK)], wv.at[:, pl.ds(2 * WIDE, HK)], loc.at[0])
    m_load(0).start()

    def m_first(p):
        rows = span(p * TT, TT, TT)
        nacc[rows, :] = dot_right(hh[rows, :], wv[:, 2 * WIDE : 2 * WIDE + HK])

    loop(4, m_first)
    Chunk(NF - 3).line.far_give()

    def m_chunk(kk):
        m_load(kk).wait()
        pl.when(kk + 1 < NF)(lambda: m_load(lax.min(kk + 1, NF - 1)).start())
        cut = span(lax.rem(kk, 2) * WIDE, WIDE, WIDE)

        def m_tile(p):
            rows = span(p * TT, TT, TT)
            for j in range(0, W, 512):
                cols = slice(j, j + 512)
                nacc[rows, cols] = nacc[rows, cols] + dot_right(hf[kk, rows, :], wv[cols, cut])

        loop(4, m_tile)

    loop(NF, m_chunk)
    for n in range(4):
        sum_pair(n, 1).start()
    for n in range(4):
        sum_take(n, 1)
    for n in range(4):
        sum_give(n, 1)
    ready()
    y_copy(ga.at[own_half, :], ga.at[other_half, :], 2).wait_recv()

    PER = 2 * WIDE // HEAD_SIZE

    def cell(h, level):
        return (level * 2 + h // PER) * TT, span(h % PER * HEAD_SIZE, HEAD_SIZE, HEAD_SIZE)

    grad_mixed = dot_rows(ga[...], wo_b[...]).astype(BF)
    for h in range(HEADS):
        row, cut = cell(h, 1)
        gu[pl.ds(row, TT), cut] = grad_mixed[:, h * HEAD_SIZE : (h + 1) * HEAD_SIZE]

    HR = 2 * LR
    tile_rows = R4 * 128 // math.gcd(R4, 128)
    quads = tile_rows // R4

    def spread_rows(i, values, store):
        for b in range(quads):
            for q_ in range(QUADS):
                rows = values[(b * QUADS + q_) * R : (b * QUADS + q_ + 1) * R]
                if not sz.whole:
                    rows = jnp.concatenate([rows, jnp.zeros((RP - R, rows.shape[1]), F32)], axis=0)
                where = ((q_ % 2) * 2 + q_ // 2) * O + i * quads + b
                store(span(where * RP, RP, RP), rows.astype(BF))

    out_cols = pl.ds(QW, QW)

    def out_products(i):
        cols = span(i * tile_rows, tile_rows, 128)
        values = dot_left(ga[:, cols], mh[...])

        def store(rows, part):
            cb[rows, out_cols] = part

        spread_rows(i, values, store)

    loop(W // tile_rows, out_products)

    class Part:
        def __init__(self, i, pieces, temps, cores, overs, col, near, out):
            self.i, self.pieces, self.temps, self.cores, self.overs = i, pieces, temps, cores, overs
            first = (c * 2 + x) * LR
            self.line = Line(
                NF + 1 + i, RP, [p.at[span(first, LR, RP), :] for p in pieces], col, near, out, temps
            )

        def to_core(self, k):
            rows = span((1 - c) * HR, HR, RP)
            return remote(
                self.pieces[k].at[rows, :], self.cores[k], s_pc.at[self.i + k], r_pc.at[self.i + k], core
            )

        def to_x(self, k):
            rows = span((c * 2 + 1 - x) * LR, LR, RP)
            return remote(
                self.pieces[k].at[rows, :], self.overs[k], s_px.at[self.i + k], r_px.at[self.i + k], over_x
            )

        def send_core(self):
            for k in range(len(self.pieces)):
                self.to_core(k).start()

        def take(self, copies, bufs, start, n):
            for k, p in enumerate(self.pieces):
                copies(k).wait_recv()
                local(bufs[k], self.temps[k].at[pl.ds(0, n), :], loc.at[4 + k]).start()
            for k, p in enumerate(self.pieces):
                local(bufs[k], self.temps[k].at[pl.ds(0, n), :], loc.at[4 + k]).wait()
                add_into(p.at[span(start, n, RP), :], self.temps[k], n)

        def send_x(self):
            self.take(self.to_core, self.cores, c * HR, HR)
            for k in range(len(self.pieces)):
                self.to_x(k).start()

        def send_along(self):
            self.take(self.to_x, self.overs, (c * 2 + x) * LR, LR)
            self.line.first()

        def sent(self):
            for k in range(len(self.pieces)):
                self.to_core(k).wait_send()
                self.to_x(k).wait_send()
            self.line.sent()

    NQ = GW // WIDE
    temp_q = [
        xb.at[pl.ds((k // 2) * HR, HR), pl.ds(GW + (k % 2) * WIDE, WIDE)] for k in range(NQ)
    ]
    part_q = Part(
        0, [hf.at[k] for k in range(NQ)], temp_q,
        [rcq.at[k] for k in range(NQ)], [rxq.at[k] for k in range(NQ)],
        [colq.at[k] for k in range(NQ)], [nearq.at[k] for k in range(NQ)],
        [outq.at[k] for k in range(NQ)],
    )
    part_o = Part(
        NQ, [cb.at[:, out_cols]], [rt.at[:, pl.ds(0, QW)]], [rco], [rxo], [colo], [nearo], [outo]
    )
    part_o.send_core()
    Chunk(NF - 2).line.far_take()

    kv_sums = nacc.at[rows_of(*order[1], c), :]
    kv_sums[:, : 4 * HEAD_SIZE] = jnp.zeros((T, 4 * HEAD_SIZE), F32)

    def attend_back(h):
        qcol = span(h * HEAD_SIZE, HEAD_SIZE, HEAD_SIZE)
        row, cut = cell(h, 1)
        to_row, to_cut = cell(h, 0)
        for part in range(2):
            rows = slice(part * seq, (part + 1) * seq)
            keys = slice(0, (part + 1) * seq)
            queries = qkv[rows, qcol]
            probs = chances(h, part, queries)
            upstream = gu[span(row + part * seq, seq, seq), cut]
            grad_probs = dot_right(upstream, qkv[keys, VALUE])
            inner = jnp.sum(grad_probs * probs, axis=-1, keepdims=True)
            grad_scores = (probs * (grad_probs - inner)).astype(BF)
            grad_queries = dot_rows(grad_scores, qkv[keys, KEY]) * FACTOR
            gu[span(to_row + part * seq, seq, seq), to_cut] = turn(grad_queries, -1.0, rows).astype(BF)
            grad_keys = dot_left(grad_scores, queries) * FACTOR
            grad_values = dot_left(probs.astype(BF), upstream)
            for i in range(part + 1):
                kcut, vcut = head_cols(i), head_cols(2 + i)
                piece = slice(i * seq, (i + 1) * seq)
                kv_sums[:, kcut] = kv_sums[:, kcut] + grad_keys[piece]
                kv_sums[:, vcut] = kv_sums[:, vcut] + grad_values[piece]

    loop(HEADS, attend_back)
    Chunk(NF - 2).line.far_give()
    for i in range(2):
        rows = slice(i * seq, (i + 1) * seq)
        row, cut = cell(HEADS, 0)
        gu[pl.ds(row + i * seq, seq), cut] = turn(kv_sums[:, head_cols(i)], -1.0, rows).astype(BF)
        row, cut = cell(HEADS + 1, 0)
        gu[pl.ds(row + i * seq, seq), cut] = kv_sums[:, head_cols(2 + i)].astype(BF)

    half_cols = 2 * WIDE

    def lin_back(start):
        return dot_right(
            gu[span(start, T, T), :], wq_b[:, :half_cols]
        ) + dot_right(gu[span(TT + start, T, T), :], wq_b[:, half_cols:])

    st[...] = lin_back((1 - y) * T).astype(BF)
    y_copy(st, ar.at[1], 3).start()
    Chunk(NF - 3).line.cross_take()

    def lin_products(i):
        cols = span(i * tile_rows, tile_rows, 128)
        for side in range(2):
            values = dot_left(xa[:, cols], gu[side * TT : (side + 1) * TT, :])

            def store(rows, part):
                hf[2 * side, rows, :] = part[:, :WIDE]
                hf[2 * side + 1, rows, :] = part[:, WIDE:]

            spread_rows(i, values, store)

    loop(W // tile_rows, lin_products)
    part_q.send_core()
    Chunk(NF - 3).line.cross_give()
    part_o.send_x()
    Chunk(NF - 4).line.last_take()
    grad_lin = nacc.at[rows_of(*order[0], c), :]
    grad_lin[...] = lin_back(y * T)
    for side in range(2):
        cut = slice(side * half_cols, (side + 1) * half_cols)
        sums = jnp.sum(gu[side * TT : (side + 1) * TT, :].astype(F32), axis=0, keepdims=True)
        sv[2:3, cut] = sums
    Chunk(NF - 4).finish_give()
    part_q.send_x()
    Chunk(NF - 2).line.cross_take()
    tokens_again = ga.at[other_half, :]
    y_copy(ga.at[own_half, :], ga.at[own_half, :], 2).wait_send()
    local(tok_ref, tokens_again, loc.at[1]).start()
    Chunk(NF - 2).line.cross_give()
    part_o.send_along()
    Chunk(NF - 3).finish()
    Chunk(NF - 1).line.far_take()
    Chunk(NF - 1).line.far_give()
    part_q.send_along()
    local(tok_ref, tokens_again, loc.at[1]).wait()
    y_copy(st, ar.at[1], 3).wait()

    def back_first(i):
        a = span(i * 32, 32, 32)
        values = tokens_again[a, :].astype(F32)
        grad = grad_lin[a, :] + ar[1, a, :].astype(F32)
        scale = lax.rsqrt(jnp.mean(values * values, axis=-1, keepdims=True) + norm_eps)
        scaled = grad * vec[0:1, :]
        mean = jnp.mean(scaled * values, axis=-1, keepdims=True)
        own[a, :] = own[a, :] + (scale * scaled - values * (scale * scale * scale) * mean)
        sv[0:1, :] = sv[0:1, :] + jnp.sum(grad * values * scale, axis=0, keepdims=True)

    loop(T // 32, back_first)
    local(own, gtok_ref, loc.at[1]).start()

    def small(dq, dy):
        to_q, to_y = lax.rem(q + dq, QUADS), lax.rem(y + dy, 2)
        return remote(
            sv, svr.at[q * 2 + y], s_v.at[dq * 2 + dy], r_v.at[q * 2 + y], at(o, to_q, to_y)
        )

    def small_from(dq, dy):
        from_q, from_y = lax.rem(q + dq, QUADS), lax.rem(y + dy, 2)
        return remote(
            sv, svr.at[from_q * 2 + from_y], s_v.at[dq * 2 + dy],
            r_v.at[from_q * 2 + from_y], at(o, from_q, from_y),
        )

    def small_along(step):
        return remote(sv, svz.at[o], s_vz.at[step], r_vz.at[o], at(lax.rem(o + step, O), q, y))

    def small_along_from(step):
        place = lax.rem(o + step, O)
        return remote(sv, svz.at[place], s_vz.at[step], r_vz.at[place], at(place, q, y))

    peers = [(dq, dy) for dq in range(QUADS) for dy in range(2) if dq or dy]
    for dq, dy in peers:
        small(dq, dy).start()
    svr[q * 2 + y] = sv[...]

    Chunk(NF - 2).finish()
    part_o.line.far_take()
    part_o.line.far_give()

    def layer_out(a, total):
        tk[a, :] = (mid[a, :] + total).astype(BF)

    sum_close(1, layer_out)
    local(tk, mixed_ref, loc.at[2]).start()
    for dq, dy in peers:
        small_from(dq, dy).wait_recv()
        small(dq, dy).wait_send()
    gains = svr[0]
    for i in range(1, 2 * QUADS):
        gains = gains + svr[i]
    biases = svr[y]
    for i in range(1, QUADS):
        biases = biases + svr[i * 2 + y]
    sv[...] = gains
    sv[2:3, :] = biases[2:3, :]
    for step in range(1, O):
        small_along(step).start()
    svz[o] = sv[...]
    part_q.line.far_take()
    part_q.line.far_give()
    Chunk(NF - 1).line.cross_take()
    Chunk(NF - 1).line.cross_give()
    part_o.line.cross_take()
    part_o.line.cross_give()
    part_q.line.cross_take()
    part_q.line.cross_give()
    Chunk(NF - 1).finish()
    part_o.line.last_take()
    part_o.line.last_give()
    local(part_o.line.block(0, o), gao_ref, loc.at[3]).start()
    for step in range(1, O):
        small_along_from(step).wait_recv()
        small_along(step).wait_send()
    total = svz[0]
    for i in range(1, O):
        total = total + svz[i]
    sv[...] = total
    local(sv, sums_ref, loc.at[8]).start()
    part_q.line.last_take()
    part_q.line.last_give()
    for k in range(NQ):
        local(part_q.line.block(k, o), gaq_ref.at[k], loc.at[4 + k]).start()

    gather_q.sent()
    gather_o.sent()
    y_copy(xa.at[own_half, :], xa.at[own_half, :], 0).wait_send()
    part_o.sent()
    part_q.sent()
    head.finished()
    loop(NF, lambda kk: Chunk(kk).finished())
    local(own, gtok_ref, loc.at[1]).wait()
    local(tk, mixed_ref, loc.at[2]).wait()
    local(part_o.line.block(0, o), gao_ref, loc.at[3]).wait()
    local(sv, sums_ref, loc.at[8]).wait()
    for k in range(NQ):
        local(part_q.line.block(k, o), gaq_ref.at[k], loc.at[4 + k]).wait()


def layer(sz, tokens, cotangent, wq, wo, wh, wf, vec, rope):
    O, NF, T = sz.outer, sz.full, sz.tokens
    H = O // 2
    HK, W, RP = sz.head, sz.wide, sz.pad
    R4, LR = QUADS * sz.rows, O * sz.pad
    HR = 2 * LR
    QW, GW = sz.query, sz.query + 2 * sz.key
    NQ = GW // WIDE
    PT = 2 * QUADS * T
    NL = NF + 1 + NQ + 1
    A, B = 3 * HK, 3 * WIDE
    out = jax.ShapeDtypeStruct
    outs = [
        out((QUADS, RP, A), BF),
        out((NF, QUADS, RP, B), BF),
        out((NQ, RP, WIDE), BF),
        out((RP, QW), BF),
        out((T, W), BF),
        out((T, W), F32),
        out((8, W), F32),
        out((W, A), BF),
        out((NF, W, B), BF),
        out((H, H * R4, A), BF),
        out((NF, H, H * R4, B), BF),
        out((H, R4, A), BF),
        out((NF, H, R4, B), BF),
        out((H * R4, A), BF),
        out((NF, H * R4, B), BF),
        out((2, 4, T, W), F32),
        out((2, 3, T, W), BF),
        out((sz.dp * RP, GW), BF),
        out((sz.dp * RP, QW), BF),
        out((NQ, HR, WIDE), BF),
        out((HR, QW), BF),
        out((NQ, LR, WIDE), BF),
        out((LR, QW), BF),
        out((NQ, H, H * RP, WIDE), BF),
        out((H, H * RP, QW), BF),
        out((NQ, H, RP, WIDE), BF),
        out((H, RP, QW), BF),
        out((NQ, H * RP, WIDE), BF),
        out((H * RP, QW), BF),
    ]
    if not sz.whole:
        outs += [out((QUADS, RP, A), BF), out((NF, QUADS, RP, B), BF)]
    dma = pltpu.SemaphoreType.DMA
    vm = pltpu.VMEM
    scratch = [
        vm((PT, W), BF),
        vm((PT, W), BF),
        vm((PT, W), F32),
        vm((W, B), BF),
        vm((W, A), BF),
        vm((NF, W, B), BF),
        vm((PT, HK), BF),
        vm((NF, PT, WIDE), BF),
        vm((PT, 2 * WIDE), BF),
        vm((3, T, W), BF),
        vm((T, W), BF),
        vm((max(W // 2, HR), B), BF),
        vm((T, W), F32),
        vm((2 * T, W), BF),
        vm((2 * T, GW), BF),
        vm((2 * T, QW), BF),
        vm((2, T, W), BF),
        vm((T, W), BF),
        vm((T, W), F32),
        vm((2 * T, W), BF),
        vm((8, W), F32),
        vm((2 * QUADS, 8, W), F32),
        vm((O, 8, W), F32),
        dma((NF + 1, 4)),
        dma((NF + 1, 3)),
        dma((NF + 1, H)),
        dma((NF + 1, H)),
        dma((NF + 1,)),
        dma((NF + 1,)),
        dma((NF + 1, H)),
        dma((NF + 1,)),
        dma((NL,)),
        dma((NL, H)),
        dma((NL, H)),
        dma((NL, H)),
        dma((NL,)),
        dma((NL,)),
        dma((NF + 1, 4)),
        dma((NF + 1, 3)),
        dma((2, 9)),
        dma((2, 9)),
        dma((2, 7)),
        dma((2, 7)),
        dma((4,)),
        dma((4,)),
        dma((2, O)),
        dma((2, O)),
        dma((2, O)),
        dma((2, O)),
        dma((2, 2, O)),
        dma((2, 2, O)),
        dma((NQ + 1,)),
        dma((NQ + 1,)),
        dma((NQ + 1,)),
        dma((NQ + 1,)),
        dma((2 * QUADS,)),
        dma((2 * QUADS,)),
        dma((O,)),
        dma((O,)),
        dma((20,)),
    ]
    if not sz.whole:
        scratch += [vm((QUADS * RP, max(B, GW)), BF), vm((R4, B), BF)]
    any_spec = pl.BlockSpec(memory_space=pl.ANY)
    vmem_spec = pl.BlockSpec(memory_space=pltpu.VMEM)
    results = pl.pallas_call(
        lambda *refs: layer_kernel(sz, *refs),
        out_shape=outs,
        in_specs=[any_spec] * 6 + [vmem_spec] * 2,
        out_specs=[any_spec] * len(outs),
        scratch_shapes=scratch,
        compiler_params=pltpu.CompilerParams(
            collective_id=0, has_side_effects=True, vmem_limit_bytes=64 << 20
        ),
        name="layer",
    )(tokens, cotangent, wq, wo, wh, wf, vec, rope)
    return results[:7]


def per_device(
    sz,
    tokens,
    w_query,
    key_weight,
    value_weight,
    b_query,
    key_bias,
    value_bias,
    w_out,
    gain_attn,
    gain_mlp,
    w_gate,
    w_up,
    w_down,
    cotangent,
):
    rows, hidden_units = w_gate.shape
    more = sz.pad - sz.rows
    w3 = jnp.stack([w_gate, w_up, w_down.T])
    w3 = jnp.pad(w3, ((0, 0), (0, more), (0, QUADS * sz.slice - hidden_units)))
    w3 = w3.reshape(3, sz.pad, QUADS, sz.slice)
    wh = w3[..., : sz.head].transpose(2, 1, 0, 3).reshape(QUADS, sz.pad, 3 * sz.head)
    wf = w3[..., sz.head :].reshape(3, sz.pad, QUADS, sz.full, WIDE)
    wf = wf.transpose(3, 2, 1, 0, 4).reshape(sz.full, QUADS, sz.pad, 3 * WIDE)
    wq = jnp.concatenate([w_query, key_weight, value_weight], axis=1)
    wq = jnp.pad(wq, ((0, more), (0, 0)))
    wo = jnp.pad(w_out.T, ((0, more), (0, 0)))
    bias = jnp.concatenate([b_query, key_bias, value_bias]).astype(F32)
    bias = jnp.pad(bias, (0, sz.wide - bias.shape[0]))
    vec = jnp.stack([gain_attn.astype(F32), gain_mlp.astype(F32), bias])
    vec = jnp.pad(vec, ((0, 5), (0, 0)))
    cosine, sine = rope_tables(SEQUENCE_TOKENS, HEAD_SIZE)
    midway = HEAD_SIZE // 2
    signed = jnp.concatenate([-sine[..., :midway], sine[..., midway:]], axis=-1)
    rope = jnp.stack([cosine[0, :, 0, :], signed[0, :, 0, :]])

    grad_head, grad_full, grad_q, grad_o, mixed, grad_tokens, sums = layer(
        sz, tokens, cotangent, wq, wo, wh, wf, vec, rope
    )
    grad_head = grad_head.reshape(QUADS, sz.pad, 3, sz.head).transpose(2, 1, 0, 3)
    grad_full = grad_full.reshape(sz.full, QUADS, sz.pad, 3, WIDE).transpose(3, 2, 1, 0, 4)
    grad_full = grad_full.reshape(3, sz.pad, QUADS, sz.full * WIDE)
    grads = jnp.concatenate([grad_head, grad_full], axis=-1)
    grads = grads.reshape(3, sz.pad, QUADS * sz.slice)[:, :rows, :hidden_units].astype(F32)
    grad_q = grad_q.transpose(1, 0, 2).reshape(sz.pad, -1)[:rows].astype(F32)
    grad_o = grad_o[:rows].astype(F32)
    cuts = (sz.query, sz.query + sz.key, sz.query + 2 * sz.key)
    return (
        mixed,
        grad_tokens,
        grad_q[:, : cuts[0]],
        grad_q[:, cuts[0] : cuts[1]],
        grad_q[:, cuts[1] :],
        sums[2, : cuts[0]],
        sums[2, cuts[0] : cuts[1]],
        sums[2, cuts[1] : cuts[2]],
        grad_o.T,
        sums[0],
        sums[1],
        grads[0],
        grads[1],
        grads[2].T,
    )


def solution(mesh):
    dp = mesh.shape["dp"]

    def whole(*args):
        def shard(*blocks):
            tokens, w_query, key_weight, w_gate = blocks[0], blocks[1], blocks[2], blocks[10]
            sz = Sizes(dp, w_gate.shape, tokens.shape[0], w_query.shape[1], key_weight.shape[1])
            return per_device(sz, *blocks)

        return jax.shard_map(
            shard, mesh=mesh, in_specs=in_specs, out_specs=out_specs, check_vma=False
        )(*args)

    in_specs = (
        P(("dp", "tensor"), None),
        P("dp", "tensor"),
        P("dp", "tensor"),
        P("dp", "tensor"),
        P("tensor"),
        P("tensor"),
        P("tensor"),
        P("tensor", "dp"),
        P(),
        P(),
        P("dp", "tensor"),
        P("dp", "tensor"),
        P("tensor", "dp"),
        P(("dp", "tensor"), None),
    )
    out_specs = (
        P(("dp", "tensor"), None),
        P(("dp", "tensor"), None),
        P("dp", "tensor"),
        P("dp", "tensor"),
        P("dp", "tensor"),
        P("tensor"),
        P("tensor"),
        P("tensor"),
        P("tensor", "dp"),
        P(),
        P(),
        P("dp", "tensor"),
        P("dp", "tensor"),
        P("tensor", "dp"),
    )
    return whole
```

```python
import math

import jax
import jax.numpy as jnp
import numpy as np
from jax import lax
from jax.experimental import pallas as pl
from jax.experimental.pallas import tpu as pltpu
from jax.sharding import PartitionSpec as P

QUERY_HEADS = 12
KEY_VALUE_HEADS = 2
HEAD_SIZE = 128
SEQUENCE_TOKENS = 512

QUADS = 4
WIDE = 256

norm_eps = 1e-06
rope_base = 1000000.0
BF = jnp.bfloat16
F32 = jnp.float32
MESH = pl.DeviceIdType.MESH


def rope_tables(length, columns):
    midway = columns // 2
    inverse = np.exp(
        np.arange(midway, dtype=np.float32) * np.float32(-2.0 * math.log(rope_base) / columns)
    )
    angles = np.arange(length, dtype=np.float32)[:, None] * inverse[None, :].astype(np.float32)
    cosine, sine = np.cos(angles.astype(np.float64)), np.sin(angles.astype(np.float64))
    tables = np.stack([np.concatenate([cosine, cosine], -1), np.concatenate([-sine, sine], -1)])
    return tables.astype(np.float32)


def dot_rows(left, right):
    return jnp.dot(left, right, preferred_element_type=F32)


def dot_left(left, right):
    return lax.dot_general(left, right, (((0,), (0,)), ((), ())), preferred_element_type=F32)


def dot_right(left, right):
    return lax.dot_general(left, right, (((1,), (1,)), ((), ())), preferred_element_type=F32)


def round_up(value, step):
    return (value + step - 1) // step * step


class Sizes:
    def __init__(self, dp, gate_shape, tokens, query, key):
        self.dp = dp
        self.outer = dp // QUADS
        self.rows, self.hidden = gate_shape
        self.pad = round_up(self.rows, 16)
        self.whole = self.pad == self.rows
        self.wide = dp * self.rows
        self.full = (self.hidden - 1) // (QUADS * WIDE)
        self.rest = self.hidden - self.full * QUADS * WIDE
        self.head = round_up(-(-self.rest // QUADS), 128)
        self.tokens, self.query, self.key = tokens, query, key


def layer_kernel(sz, *refs):
    refs = iter(refs)

    def some(n):
        return [next(refs) for _ in range(n)]

    tok_ref, cot_ref, wq_ref, wo_ref, wh_ref, wg_ref, wu_ref, wd_ref, vec, rope = some(10)
    gw_refs = some(3)
    gwq_ref, gwk_ref, gwv_ref, gao_ref, mixed_ref, gtok_ref, sums_ref, gh_ref, gf_ref = some(9)
    wagh, wagf, colh, colf, nearh, nearf, outh, outf = some(8)
    pairbuf, chipbuf, gq, go = some(4)
    rcq, rco, rxq, rxo, colq, colo, nearq, nearo, outq, outo = some(10)
    abh, abf = (None, None) if sz.whole else some(2)
    xb, cb, nacc, wv, pbh, pb, hh, hf, gu, nsd, tk, rt, own = some(13)
    xa, qkv, mh, ar, st, mid, ga, sv, svr, svz = some(10)
    s_a2a, r_a2a, s_own, r_own, s_far, r_far, s_fwd, r_fwd = some(8)
    s_col, r_col, s_nr, r_nr, s_out, r_out, s_fin, r_fin = some(8)
    s_tok, r_tok, s_sum, r_sum, s_y, r_y, s_gz, r_gz, s_gx, r_gx, s_gc, r_gc = some(12)
    s_pc, r_pc, s_px, r_px, s_v, r_v, s_vz, r_vz, loc = some(9)
    stage, joined = (None, None) if sz.whole else some(2)

    O, NF, T = sz.outer, sz.full, sz.tokens
    H = O // 2
    HK, W, R, RP = sz.head, sz.wide, sz.rows, sz.pad
    R4, LR = QUADS * R, O * RP
    QW = sz.query
    GW = sz.query + 2 * sz.key
    HEADS = QW // HEAD_SIZE
    PIECES = -(-sz.hidden // W)
    FACTOR = 1.0 / math.sqrt(HEAD_SIZE)
    me = lax.axis_index("dp")
    y = lax.axis_index("tensor")
    o, q = me // QUADS, me % QUADS
    x, c = q // 2, q % 2
    half, pos = o // H, o % H
    base, far = half * H, (1 - half) * H
    middle_pos = (1 - half) * (H - 1)
    is_middle = pos == middle_pos

    def at(o_, q_, y_):
        return (o_ * QUADS + q_, y_)

    mid_dev = at(base + middle_pos, q, y)
    far_mid = at(far + half * (H - 1), q, y)
    core = at(o, x * 2 + 1 - c, y)
    over_x = at(o, (1 - x) * 2 + c, y)
    over_y = at(o, q, 1 - y)
    chips = [(1 - x, 1 - y), (1 - x, y), (x, 1 - y)]
    order = chips + [(x, y)]

    def remote(src, dst, ssem, rsem, dev):
        return pltpu.make_async_remote_copy(
            src_ref=src, dst_ref=dst, send_sem=ssem, recv_sem=rsem,
            device_id=dev, device_id_type=MESH,
        )

    def local(src, dst, sem):
        return pltpu.make_async_copy(src, dst, sem)

    def move(src, dst, sem):
        local(src, dst, sem).start()
        local(src, dst, sem).wait()

    def span(start, size, unit):
        return pl.ds(pl.multiple_of(start, unit), size)

    def loop(n, step):
        def run(i, carry):
            step(i)
            return carry

        lax.fori_loop(0, n, run, 0)

    bar = pltpu.get_barrier_semaphore()

    def greet(dev):
        pl.semaphore_signal(bar, inc=1, device_id=dev, device_id_type=MESH)

    for dq in range(QUADS):
        for yy in range(2):
            if dq or yy:
                greet(at(o, lax.rem(q + dq, QUADS), (y + yy) % 2))
    for step in range(1, O):
        greet(at(lax.rem(o + step, O), q, y))
    pl.semaphore_wait(bar, 2 * QUADS - 1 + O - 1)

    def add_into(dst, src, n):
        rows = 32

        def step(i):
            here = span(i * rows, rows, rows)
            dst[here, :] = (dst[here, :].astype(F32) + src[here, :].astype(F32)).astype(BF)

        loop(n // rows, step)

    class Line:
        def __init__(self, i, rows, pieces, col, near, out, temps):
            self.i, self.rows, self.pieces = i, rows, pieces
            self.col, self.near_, self.out, self.temps = col, near, out, temps

        def block(self, k, b, n=1):
            return self.pieces[k].at[span(b * self.rows, n * self.rows, self.rows), :]

        def temp(self, k, start, n):
            return self.temps[k].at[pl.ds(start * self.rows, n * self.rows), :]

        def to_middle(self, k, t):
            return remote(
                self.block(k, far, H), self.col[k].at[t],
                s_col.at[self.i + k], r_col.at[self.i + k, t], mid_dev,
            )

        def near(self, k, to, t):
            return remote(
                self.block(k, base + to), self.near_[k].at[t],
                s_nr.at[self.i + k, to], r_nr.at[self.i + k, t], at(base + to, q, y),
            )

        def cross(self, k):
            return remote(
                self.block(k, far, H), self.out[k], s_out.at[self.i + k], r_out.at[self.i + k], far_mid
            )

        def first(self):
            @pl.when(jnp.logical_not(is_middle))
            def _():
                for k in range(len(self.pieces)):
                    self.to_middle(k, pos).start()
                for k in range(len(self.pieces)):
                    for t in range(H):
                        pl.when(pos != t)(lambda: self.near(k, t, pos).start())

        def far_copy(self, k, t):
            return local(self.col[k].at[t], self.temp(k, 0, H), loc.at[4 + k])

        def far_add(self, t):
            for k in range(len(self.pieces)):
                self.far_copy(k, t).wait()
                add_into(self.block(k, far, H), self.temp(k, 0, H), H * self.rows)

        def far_take(self):
            @pl.when(is_middle)
            def _():
                for i in range(H - 1):
                    t = jnp.where(half == 0, i, i + 1)
                    for k in range(len(self.pieces)):
                        self.to_middle(k, t).wait_recv()
                        self.far_copy(k, t).start()
                    if i < H - 2:
                        self.far_add(t)

        def far_give(self):
            @pl.when(is_middle)
            def _():
                self.far_add(jnp.where(half == 0, H - 2, H - 1))
                for k in range(len(self.pieces)):
                    self.cross(k).start()

        def out_copy(self, k):
            return local(self.out[k], self.temp(k, 0, H), loc.at[4 + k])

        def cross_take(self):
            @pl.when(is_middle)
            def _():
                for k in range(len(self.pieces)):
                    self.cross(k).wait_recv()
                    self.out_copy(k).start()

        def cross_give(self):
            @pl.when(is_middle)
            def _():
                for k in range(len(self.pieces)):
                    self.out_copy(k).wait()
                    add_into(self.block(k, base, H), self.temp(k, 0, H), H * self.rows)
                    for t in range(H):
                        pl.when(pos != t)(lambda: self.near(k, t, pos).start())

        def near_copy(self, k, t):
            return local(self.near_[k].at[t], self.temp(k, 0, 1), loc.at[4 + k])

        def near_add(self, t):
            for k in range(len(self.pieces)):
                self.near_copy(k, t).wait()
                add_into(self.block(k, o), self.temp(k, 0, 1), self.rows)

        def last_take(self):
            for i in range(H - 1):
                t = jnp.where(pos <= i, i + 1, i)
                for k in range(len(self.pieces)):
                    self.near(k, pos, t).wait_recv()
                    self.near_copy(k, t).start()
                if i < H - 2:
                    self.near_add(t)

        def last_give(self):
            self.near_add(jnp.where(pos <= H - 2, H - 1, H - 2))

        def sent(self):
            for k in range(len(self.pieces)):
                pl.when(jnp.logical_not(is_middle))(lambda: self.to_middle(k, pos).wait_send())
                pl.when(is_middle)(lambda: self.cross(k).wait_send())
                for t in range(H):
                    pl.when(pos != t)(lambda: self.near(k, t, pos).wait_send())

    class Chunk:
        def __init__(self, kk):
            self.head = kk is None
            if self.head:
                self.i, self.fk = 0, HK
                self.wag, self.pb, self.out = wagh, pbh, gh_ref
                self.moves = [(wh_ref.at, pl.ds(0, 3 * HK))]
                self.hid, self.ab = hh, abh
                col, near, out = colh, nearh, outh
            else:
                self.i, self.fk = kk + 1, WIDE
                self.kk, self.wag, self.pb, self.out = kk, wagf.at[kk], pb.at[kk], gf_ref.at[kk]
                self.moves = [
                    (ref, pl.ds(m * WIDE, WIDE)) for m, ref in enumerate((wg_ref, wu_ref, wd_ref))
                ]
                self.hid, self.ab = hf.at[kk], None if abf is None else abf.at[kk]
                col, near, out = colf.at[kk], nearf.at[kk], outf.at[kk]
            self.cols = pl.ds(0, 3 * self.fk)
            self.wv = wv.at[:, self.cols]
            self.line = Line(self.i, R4, [self.pb], [col], [near], [out], [rt.at[:, self.cols]])

        def block(self, ref, b, n=1):
            return ref.at[span(b * R4, n * R4, R4), :]

        def part(self, ref, b, q_):
            return ref.at[span((b * QUADS + q_) * R, R, R), :]

        def mine(self):
            return self.part(self.wag, o, q) if sz.whole else self.ab.at[q]

        def source(self, m, to):
            ref = self.moves[m][0]
            return wh_ref.at[to] if self.head else ref.at[:, span((self.kk * QUADS + to) * WIDE, WIDE, WIDE)]

        def a2a(self, m, dq):
            to = lax.rem(q + dq, QUADS)
            return remote(
                self.source(m, to), self.mine().at[:, self.moves[m][1]],
                s_a2a.at[self.i, m, dq - 1], r_a2a.at[self.i, m, dq - 1], at(o, to, y),
            )

        def a2a_own(self, m):
            return local(self.source(m, q), self.mine().at[:, self.moves[m][1]], s_a2a.at[self.i, m, 3])

        def a2a_start(self):
            for m in range(len(self.moves)):
                self.a2a_own(m).start()
                for dq in (1, 2, 3):
                    self.a2a(m, dq).start()

        def join(self):
            for i in range(QUADS):
                move(self.ab.at[i], stage.at[pl.ds(i * RP, RP), self.cols], loc.at[3])
            rows = [stage[i * RP : i * RP + RP, self.cols].astype(F32)[:R] for i in range(QUADS)]
            joined[:, self.cols] = jnp.concatenate(rows, axis=0).astype(BF)
            move(joined.at[:, self.cols], self.block(self.wag, o), loc.at[3])

        def own_to(self, to, t):
            return remote(
                self.block(self.wag, base + t), self.block(self.wag, base + t),
                s_own.at[self.i, to], r_own.at[self.i, t], at(base + to, q, y),
            )

        def half_far(self, half_):
            rows = self.block(self.wag, half_ * H, H)
            return remote(rows, rows, s_far.at[self.i], r_far.at[self.i], far_mid)

        def forward(self, half_, to):
            rows = self.block(self.wag, half_ * H, H)
            return remote(
                rows, rows, s_fwd.at[self.i, to], r_fwd.at[self.i], at(base + to, q, y),
            )

        def gather_own(self):
            for m in range(len(self.moves)):
                self.a2a_own(m).wait()
                for dq in (1, 2, 3):
                    self.a2a(m, dq).wait_recv()
            if not sz.whole:
                self.join()
            for t in range(H):
                pl.when(pos != t)(lambda: self.own_to(t, pos).start())

        def gather_half(self):
            @pl.when(is_middle)
            def _():
                for t in range(H):
                    pl.when(pos != t)(lambda: self.own_to(pos, t).wait_recv())
                self.half_far(half).start()

        def gather_far(self):
            @pl.when(is_middle)
            def _():
                self.half_far(1 - half).wait_recv()
                for t in range(H):
                    pl.when(pos != t)(lambda: self.forward(1 - half, t).start())

        def gather_wait(self):
            @pl.when(jnp.logical_not(is_middle))
            def _():
                for t in range(H):
                    pl.when(pos != t)(lambda: self.own_to(pos, t).wait_recv())
                self.forward(1 - half, pos).wait_recv()

        def gather_sent(self):
            for m in range(len(self.moves)):
                for dq in (1, 2, 3):
                    self.a2a(m, dq).wait_send()
            pl.when(is_middle)(lambda: self.half_far(half).wait_send())
            for t in range(H):

                @pl.when(pos != t)
                def _():
                    self.own_to(t, pos).wait_send()
                    pl.when(is_middle)(lambda: self.forward(1 - half, t).wait_send())

        def load(self):
            return local(self.wag, self.wv, loc.at[0])

        def result(self, q_):
            return self.part(self.pb, o, q_) if sz.whole else self.ab.at[q_]

        def give(self, dq):
            to = lax.rem(q + dq, QUADS)
            return remote(
                self.result(to), self.out.at[q],
                s_fin.at[self.i, dq - 1], r_fin.at[self.i, dq - 1], at(o, to, y),
            )

        def give_own(self):
            return local(self.result(q), self.out.at[q], s_fin.at[self.i, 3])

        def split(self):
            rows = self.block(self.pb, o)[...].astype(F32)
            for i in range(QUADS):
                part = rows[i * R : (i + 1) * R]
                part = jnp.concatenate([part, jnp.zeros((RP - R, 3 * self.fk), F32)], axis=0)
                stage[i * RP : i * RP + RP, self.cols] = part.astype(BF)
            for i in range(QUADS):
                move(stage.at[pl.ds(i * RP, RP), self.cols], self.ab.at[i], loc.at[3])

        def finish(self):
            self.line.last_take()
            self.finish_give()

        def finish_give(self):
            self.line.last_give()
            if not sz.whole:
                self.split()
            self.give_own().start()
            for dq in (1, 2, 3):
                self.give(dq).start()

        def collect(self):
            self.give_own().wait()
            for dq in (1, 2, 3):
                self.give(dq).wait_recv()

            def rows(i):
                return wv.at[span(i * RP, RP, RP), self.cols]

            for i in range(QUADS):
                local(self.out.at[i], rows(i), loc.at[16 + i]).start()
            for i in range(QUADS):
                local(self.out.at[i], rows(i), loc.at[16 + i]).wait()
                if self.head:
                    first, n = NF * QUADS * WIDE + i * HK, min(HK, sz.rest - i * HK)
                else:
                    first, n = (self.kk * QUADS + i) * WIDE, WIDE
                if n > 0:
                    for m in range(3):
                        to = span((m * PIECES + first // W) * RP, RP, RP)
                        nacc[to, span(first % W, n, 128)] = rows(i)[:, m * self.fk : m * self.fk + n].astype(F32)

        def finished(self):
            for dq in (1, 2, 3):
                self.give(dq).wait_send()
            self.gather_sent()
            self.line.sent()

    def chip_rows(xx, yy):
        return span((xx * 2 + yy) * (2 * T), 2 * T, 2 * T)

    def rows_of(xx, yy, cc):
        return span(((xx * 2 + yy) * 2 + cc) * T, T, T)

    mine = rows_of(x, y, c)

    def tok(src, buf, which, n):
        dev = core if n == 3 else (over_x, over_y)[n - 1]
        return remote(src, buf.at[mine, :], s_tok.at[which, n], r_tok.at[which, n], dev)

    def tok_half(buf, which, n):
        start = rows_of(*chips[n], c).start
        rows = span(start + (n - 1) * (T // 2), T // 2, T // 2)
        return remote(
            buf.at[rows, :], buf.at[rows, :],
            s_tok.at[which, 6 + n], r_tok.at[which, 6 + n], (over_y, over_x)[n - 1],
        )

    def tok_pass(buf, which, n):
        rows = rows_of(*chips[n], c)
        return remote(
            buf.at[rows, :], buf.at[rows, :],
            s_tok.at[which, 4 + n], r_tok.at[which, 4 + n], core,
        )

    def tok_start(src, buf, which):
        for n in (3, 2, 1):
            tok(src, buf, which, n).start()

    def tok_next(src, buf, which):
        for n in (2, 1):
            tok(src, buf, which, n).wait_recv()
            tok_half(buf, which, n).start()
            tok_pass(buf, which, n).start()

    def tok_across(buf, which):
        for n in (2, 1):
            tok_half(buf, which, n).wait_recv()
        tok_pass(buf, which, 0).start()

    def tok_sent(src, buf, which):
        for n in (1, 2, 3):
            tok(src, buf, which, n).wait_send()
        for n in (1, 2):
            tok_half(buf, which, n).wait_send()
        for n in range(3):
            tok_pass(buf, which, n).wait_send()

    def sum_pair(n, which):
        return remote(
            nacc.at[rows_of(*order[n], 1 - c), :], pairbuf.at[which, n],
            s_sum.at[which, n], r_sum.at[which, n], core,
        )

    def sum_chip(n, which):
        xx, yy = chips[n]
        return remote(
            nsd.at[n], chipbuf.at[which, n],
            s_sum.at[which, 4 + n], r_sum.at[which, 4 + n], at(o, xx * 2 + c, yy),
        )

    def sum_fetch(n, which):
        return local(pairbuf.at[which, n], nacc.at[rows_of(*order[n], 1 - c), :], loc.at[12 + n])

    def sum_take(n, which):
        sum_pair(n, which).wait()
        sum_fetch(n, which).start()

    def sum_give(n, which):
        here, spare = nacc.at[rows_of(*order[n], c), :], nacc.at[rows_of(*order[n], 1 - c), :]
        sum_fetch(n, which).wait()

        def step(i):
            a = span(i * 32, 32, 32)
            total = here[a, :] + spare[a, :]
            if n < 3:
                nsd[n, a, :] = total.astype(BF)
            elif which == 0:
                own[a, :] = total
            else:
                here[a, :] = total

        loop(T // 32, step)
        if n < 3:
            sum_chip(n, which).start()

    def sum_close(which, finish):
        here = own if which == 0 else nacc.at[mine, :]
        for n in range(3):
            sum_chip(n, which).wait_recv()
            move(chipbuf.at[which, n], tk, loc.at[7])

            def step(i):
                a = span(i * 32, 32, 32)
                total = here[a, :] + tk[a, :].astype(F32)
                if n < 2:
                    here[a, :] = total
                else:
                    finish(a, total)

            loop(T // 32, step)
        for n in range(3):
            sum_chip(n, which).wait_send()

    class Gather:
        def __init__(self, i, src, buf):
            self.i, self.src, self.buf = i, src, buf

        def rows(self, o_, x_, c_):
            return self.buf.at[span(((o_ * 2 + x_) * 2 + c_) * RP, RP, RP), :]

        def place(self, step):
            return lax.rem(o - step + O, O)

        def send(self, step):
            return remote(
                self.src, self.rows(o, x, c), s_gz.at[self.i, step], r_gz.at[self.i, step],
                at(lax.rem(o + step, O), q, y),
            )

        def over(self, step):
            rows = self.rows(self.place(step), x, c)
            src = self.src if step == 0 else rows
            return remote(src, rows, s_gx.at[self.i, step], r_gx.at[self.i, step], over_x)

        def across(self, step, far_x):
            rows = self.rows(self.place(step), (1 - x) if far_x else x, c)
            src = self.src if step == 0 and not far_x else rows
            return remote(
                src, rows, s_gc.at[self.i, far_x, step], r_gc.at[self.i, far_x, step], core,
            )

        def own(self):
            return local(self.src, self.rows(o, x, c), s_gz.at[self.i, 0])

        def start(self):
            for step in range(1, O):
                self.send(step).start()
            self.over(0).start()
            self.across(0, 0).start()
            self.own().start()

        def pass_on(self):
            for step in range(1, O):
                self.send(step).wait_recv()
                self.over(step).start()
                self.across(step, 0).start()
                self.pass_over(step - 1)

        def pass_over(self, step):
            self.over(step).wait_recv()
            self.across(step, 1).start()

        def wait(self):
            for far_x in range(2):
                for step in range(O):
                    self.across(step, far_x).wait_recv()
            self.own().wait()

        def sent(self):
            for step in range(1, O):
                self.send(step).wait_send()
            for step in range(O):
                self.over(step).wait_send()
                self.across(step, 0).wait_send()
                self.across(step, 1).wait_send()

    def fetch(parts, sem):
        if sz.whole:
            copies = [local(buf.at[:, cols], dst, loc.at[sem + i]) for i, (buf, cols, dst) in enumerate(parts)]
            for copy in copies:
                copy.start()

            def wait():
                for copy in copies:
                    copy.wait()

            return wait
        for buf, cols, dst in parts:
            n = dst.shape[-1]

            def step(b):
                rows = span(b * QUADS * RP, QUADS * RP, QUADS * RP)
                move(buf.at[rows, cols], stage.at[:, pl.ds(0, n)], loc.at[sem])
                part = [stage[i * RP : i * RP + RP, :n].astype(F32)[:R] for i in range(QUADS)]
                dst[span(b * R4, R4, R4), :] = jnp.concatenate(part, axis=0).astype(BF)

            loop(O, step)
        return lambda: None

    def y_copy(src, dst, i):
        return remote(src, dst, s_y.at[i], r_y.at[i], over_y)

    QUERY, KEY, VALUE = pl.ds(0, QW), pl.ds(QW, sz.key), pl.ds(QW + sz.key, sz.key)
    REST = pl.ds(QW, 2 * sz.key)
    TT = 2 * T
    seq = TT // 2

    def head_cols(h):
        return pl.ds(h * HEAD_SIZE, HEAD_SIZE)

    def turn(u, sign, rows):
        return u * rope[0, rows, :] + sign * pltpu.roll(u, HEAD_SIZE // 2, 1) * rope[1, rows, :]

    gather_q = Gather(0, wq_ref, gq)
    gather_o = Gather(1, wo_ref, go)
    head = Chunk(None)

    gather_q.start()
    local(tok_ref, tk, loc.at[1]).start()
    head.a2a_start()
    Chunk(0).a2a_start()
    local(tok_ref, tk, loc.at[1]).wait()

    def norm_first(i):
        a = span(i * 32, 32, 32)
        values = tk[a, :].astype(F32)
        scale = lax.rsqrt(jnp.mean(values * values, axis=-1, keepdims=True) + norm_eps)
        xa[span(y * T + i * 32, 32, 32), :] = (values * scale * vec[0:1, :]).astype(BF)

    loop(T // 32, norm_first)
    own_half, other_half = span(y * T, T, T), span((1 - y) * T, T, T)
    y_copy(xa.at[own_half, :], xa.at[own_half, :], 0).start()
    sv[...] = jnp.zeros_like(sv)
    head.gather_own()
    gather_q.pass_on()
    gather_o.start()
    gather_q.pass_over(O - 1)
    Chunk(0).gather_own()
    head.gather_half()
    gather_q.wait()
    wq_v, wr_v, wo_v = pb.at[0], pb.at[1, :, pl.ds(0, 2 * sz.key)], pb.at[2]
    ready = fetch([(gq, QUERY, wq_v), (gq, REST, wr_v)], 1)
    Chunk(1).a2a_start()
    tok_start(cot_ref, cb, 1)
    local(cot_ref, cb.at[mine, :], loc.at[3]).start()
    y_copy(xa.at[own_half, :], xa.at[other_half, :], 0).wait_recv()
    ready()

    def project(i):
        rows = span(i * seq, seq, seq)
        lin = dot_rows(xa[rows, :], wq_v[...]) + vec[2:3, :QW]
        for h in range(HEADS):
            qkv[rows, head_cols(h)] = turn(lin[:, h * HEAD_SIZE : (h + 1) * HEAD_SIZE], 1.0, rows).astype(BF)
        lin = dot_rows(xa[rows, :], wr_v[...]) + vec[2:3, QW:GW]
        for h in range(sz.key // HEAD_SIZE):
            cut = slice(h * HEAD_SIZE, (h + 1) * HEAD_SIZE)
            qkv[rows, head_cols(HEADS + h)] = turn(lin[:, cut], 1.0, rows).astype(BF)
        qkv[rows, VALUE] = lin[:, sz.key :].astype(BF)

    loop(2, project)
    gather_o.pass_on()
    head.gather_far()
    Chunk(0).gather_half()
    SHARE = QW // sz.key

    def chances(h, part, queries):
        keys = slice(0, (part + 1) * seq)
        kcol = span(QW + (h // SHARE) * HEAD_SIZE, HEAD_SIZE, HEAD_SIZE)
        scores = dot_right(queries, qkv[keys, kcol]) * FACTOR
        row = lax.broadcasted_iota(jnp.int32, scores.shape, 0) + part * seq
        col = lax.broadcasted_iota(jnp.int32, scores.shape, 1)
        scores = jnp.where(row >= col, scores, -1e30)
        exponent = jnp.exp(scores - jnp.max(scores, axis=-1, keepdims=True))
        return exponent / jnp.sum(exponent, axis=-1, keepdims=True)

    def attend(h):
        qcol = span(h * HEAD_SIZE, HEAD_SIZE, HEAD_SIZE)
        vcol = span(QW + sz.key + (h // SHARE) * HEAD_SIZE, HEAD_SIZE, HEAD_SIZE)
        for part in range(2):
            rows = slice(part * seq, (part + 1) * seq)
            probs = chances(h, part, qkv[rows, qcol]).astype(BF)
            mh[rows, qcol] = dot_rows(probs, qkv[0 : (part + 1) * seq, vcol]).astype(BF)

    loop(HEADS, attend)
    gather_o.pass_over(O - 1)
    Chunk(1).gather_own()
    gather_o.wait()
    ready = fetch([(go, pl.ds(0, QW), wo_v)], 1)
    tok_next(cot_ref, cb, 1)
    ready()
    st[...] = dot_right(mh[other_half, :], wo_v[...]).astype(BF)
    y_copy(st, ar.at[0], 1).start()
    mid[...] = dot_right(mh[own_half, :], wo_v[...]) + tk[...].astype(F32)
    Chunk(2).a2a_start()
    Chunk(0).gather_far()
    Chunk(1).gather_half()
    tok_across(cb, 1)
    y_copy(st, ar.at[0], 1).wait_recv()

    def norm_second(i):
        a = span(i * 32, 32, 32)
        values = mid[a, :] + ar[0, a, :].astype(F32)
        mid[a, :] = values
        scale = lax.rsqrt(jnp.mean(values * values, axis=-1, keepdims=True) + norm_eps)
        xb[span(((x * 2 + y) * 2 + c) * T + i * 32, 32, 32), :] = (values * scale * vec[1:2, :]).astype(BF)

    loop(T // 32, norm_second)

    xsrc = xb.at[mine, :]
    tok_start(xsrc, xb, 0)
    local(cot_ref, cb.at[mine, :], loc.at[3]).wait()
    tok(cot_ref, cb, 1, 3).wait_recv()
    for n in range(3):
        tok_pass(cb, 1, n).wait_recv()
    head.gather_wait()
    head.load().start()
    Chunk(2).gather_own()
    head.load().wait()

    def tile(ch, rows, first):
        fk = ch.fk
        both = dot_rows(xb[rows, :], ch.wv[:, : 2 * fk])
        back = dot_rows(cb[rows, :], ch.wv[:, 2 * fk :])
        gate, upper = both[:, :fk], both[:, fk:]
        sigma = jax.nn.sigmoid(gate)
        silu = gate * sigma
        ch.hid[rows, :] = (silu * upper).astype(BF)
        gu[rows, :fk] = (back * upper * (sigma * (1.0 + gate * (1.0 - sigma)))).astype(BF)
        gu[rows, fk : 2 * fk] = (back * silu).astype(BF)
        for j in range(0, W, 512):
            cols = slice(j, j + 512)
            total = dot_right(gu[rows, : 2 * fk], ch.wv[cols, : 2 * fk])
            if first:
                nacc[rows, cols] = total
            else:
                nacc[rows, cols] = nacc[rows, cols] + total

    TD = 512 if W % 512 == 0 else 256

    def products(ch):
        fk = ch.fk

        def step(i):
            cols = span(i * TD, TD, TD)
            ch.pb[cols, : 2 * fk] = dot_left(xb[:, cols], gu[:, : 2 * fk]).astype(BF)
            ch.pb[cols, 2 * fk :] = dot_left(cb[:, cols], ch.hid[...]).astype(BF)

        loop(W // TD, step)

    tok(xsrc, xb, 0, 3).wait_recv()
    tile(head, chip_rows(*order[3]), True)
    tok_next(xsrc, xb, 0)
    tok_pass(xb, 0, 2).wait_recv()
    tile(head, chip_rows(*order[2]), True)
    Chunk(1).gather_far()
    Chunk(2).gather_half()
    tok_pass(xb, 0, 1).wait_recv()
    tile(head, chip_rows(*order[1]), True)
    tok_across(xb, 0)
    for kk in range(3, NF):
        Chunk(kk).a2a_start()
    Chunk(0).gather_wait()
    tok_pass(xb, 0, 0).wait_recv()
    tile(head, chip_rows(*order[0]), True)
    Chunk(0).load().start()
    products(head)
    head.line.first()

    def body(kk):
        ch, nxt = Chunk(kk), Chunk(lax.min(kk + 1, NF - 1))
        two, three = Chunk(lax.max(kk - 2, 0)), Chunk(lax.max(kk - 3, 0))
        last = kk == NF - 1
        later = Chunk(lax.min(kk + 3, NF - 1))
        pl.when(kk + 3 < NF)(later.gather_own)
        ch.load().wait()

        def visit(p):
            for n in range(3):
                pl.when(last & (p == n + 1))(lambda: sum_take(n, 0))
            pl.when((kk == 1) & (p == 1))(head.line.far_take)
            pl.when((kk == 2) & (p == 0))(head.line.cross_take)
            pl.when((kk >= 2) & (kk < NF - 1) & (p == 2))(two.line.far_take)
            pl.when((kk == 3) & (p == 0))(head.line.last_take)
            xx = jnp.where(p < 2, 1 - x, x)
            yy = jnp.where(p % 2 == 0, 1 - y, y)
            tile(ch, chip_rows(xx, yy), False)
            for n in range(4):
                pl.when(last & (p == n))(lambda: sum_pair(n, 0).start())
            for n in range(3):
                pl.when(last & (p == n + 1))(lambda: sum_give(n, 0))

            pl.when((kk == 1) & (p == 1))(head.line.far_give)
            pl.when((kk == 2) & (p == 0))(head.line.cross_give)
            pl.when((kk >= 2) & (kk < NF - 1) & (p == 2))(two.line.far_give)
            pl.when((kk == 3) & (p == 0))(head.finish_give)
            pl.when((kk + 3 < NF) & (p == 2))(later.gather_half)

        loop(4, visit)
        pl.when(last)(lambda: sum_take(3, 0))

        @pl.when(kk < NF - 1)
        def _():
            pl.when(kk == 0)(Chunk(1).gather_wait)
            pl.when(kk > 1)(nxt.gather_far)
            pl.when(kk > 0)(nxt.gather_wait)
            nxt.load().start()

        pl.when(kk >= 3)(three.line.cross_take)
        products(ch)
        ch.line.first()
        pl.when(kk >= 3)(three.line.cross_give)
        pl.when(last)(lambda: sum_give(3, 0))
        pl.when(kk == 0)(Chunk(2).gather_far)

    loop(NF, body)

    y_copy(st, ar.at[0], 1).wait_send()
    local(cot_ref, st, loc.at[1]).start()
    wo_b, wq_b = cb.at[pl.ds(0, W), pl.ds(0, QW)], xb.at[pl.ds(0, W), pl.ds(0, GW)]
    tok_sent(cot_ref, cb, 1)
    tok_sent(xsrc, xb, 0)
    ready = fetch([(go, pl.ds(0, QW), wo_b), (gq, pl.ds(0, GW), wq_b)], 2)
    local(cot_ref, st, loc.at[1]).wait()

    def back_second(a, grad):
        values = mid[a, :]
        scale = lax.rsqrt(jnp.mean(values * values, axis=-1, keepdims=True) + norm_eps)
        scaled = grad * vec[1:2, :]
        mean = jnp.mean(scaled * values, axis=-1, keepdims=True)
        total = st[a, :].astype(F32) + (scale * scaled - values * (scale * scale * scale) * mean)
        own[a, :] = total
        tk[a, :] = total.astype(BF)
        sv[1:2, :] = sv[1:2, :] + jnp.sum(grad * values * scale, axis=0, keepdims=True)

    def m_load(kk):
        return local(
            wagf.at[kk, :, pl.ds(2 * WIDE, WIDE)], wv.at[:, span(lax.rem(kk, 2) * WIDE, WIDE, WIDE)], loc.at[8],
        )

    move(wagh.at[:, pl.ds(2 * HK, HK)], wv.at[:, pl.ds(2 * WIDE, HK)], loc.at[0])
    m_load(0).start()

    def m_first(p):
        rows = span(p * TT, TT, TT)
        nacc[rows, :] = dot_right(hh[rows, :], wv[:, 2 * WIDE : 2 * WIDE + HK])

    loop(4, m_first)

    def m_chunk(kk):
        m_load(kk).wait()
        pl.when(kk + 1 < NF)(lambda: m_load(lax.min(kk + 1, NF - 1)).start())
        cut = span(lax.rem(kk, 2) * WIDE, WIDE, WIDE)

        def m_tile(p):
            rows = span(p * TT, TT, TT)
            for j in range(0, W, 512):
                cols = slice(j, j + 512)
                nacc[rows, cols] = nacc[rows, cols] + dot_right(hf[kk, rows, :], wv[cols, cut])

        loop(4, m_tile)

    loop(NF, m_chunk)
    for n in range(4):
        sum_pair(n, 1).start()
    Chunk(NF - 3).line.far_take()
    sum_close(0, back_second)
    ga[own_half, :] = tk[...]
    y_copy(ga.at[own_half, :], ga.at[own_half, :], 2).start()
    Chunk(NF - 3).line.far_give()
    for n in range(4):
        sum_take(n, 1)
    for n in range(4):
        sum_give(n, 1)
    ready()
    y_copy(ga.at[own_half, :], ga.at[other_half, :], 2).wait_recv()

    PER = 2 * WIDE // HEAD_SIZE

    def cell(h, level):
        return (level * 2 + h // PER) * TT, span(h % PER * HEAD_SIZE, HEAD_SIZE, HEAD_SIZE)

    grad_mixed = dot_rows(ga[...], wo_b[...]).astype(BF)
    for h in range(HEADS):
        row, cut = cell(h, 1)
        gu[pl.ds(row, TT), cut] = grad_mixed[:, h * HEAD_SIZE : (h + 1) * HEAD_SIZE]

    HR = 2 * LR
    tile_rows = R4 * 128 // math.gcd(R4, 128)
    quads = tile_rows // R4

    def spread_rows(i, values, store):
        for b in range(quads):
            for q_ in range(QUADS):
                rows = values[(b * QUADS + q_) * R : (b * QUADS + q_ + 1) * R]
                if not sz.whole:
                    rows = jnp.concatenate([rows, jnp.zeros((RP - R, rows.shape[1]), F32)], axis=0)
                where = ((q_ % 2) * 2 + q_ // 2) * O + i * quads + b
                store(span(where * RP, RP, RP), rows.astype(BF))

    out_cols = pl.ds(QW, QW)

    def out_products(i):
        cols = span(i * tile_rows, tile_rows, 128)
        values = dot_left(ga[:, cols], mh[...])

        def store(rows, part):
            cb[rows, out_cols] = part

        spread_rows(i, values, store)

    loop(W // tile_rows, out_products)

    class Part:
        def __init__(self, i, pieces, temps, cores, overs, col, near, out):
            self.i, self.pieces, self.temps, self.cores, self.overs = i, pieces, temps, cores, overs
            first = (c * 2 + x) * LR
            self.line = Line(
                NF + 1 + i, RP, [p.at[span(first, LR, RP), :] for p in pieces], col, near, out, temps
            )

        def to_core(self, k):
            rows = span((1 - c) * HR, HR, RP)
            return remote(
                self.pieces[k].at[rows, :], self.cores[k], s_pc.at[self.i + k], r_pc.at[self.i + k], core
            )

        def to_x(self, k):
            rows = span((c * 2 + 1 - x) * LR, LR, RP)
            return remote(
                self.pieces[k].at[rows, :], self.overs[k], s_px.at[self.i + k], r_px.at[self.i + k], over_x
            )

        def send_core(self):
            for k in range(len(self.pieces)):
                self.to_core(k).start()

        def take(self, copies, bufs, start, n):
            for k, p in enumerate(self.pieces):
                copies(k).wait_recv()
                local(bufs[k], self.temps[k].at[pl.ds(0, n), :], loc.at[4 + k]).start()
            for k, p in enumerate(self.pieces):
                local(bufs[k], self.temps[k].at[pl.ds(0, n), :], loc.at[4 + k]).wait()
                add_into(p.at[span(start, n, RP), :], self.temps[k], n)

        def send_x(self):
            self.take(self.to_core, self.cores, c * HR, HR)
            for k in range(len(self.pieces)):
                self.to_x(k).start()

        def send_along(self):
            self.take(self.to_x, self.overs, (c * 2 + x) * LR, LR)
            self.line.first()

        def sent(self):
            for k in range(len(self.pieces)):
                self.to_core(k).wait_send()
                self.to_x(k).wait_send()
            self.line.sent()

    NQ = GW // WIDE

    def side_part(side):
        ks = range(side * NQ // 2, (side + 1) * NQ // 2)
        temps = [xb.at[pl.ds((k // 2) * HR, HR), pl.ds(GW + (k % 2) * WIDE, WIDE)] for k in ks]

        def each(ref):
            return [ref.at[k] for k in ks]

        return Part(
            ks[0], each(hf), temps, each(rcq), each(rxq), each(colq), each(nearq), each(outq)
        )

    part_a, part_b = side_part(0), side_part(1)
    part_o = Part(
        NQ, [cb.at[:, out_cols]], [rt.at[:, pl.ds(0, QW)]], [rco], [rxo], [colo], [nearo], [outo]
    )
    part_o.send_core()
    Chunk(NF - 2).line.far_take()

    kv_sums = nacc.at[rows_of(*order[1], c), :]
    kv_sums[:, : 4 * HEAD_SIZE] = jnp.zeros((T, 4 * HEAD_SIZE), F32)

    def attend_back(h):
        qcol = span(h * HEAD_SIZE, HEAD_SIZE, HEAD_SIZE)
        row, cut = cell(h, 1)
        to_row, to_cut = cell(h, 0)
        for part in range(2):
            rows = slice(part * seq, (part + 1) * seq)
            keys = slice(0, (part + 1) * seq)
            queries = qkv[rows, qcol]
            probs = chances(h, part, queries)
            upstream = gu[span(row + part * seq, seq, seq), cut]
            grad_probs = dot_right(upstream, qkv[keys, VALUE])
            inner = jnp.sum(grad_probs * probs, axis=-1, keepdims=True)
            grad_scores = (probs * (grad_probs - inner)).astype(BF)
            grad_queries = dot_rows(grad_scores, qkv[keys, KEY]) * FACTOR
            gu[span(to_row + part * seq, seq, seq), to_cut] = turn(grad_queries, -1.0, rows).astype(BF)
            grad_keys = dot_left(grad_scores, queries) * FACTOR
            grad_values = dot_left(probs.astype(BF), upstream)
            for i in range(part + 1):
                kcut, vcut = head_cols(i), head_cols(2 + i)
                piece = slice(i * seq, (i + 1) * seq)
                kv_sums[:, kcut] = kv_sums[:, kcut] + grad_keys[piece]
                kv_sums[:, vcut] = kv_sums[:, vcut] + grad_values[piece]

    half_cols = 2 * WIDE

    def lin_products(side):
        def step(i):
            cols = span(i * tile_rows, tile_rows, 128)
            values = dot_left(xa[:, cols], gu[side * TT : (side + 1) * TT, :])

            def store(rows, part):
                hf[2 * side, rows, :] = part[:, :WIDE]
                hf[2 * side + 1, rows, :] = part[:, WIDE:]

            spread_rows(i, values, store)

        loop(W // tile_rows, step)

    def lin_back(start):
        return dot_right(
            gu[span(start, T, T), :], wq_b[:, :half_cols]
        ) + dot_right(gu[span(TT + start, T, T), :], wq_b[:, half_cols:])

    def heads_back(first, n):
        loop(n, lambda h: attend_back(first + h))

    heads_back(0, PER)
    Chunk(NF - 2).line.far_give()
    lin_products(0)
    part_a.send_core()
    part_o.send_x()
    heads_back(PER, HEADS - PER)
    for i in range(2):
        rows = slice(i * seq, (i + 1) * seq)
        row, cut = cell(HEADS, 0)
        gu[pl.ds(row + i * seq, seq), cut] = turn(kv_sums[:, head_cols(i)], -1.0, rows).astype(BF)
        row, cut = cell(HEADS + 1, 0)
        gu[pl.ds(row + i * seq, seq), cut] = kv_sums[:, head_cols(2 + i)].astype(BF)
    lin_products(1)
    part_b.send_core()
    part_a.send_x()
    Chunk(NF - 3).line.cross_take()
    st[...] = lin_back((1 - y) * T).astype(BF)
    y_copy(st, ar.at[1], 3).start()
    Chunk(NF - 3).line.cross_give()
    part_b.send_x()
    part_o.send_along()
    Chunk(NF - 4).line.last_take()
    grad_lin = nacc.at[rows_of(*order[0], c), :]
    grad_lin[...] = lin_back(y * T)
    for side in range(2):
        cut = slice(side * half_cols, (side + 1) * half_cols)
        sums = jnp.sum(gu[side * TT : (side + 1) * TT, :].astype(F32), axis=0, keepdims=True)
        sv[2:3, cut] = sums
    Chunk(NF - 4).finish_give()
    part_a.send_along()
    Chunk(NF - 2).line.cross_take()
    tokens_again = ga.at[other_half, :]
    y_copy(ga.at[own_half, :], ga.at[own_half, :], 2).wait_send()
    local(tok_ref, tokens_again, loc.at[1]).start()
    Chunk(NF - 2).line.cross_give()
    part_b.send_along()
    Chunk(NF - 3).finish()
    Chunk(NF - 1).line.far_take()
    Chunk(NF - 1).line.far_give()
    part_o.line.far_take()
    part_o.line.far_give()
    part_a.line.far_take()
    part_a.line.far_give()
    local(tok_ref, tokens_again, loc.at[1]).wait()
    y_copy(st, ar.at[1], 3).wait()

    def back_first(i):
        a = span(i * 32, 32, 32)
        values = tokens_again[a, :].astype(F32)
        grad = grad_lin[a, :] + ar[1, a, :].astype(F32)
        scale = lax.rsqrt(jnp.mean(values * values, axis=-1, keepdims=True) + norm_eps)
        scaled = grad * vec[0:1, :]
        mean = jnp.mean(scaled * values, axis=-1, keepdims=True)
        own[a, :] = own[a, :] + (scale * scaled - values * (scale * scale * scale) * mean)
        sv[0:1, :] = sv[0:1, :] + jnp.sum(grad * values * scale, axis=0, keepdims=True)

    loop(T // 32, back_first)
    local(own, gtok_ref, loc.at[1]).start()

    def small(dq, dy):
        to_q, to_y = lax.rem(q + dq, QUADS), lax.rem(y + dy, 2)
        return remote(
            sv, svr.at[q * 2 + y], s_v.at[dq * 2 + dy], r_v.at[q * 2 + y], at(o, to_q, to_y)
        )

    def small_from(dq, dy):
        from_q, from_y = lax.rem(q + dq, QUADS), lax.rem(y + dy, 2)
        return remote(
            sv, svr.at[from_q * 2 + from_y], s_v.at[dq * 2 + dy],
            r_v.at[from_q * 2 + from_y], at(o, from_q, from_y),
        )

    def small_along(step):
        return remote(sv, svz.at[o], s_vz.at[step], r_vz.at[o], at(lax.rem(o + step, O), q, y))

    def small_along_from(step):
        place = lax.rem(o + step, O)
        return remote(sv, svz.at[place], s_vz.at[step], r_vz.at[place], at(place, q, y))

    peers = [(dq, dy) for dq in range(QUADS) for dy in range(2) if dq or dy]
    for dq, dy in peers:
        small(dq, dy).start()
    svr[q * 2 + y] = sv[...]

    part_b.line.far_take()
    part_b.line.far_give()
    Chunk(NF - 2).finish()

    def layer_out(a, total):
        tk[a, :] = (mid[a, :] + total).astype(BF)

    sum_close(1, layer_out)
    local(tk, mixed_ref, loc.at[2]).start()
    for dq, dy in peers:
        small_from(dq, dy).wait_recv()
        small(dq, dy).wait_send()
    gains = svr[0]
    for i in range(1, 2 * QUADS):
        gains = gains + svr[i]
    biases = svr[y]
    for i in range(1, QUADS):
        biases = biases + svr[i * 2 + y]
    sv[...] = gains
    sv[2:3, :] = biases[2:3, :]
    for step in range(1, O):
        small_along(step).start()
    svz[o] = sv[...]
    Chunk(NF - 1).line.cross_take()
    Chunk(NF - 1).line.cross_give()
    for part in (part_o, part_a, part_b):
        part.line.cross_take()
        part.line.cross_give()
    head.collect()
    loop(NF - 1, lambda kk: Chunk(kk).collect())
    Chunk(NF - 1).finish()
    for step in range(1, O):
        small_along_from(step).wait_recv()
        small_along(step).wait_send()
    total = svz[0]
    for i in range(1, O):
        total = total + svz[i]
    sv[...] = total
    local(sv, sums_ref, loc.at[8]).start()
    low = span(3 * PIECES * RP, RP, RP)
    lower = span((3 * PIECES + 1) * RP, RP, RP)
    for part in (part_o, part_a, part_b):
        part.line.last_take()
        part.line.last_give()
    nacc[low, :QW] = part_o.line.block(0, o)[...].astype(F32)
    for side, part in enumerate((part_a, part_b)):
        for k in range(NQ // 2):
            cut = slice((side * NQ // 2 + k) * WIDE, (side * NQ // 2 + k + 1) * WIDE)
            nacc[lower, cut] = part.line.block(k, o)[...].astype(F32)
    outputs = [
        local(nacc.at[low, pl.ds(0, QW)], gao_ref, loc.at[3]),
        local(nacc.at[lower, QUERY], gwq_ref, loc.at[4]),
        local(nacc.at[lower, KEY], gwk_ref, loc.at[5]),
        local(nacc.at[lower, VALUE], gwv_ref, loc.at[6]),
    ]
    for copy in outputs:
        copy.start()
    Chunk(NF - 1).collect()
    for m in range(3):
        for j in range(PIECES):
            n = min(W, sz.hidden - j * W)
            here = nacc.at[pl.ds((m * PIECES + j) * RP, RP), pl.ds(0, n)]
            outputs.append(local(here, gw_refs[m].at[:, pl.ds(j * W, n)], loc.at[20 + m * PIECES + j]))
            outputs[-1].start()

    for copy in outputs:
        copy.wait()
    gather_q.sent()
    gather_o.sent()
    y_copy(xa.at[own_half, :], xa.at[own_half, :], 0).wait_send()
    part_o.sent()
    part_a.sent()
    part_b.sent()
    head.finished()
    loop(NF, lambda kk: Chunk(kk).finished())
    local(own, gtok_ref, loc.at[1]).wait()
    local(tk, mixed_ref, loc.at[2]).wait()
    local(sv, sums_ref, loc.at[8]).wait()


def layer(sz, tokens, cotangent, wq, wo, wh, wg, wu, wd, vec, rope):
    O, NF, T = sz.outer, sz.full, sz.tokens
    H = O // 2
    HK, W, RP = sz.head, sz.wide, sz.pad
    R4, LR = QUADS * sz.rows, O * sz.pad
    HR = 2 * LR
    QW, GW = sz.query, sz.query + 2 * sz.key
    NQ = GW // WIDE
    PT = 2 * QUADS * T
    NL = NF + 1 + NQ + 1
    A, B = 3 * HK, 3 * WIDE
    PIECES = -(-sz.hidden // W)
    out = jax.ShapeDtypeStruct
    outs = [
        out((RP, sz.hidden), F32),
        out((RP, sz.hidden), F32),
        out((RP, sz.hidden), F32),
        out((RP, QW), F32),
        out((RP, sz.key), F32),
        out((RP, sz.key), F32),
        out((RP, QW), F32),
        out((T, W), BF),
        out((T, W), F32),
        out((8, W), F32),
        out((QUADS, RP, A), BF),
        out((NF, QUADS, RP, B), BF),
        out((W, A), BF),
        out((NF, W, B), BF),
        out((H, H * R4, A), BF),
        out((NF, H, H * R4, B), BF),
        out((H, R4, A), BF),
        out((NF, H, R4, B), BF),
        out((H * R4, A), BF),
        out((NF, H * R4, B), BF),
        out((2, 4, T, W), F32),
        out((2, 3, T, W), BF),
        out((sz.dp * RP, GW), BF),
        out((sz.dp * RP, QW), BF),
        out((NQ, HR, WIDE), BF),
        out((HR, QW), BF),
        out((NQ, LR, WIDE), BF),
        out((LR, QW), BF),
        out((NQ, H, H * RP, WIDE), BF),
        out((H, H * RP, QW), BF),
        out((NQ, H, RP, WIDE), BF),
        out((H, RP, QW), BF),
        out((NQ, H * RP, WIDE), BF),
        out((H * RP, QW), BF),
    ]
    if not sz.whole:
        outs += [out((QUADS, RP, A), BF), out((NF, QUADS, RP, B), BF)]
    dma = pltpu.SemaphoreType.DMA
    vm = pltpu.VMEM
    scratch = [
        vm((PT, W), BF),
        vm((PT, W), BF),
        vm((PT, W), F32),
        vm((W, B), BF),
        vm((W, A), BF),
        vm((NF, W, B), BF),
        vm((PT, HK), BF),
        vm((NF, PT, WIDE), BF),
        vm((PT, 2 * WIDE), BF),
        vm((3, T, W), BF),
        vm((T, W), BF),
        vm((max(W // 2, HR), B), BF),
        vm((T, W), F32),
        vm((2 * T, W), BF),
        vm((2 * T, GW), BF),
        vm((2 * T, QW), BF),
        vm((2, T, W), BF),
        vm((T, W), BF),
        vm((T, W), F32),
        vm((2 * T, W), BF),
        vm((8, W), F32),
        vm((2 * QUADS, 8, W), F32),
        vm((O, 8, W), F32),
        dma((NF + 1, 3, 4)),
        dma((NF + 1, 3, 3)),
        dma((NF + 1, H)),
        dma((NF + 1, H)),
        dma((NF + 1,)),
        dma((NF + 1,)),
        dma((NF + 1, H)),
        dma((NF + 1,)),
        dma((NL,)),
        dma((NL, H)),
        dma((NL, H)),
        dma((NL, H)),
        dma((NL,)),
        dma((NL,)),
        dma((NF + 1, 4)),
        dma((NF + 1, 3)),
        dma((2, 9)),
        dma((2, 9)),
        dma((2, 7)),
        dma((2, 7)),
        dma((4,)),
        dma((4,)),
        dma((2, O)),
        dma((2, O)),
        dma((2, O)),
        dma((2, O)),
        dma((2, 2, O)),
        dma((2, 2, O)),
        dma((NQ + 1,)),
        dma((NQ + 1,)),
        dma((NQ + 1,)),
        dma((NQ + 1,)),
        dma((2 * QUADS,)),
        dma((2 * QUADS,)),
        dma((O,)),
        dma((O,)),
        dma((20 + 3 * PIECES,)),
    ]
    if not sz.whole:
        scratch += [vm((QUADS * RP, max(B, GW)), BF), vm((R4, B), BF)]
    any_spec = pl.BlockSpec(memory_space=pl.ANY)
    vmem_spec = pl.BlockSpec(memory_space=pltpu.VMEM)
    results = pl.pallas_call(
        lambda *refs: layer_kernel(sz, *refs),
        out_shape=outs,
        in_specs=[any_spec] * 8 + [vmem_spec] * 2,
        out_specs=[any_spec] * len(outs),
        scratch_shapes=scratch,
        compiler_params=pltpu.CompilerParams(
            collective_id=0, has_side_effects=True, vmem_limit_bytes=64 << 20
        ),
        name="layer",
    )(tokens, cotangent, wq, wo, wh, wg, wu, wd, vec, rope)
    return results[:10]


def per_device(
    sz,
    tokens,
    w_query,
    key_weight,
    value_weight,
    b_query,
    key_bias,
    value_bias,
    w_out,
    gain_attn,
    gain_mlp,
    w_gate,
    w_up,
    w_down,
    cotangent,
):
    rows = sz.rows
    more = sz.pad - sz.rows

    def fill(values):
        return jnp.pad(values, ((0, more), (0, 0))) if more else values

    wg, wu, wd = fill(w_gate), fill(w_up), fill(w_down.T)
    start = sz.hidden - sz.rest
    wh = jnp.stack([wg[:, start:], wu[:, start:], wd[:, start:]], axis=1)
    wh = jnp.pad(wh, ((0, 0), (0, 0), (0, QUADS * sz.head - sz.rest)))
    wh = wh.reshape(sz.pad, 3, QUADS, sz.head).transpose(2, 0, 1, 3)
    wh = wh.reshape(QUADS, sz.pad, 3 * sz.head)
    wq = jnp.concatenate([w_query, key_weight, value_weight], axis=1)
    wq, wo = fill(wq), fill(w_out.T)
    bias = jnp.concatenate([b_query, key_bias, value_bias]).astype(F32)
    bias = jnp.pad(bias, (0, sz.wide - bias.shape[0]))
    vec = jnp.stack([gain_attn.astype(F32), gain_mlp.astype(F32), bias])
    vec = jnp.pad(vec, ((0, 5), (0, 0)))
    rope = jnp.asarray(rope_tables(SEQUENCE_TOKENS, HEAD_SIZE))

    grad_gate, grad_up, grad_down, grad_q, grad_k, grad_v, grad_o, mixed, grad_tokens, sums = layer(
        sz, tokens, cotangent, wq, wo, wh, wg, wu, wd, vec, rope
    )
    cuts = (sz.query, sz.query + sz.key, sz.query + 2 * sz.key)
    return (
        mixed,
        grad_tokens,
        grad_q[:rows],
        grad_k[:rows],
        grad_v[:rows],
        sums[2, : cuts[0]],
        sums[2, cuts[0] : cuts[1]],
        sums[2, cuts[1] : cuts[2]],
        grad_o[:rows].T,
        sums[0],
        sums[1],
        grad_gate[:rows],
        grad_up[:rows],
        grad_down[:rows].T,
    )


def solution(mesh):
    dp = mesh.shape["dp"]

    def whole(*args):
        def shard(*blocks):
            tokens, w_query, key_weight, w_gate = blocks[0], blocks[1], blocks[2], blocks[10]
            sz = Sizes(dp, w_gate.shape, tokens.shape[0], w_query.shape[1], key_weight.shape[1])
            return per_device(sz, *blocks)

        return jax.shard_map(
            shard, mesh=mesh, in_specs=in_specs, out_specs=out_specs, check_vma=False
        )(*args)

    in_specs = (
        P(("dp", "tensor"), None),
        P("dp", "tensor"),
        P("dp", "tensor"),
        P("dp", "tensor"),
        P("tensor"),
        P("tensor"),
        P("tensor"),
        P("tensor", "dp"),
        P(),
        P(),
        P("dp", "tensor"),
        P("dp", "tensor"),
        P("tensor", "dp"),
        P(("dp", "tensor"), None),
    )
    out_specs = (
        P(("dp", "tensor"), None),
        P(("dp", "tensor"), None),
        P("dp", "tensor"),
        P("dp", "tensor"),
        P("dp", "tensor"),
        P("tensor"),
        P("tensor"),
        P("tensor"),
        P("tensor", "dp"),
        P(),
        P(),
        P("dp", "tensor"),
        P("dp", "tensor"),
        P("tensor", "dp"),
    )
    return whole
```

```python
import math

import jax
import jax.numpy as jnp
import numpy as np
from jax import lax
from jax.experimental import pallas as pl
from jax.experimental.pallas import tpu as pltpu
from jax.sharding import PartitionSpec as P

QUERY_HEADS = 12
KEY_VALUE_HEADS = 2
HEAD_SIZE = 128
SEQUENCE_TOKENS = 512

QUADS = 4
WIDE = 256

norm_eps = 1e-06
rope_base = 1000000.0
BF = jnp.bfloat16
F32 = jnp.float32
MESH = pl.DeviceIdType.MESH


def rope_tables(length, columns):
    midway = columns // 2
    inverse = np.exp(
        np.arange(midway, dtype=np.float32) * np.float32(-2.0 * math.log(rope_base) / columns)
    )
    angles = np.arange(length, dtype=np.float32)[:, None] * inverse[None, :].astype(np.float32)
    cosine, sine = np.cos(angles.astype(np.float64)), np.sin(angles.astype(np.float64))
    tables = np.stack([np.concatenate([cosine, cosine], -1), np.concatenate([-sine, sine], -1)])
    return tables.astype(np.float32)


def dot_rows(left, right):
    return jnp.dot(left, right, preferred_element_type=F32)


def dot_left(left, right):
    return lax.dot_general(left, right, (((0,), (0,)), ((), ())), preferred_element_type=F32)


def dot_right(left, right):
    return lax.dot_general(left, right, (((1,), (1,)), ((), ())), preferred_element_type=F32)


def round_up(value, step):
    return (value + step - 1) // step * step


class Sizes:
    def __init__(self, dp, gate_shape, tokens, query, key):
        self.dp = dp
        self.outer = dp // QUADS
        self.rows, self.hidden = gate_shape
        self.pad = round_up(self.rows, 16)
        self.whole = self.pad == self.rows
        self.wide = dp * self.rows
        self.full = (self.hidden - 1) // (QUADS * WIDE)
        self.rest = self.hidden - self.full * QUADS * WIDE
        self.head = round_up(-(-self.rest // QUADS), 128)
        self.tokens, self.query, self.key = tokens, query, key


def layer_kernel(sz, *refs):
    refs = iter(refs)

    def some(n):
        return [next(refs) for _ in range(n)]

    tok_ref, cot_ref, wq_ref, wo_ref, wh_ref, wg_ref, wu_ref, wd_ref, vec, rope = some(10)
    gw_refs = some(3)
    gwq_ref, gwk_ref, gwv_ref, gao_ref, mixed_ref, gtok_ref, sums_ref, gh_ref, gf_ref = some(9)
    wagh, wagf, colh, colf, nearh, nearf, outh, outf = some(8)
    pairbuf, chipbuf, gq, go = some(4)
    rcq, rco, rxq, rxo, colq, colo, nearq, nearo, outq, outo = some(10)
    abh, abf = (None, None) if sz.whole else some(2)
    xb, cb, nacc, wv, pbh, pb, hh, hf, gu, nsd, tk, rt, own = some(13)
    xa, qkv, mh, ar, st, mid, ga, sv, svr, svz = some(10)
    s_a2a, r_a2a, s_own, r_own, s_far, r_far, s_fwd, r_fwd = some(8)
    s_col, r_col, s_nr, r_nr, s_out, r_out, s_fin, r_fin = some(8)
    s_tok, r_tok, s_sum, r_sum, s_y, r_y, s_gz, r_gz, s_gx, r_gx, s_gc, r_gc = some(12)
    s_pc, r_pc, s_px, r_px, s_v, r_v, s_vz, r_vz, loc = some(9)
    stage, joined = (None, None) if sz.whole else some(2)

    O, NF, T = sz.outer, sz.full, sz.tokens
    H = O // 2
    HK, W, R, RP = sz.head, sz.wide, sz.rows, sz.pad
    R4, LR = QUADS * R, O * RP
    QW = sz.query
    GW = sz.query + 2 * sz.key
    HEADS = QW // HEAD_SIZE
    PIECES = -(-sz.hidden // W)
    FACTOR = 1.0 / math.sqrt(HEAD_SIZE)
    me = lax.axis_index("dp")
    y = lax.axis_index("tensor")
    o, q = me // QUADS, me % QUADS
    x, c = q // 2, q % 2
    half, pos = o // H, o % H
    base, far = half * H, (1 - half) * H
    middle_pos = (1 - half) * (H - 1)
    is_middle = pos == middle_pos

    def at(o_, q_, y_):
        return (o_ * QUADS + q_, y_)

    mid_dev = at(base + middle_pos, q, y)
    far_mid = at(far + half * (H - 1), q, y)
    core = at(o, x * 2 + 1 - c, y)
    over_x = at(o, (1 - x) * 2 + c, y)
    over_y = at(o, q, 1 - y)
    chips = [(1 - x, 1 - y), (1 - x, y), (x, 1 - y)]
    order = chips + [(x, y)]

    def remote(src, dst, ssem, rsem, dev):
        return pltpu.make_async_remote_copy(
            src_ref=src, dst_ref=dst, send_sem=ssem, recv_sem=rsem,
            device_id=dev, device_id_type=MESH,
        )

    def local(src, dst, sem):
        return pltpu.make_async_copy(src, dst, sem)

    def move(src, dst, sem):
        local(src, dst, sem).start()
        local(src, dst, sem).wait()

    def span(start, size, unit):
        return pl.ds(pl.multiple_of(start, unit), size)

    def loop(n, step):
        def run(i, carry):
            step(i)
            return carry

        lax.fori_loop(0, n, run, 0)

    bar = pltpu.get_barrier_semaphore()

    def greet(dev):
        pl.semaphore_signal(bar, inc=1, device_id=dev, device_id_type=MESH)

    for dq in range(QUADS):
        for yy in range(2):
            if dq or yy:
                greet(at(o, lax.rem(q + dq, QUADS), (y + yy) % 2))
    for step in range(1, O):
        greet(at(lax.rem(o + step, O), q, y))
    pl.semaphore_wait(bar, 2 * QUADS - 1 + O - 1)

    def add_into(dst, src, n):
        rows = 32

        def step(i):
            here = span(i * rows, rows, rows)
            dst[here, :] = (dst[here, :].astype(F32) + src[here, :].astype(F32)).astype(BF)

        loop(n // rows, step)

    class Line:
        def __init__(self, i, rows, pieces, col, near, out, temps):
            self.i, self.rows, self.pieces = i, rows, pieces
            self.col, self.near_, self.out, self.temps = col, near, out, temps

        def block(self, k, b, n=1):
            return self.pieces[k].at[span(b * self.rows, n * self.rows, self.rows), :]

        def temp(self, k, start, n):
            return self.temps[k].at[pl.ds(start * self.rows, n * self.rows), :]

        def to_middle(self, k, t):
            return remote(
                self.block(k, far, H), self.col[k].at[t],
                s_col.at[self.i + k], r_col.at[self.i + k, t], mid_dev,
            )

        def near(self, k, to, t):
            return remote(
                self.block(k, base + to), self.near_[k].at[t],
                s_nr.at[self.i + k, to], r_nr.at[self.i + k, t], at(base + to, q, y),
            )

        def cross(self, k):
            return remote(
                self.block(k, far, H), self.out[k], s_out.at[self.i + k], r_out.at[self.i + k], far_mid
            )

        def first(self):
            @pl.when(jnp.logical_not(is_middle))
            def _():
                for k in range(len(self.pieces)):
                    self.to_middle(k, pos).start()
                for k in range(len(self.pieces)):
                    for t in range(H):
                        pl.when(pos != t)(lambda: self.near(k, t, pos).start())

        def far_copy(self, k, t):
            return local(self.col[k].at[t], self.temp(k, 0, H), loc.at[4 + k])

        def far_add(self, t):
            for k in range(len(self.pieces)):
                self.far_copy(k, t).wait()
                add_into(self.block(k, far, H), self.temp(k, 0, H), H * self.rows)

        def far_take(self):
            @pl.when(is_middle)
            def _():
                for i in range(H - 1):
                    t = jnp.where(half == 0, i, i + 1)
                    for k in range(len(self.pieces)):
                        self.to_middle(k, t).wait_recv()
                        self.far_copy(k, t).start()
                    if i < H - 2:
                        self.far_add(t)

        def far_give(self):
            @pl.when(is_middle)
            def _():
                self.far_add(jnp.where(half == 0, H - 2, H - 1))
                for k in range(len(self.pieces)):
                    self.cross(k).start()

        def out_copy(self, k):
            return local(self.out[k], self.temp(k, 0, H), loc.at[4 + k])

        def cross_take(self):
            @pl.when(is_middle)
            def _():
                for k in range(len(self.pieces)):
                    self.cross(k).wait_recv()
                    self.out_copy(k).start()

        def cross_give(self):
            @pl.when(is_middle)
            def _():
                for k in range(len(self.pieces)):
                    self.out_copy(k).wait()
                    add_into(self.block(k, base, H), self.temp(k, 0, H), H * self.rows)
                    for t in range(H):
                        pl.when(pos != t)(lambda: self.near(k, t, pos).start())

        def near_copy(self, k, t):
            return local(self.near_[k].at[t], self.temp(k, 0, 1), loc.at[4 + k])

        def near_add(self, t):
            for k in range(len(self.pieces)):
                self.near_copy(k, t).wait()
                add_into(self.block(k, o), self.temp(k, 0, 1), self.rows)

        def last_take(self):
            for i in range(H - 1):
                t = jnp.where(pos <= i, i + 1, i)
                for k in range(len(self.pieces)):
                    self.near(k, pos, t).wait_recv()
                    self.near_copy(k, t).start()
                if i < H - 2:
                    self.near_add(t)

        def last_give(self):
            self.near_add(jnp.where(pos <= H - 2, H - 1, H - 2))

        def sent(self):
            for k in range(len(self.pieces)):
                pl.when(jnp.logical_not(is_middle))(lambda: self.to_middle(k, pos).wait_send())
                pl.when(is_middle)(lambda: self.cross(k).wait_send())
                for t in range(H):
                    pl.when(pos != t)(lambda: self.near(k, t, pos).wait_send())

    class Chunk:
        def __init__(self, kk):
            self.head = kk is None
            if self.head:
                self.i, self.fk = 0, HK
                self.wag, self.pb, self.out = wagh, pbh, gh_ref
                self.moves = [(wh_ref.at, pl.ds(0, 3 * HK))]
                self.hid, self.ab = hh, abh
                col, near, out = colh, nearh, outh
            else:
                self.i, self.fk = kk + 1, WIDE
                self.kk, self.wag, self.pb, self.out = kk, wagf.at[kk], pb.at[kk], gf_ref.at[kk]
                self.moves = [
                    (ref, pl.ds(m * WIDE, WIDE)) for m, ref in enumerate((wg_ref, wu_ref, wd_ref))
                ]
                self.hid, self.ab = hf.at[kk], None if abf is None else abf.at[kk]
                col, near, out = colf.at[kk], nearf.at[kk], outf.at[kk]
            self.cols = pl.ds(0, 3 * self.fk)
            self.wv = wv.at[:, self.cols]
            self.line = Line(self.i, R4, [self.pb], [col], [near], [out], [rt.at[:, self.cols]])

        def block(self, ref, b, n=1):
            return ref.at[span(b * R4, n * R4, R4), :]

        def part(self, ref, b, q_):
            return ref.at[span((b * QUADS + q_) * R, R, R), :]

        def mine(self):
            return self.part(self.wag, o, q) if sz.whole else self.ab.at[q]

        def source(self, m, to):
            ref = self.moves[m][0]
            return wh_ref.at[to] if self.head else ref.at[:, span((self.kk * QUADS + to) * WIDE, WIDE, WIDE)]

        def a2a(self, m, dq):
            to = lax.rem(q + dq, QUADS)
            return remote(
                self.source(m, to), self.mine().at[:, self.moves[m][1]],
                s_a2a.at[self.i, m, dq - 1], r_a2a.at[self.i, m, dq - 1], at(o, to, y),
            )

        def a2a_own(self, m):
            return local(self.source(m, q), self.mine().at[:, self.moves[m][1]], s_a2a.at[self.i, m, 3])

        def a2a_start(self):
            for m in range(len(self.moves)):
                self.a2a_own(m).start()
                for dq in (1, 2, 3):
                    self.a2a(m, dq).start()

        def join(self):
            for i in range(QUADS):
                move(self.ab.at[i], stage.at[pl.ds(i * RP, RP), self.cols], loc.at[3])
            rows = [stage[i * RP : i * RP + RP, self.cols].astype(F32)[:R] for i in range(QUADS)]
            joined[:, self.cols] = jnp.concatenate(rows, axis=0).astype(BF)
            move(joined.at[:, self.cols], self.block(self.wag, o), loc.at[3])

        def own_to(self, to, t):
            return remote(
                self.block(self.wag, base + t), self.block(self.wag, base + t),
                s_own.at[self.i, to], r_own.at[self.i, t], at(base + to, q, y),
            )

        def half_far(self, half_):
            rows = self.block(self.wag, half_ * H, H)
            return remote(rows, rows, s_far.at[self.i], r_far.at[self.i], far_mid)

        def forward(self, half_, to):
            rows = self.block(self.wag, half_ * H, H)
            return remote(
                rows, rows, s_fwd.at[self.i, to], r_fwd.at[self.i], at(base + to, q, y),
            )

        def gather_own(self):
            for m in range(len(self.moves)):
                self.a2a_own(m).wait()
                for dq in (1, 2, 3):
                    self.a2a(m, dq).wait_recv()
            if not sz.whole:
                self.join()
            for t in range(H):
                pl.when(pos != t)(lambda: self.own_to(t, pos).start())

        def gather_half(self):
            @pl.when(is_middle)
            def _():
                for t in range(H):
                    pl.when(pos != t)(lambda: self.own_to(pos, t).wait_recv())
                self.half_far(half).start()

        def gather_far(self):
            @pl.when(is_middle)
            def _():
                self.half_far(1 - half).wait_recv()
                for t in range(H):
                    pl.when(pos != t)(lambda: self.forward(1 - half, t).start())

        def gather_wait(self):
            @pl.when(jnp.logical_not(is_middle))
            def _():
                for t in range(H):
                    pl.when(pos != t)(lambda: self.own_to(pos, t).wait_recv())
                self.forward(1 - half, pos).wait_recv()

        def gather_sent(self):
            for m in range(len(self.moves)):
                for dq in (1, 2, 3):
                    self.a2a(m, dq).wait_send()
            pl.when(is_middle)(lambda: self.half_far(half).wait_send())
            for t in range(H):

                @pl.when(pos != t)
                def _():
                    self.own_to(t, pos).wait_send()
                    pl.when(is_middle)(lambda: self.forward(1 - half, t).wait_send())

        def load(self):
            return local(self.wag, self.wv, loc.at[0])

        def result(self, q_):
            return self.part(self.pb, o, q_) if sz.whole else self.ab.at[q_]

        def give(self, dq):
            to = lax.rem(q + dq, QUADS)
            return remote(
                self.result(to), self.out.at[q],
                s_fin.at[self.i, dq - 1], r_fin.at[self.i, dq - 1], at(o, to, y),
            )

        def give_own(self):
            return local(self.result(q), self.out.at[q], s_fin.at[self.i, 3])

        def split(self):
            rows = self.block(self.pb, o)[...].astype(F32)
            for i in range(QUADS):
                part = rows[i * R : (i + 1) * R]
                part = jnp.concatenate([part, jnp.zeros((RP - R, 3 * self.fk), F32)], axis=0)
                stage[i * RP : i * RP + RP, self.cols] = part.astype(BF)
            for i in range(QUADS):
                move(stage.at[pl.ds(i * RP, RP), self.cols], self.ab.at[i], loc.at[3])

        def finish(self):
            self.line.last_take()
            self.finish_give()

        def finish_give(self):
            self.line.last_give()
            if not sz.whole:
                self.split()
            self.give_own().start()
            for dq in (1, 2, 3):
                self.give(dq).start()

        def collect(self):
            self.give_own().wait()
            for dq in (1, 2, 3):
                self.give(dq).wait_recv()

            def rows(i):
                return wv.at[span(i * RP, RP, RP), self.cols]

            for i in range(QUADS):
                local(self.out.at[i], rows(i), loc.at[16 + i]).start()
            for i in range(QUADS):
                local(self.out.at[i], rows(i), loc.at[16 + i]).wait()
                if self.head:
                    first, n = NF * QUADS * WIDE + i * HK, min(HK, sz.rest - i * HK)
                else:
                    first, n = (self.kk * QUADS + i) * WIDE, WIDE
                if n > 0:
                    for m in range(3):
                        to = span((m * PIECES + first // W) * RP, RP, RP)
                        nacc[to, span(first % W, n, 128)] = rows(i)[:, m * self.fk : m * self.fk + n].astype(F32)

        def finished(self):
            for dq in (1, 2, 3):
                self.give(dq).wait_send()
            self.gather_sent()
            self.line.sent()

    def chip_rows(xx, yy):
        return span((xx * 2 + yy) * (2 * T), 2 * T, 2 * T)

    def rows_of(xx, yy, cc):
        return span(((xx * 2 + yy) * 2 + cc) * T, T, T)

    mine = rows_of(x, y, c)

    def tok(src, buf, which, n):
        dev = core if n == 3 else (over_x, over_y)[n - 1]
        return remote(src, buf.at[mine, :], s_tok.at[which, n], r_tok.at[which, n], dev)

    def tok_half(buf, which, n):
        start = rows_of(*chips[n], c).start
        rows = span(start + (n - 1) * (T // 2), T // 2, T // 2)
        return remote(
            buf.at[rows, :], buf.at[rows, :],
            s_tok.at[which, 6 + n], r_tok.at[which, 6 + n], (over_y, over_x)[n - 1],
        )

    def tok_pass(buf, which, n):
        rows = rows_of(*chips[n], c)
        return remote(
            buf.at[rows, :], buf.at[rows, :],
            s_tok.at[which, 4 + n], r_tok.at[which, 4 + n], core,
        )

    def tok_start(src, buf, which):
        for n in (3, 2, 1):
            tok(src, buf, which, n).start()

    def tok_next(src, buf, which):
        for n in (2, 1):
            tok(src, buf, which, n).wait_recv()
            tok_half(buf, which, n).start()
            tok_pass(buf, which, n).start()

    def tok_across(buf, which):
        for n in (2, 1):
            tok_half(buf, which, n).wait_recv()
        tok_pass(buf, which, 0).start()

    def tok_sent(src, buf, which):
        for n in (1, 2, 3):
            tok(src, buf, which, n).wait_send()
        for n in (1, 2):
            tok_half(buf, which, n).wait_send()
        for n in range(3):
            tok_pass(buf, which, n).wait_send()

    def sum_pair(n, which):
        return remote(
            nacc.at[rows_of(*order[n], 1 - c), :], pairbuf.at[which, n],
            s_sum.at[which, n], r_sum.at[which, n], core,
        )

    def sum_chip(n, which):
        xx, yy = chips[n]
        return remote(
            nsd.at[n], chipbuf.at[which, n],
            s_sum.at[which, 4 + n], r_sum.at[which, 4 + n], at(o, xx * 2 + c, yy),
        )

    def sum_fetch(n, which):
        return local(pairbuf.at[which, n], nacc.at[rows_of(*order[n], 1 - c), :], loc.at[12 + n])

    def sum_take(n, which):
        sum_pair(n, which).wait()
        sum_fetch(n, which).start()

    def sum_give(n, which):
        here, spare = nacc.at[rows_of(*order[n], c), :], nacc.at[rows_of(*order[n], 1 - c), :]
        sum_fetch(n, which).wait()

        def step(i):
            a = span(i * 32, 32, 32)
            total = here[a, :] + spare[a, :]
            if n < 3:
                nsd[n, a, :] = total.astype(BF)
            elif which == 0:
                own[a, :] = total
            else:
                here[a, :] = total

        loop(T // 32, step)
        if n < 3:
            sum_chip(n, which).start()

    def sum_close(which, finish):
        here = own if which == 0 else nacc.at[mine, :]
        for n in range(3):
            sum_chip(n, which).wait_recv()
            move(chipbuf.at[which, n], tk, loc.at[7])

            def step(i):
                a = span(i * 32, 32, 32)
                total = here[a, :] + tk[a, :].astype(F32)
                if n < 2:
                    here[a, :] = total
                else:
                    finish(a, total)

            loop(T // 32, step)
        for n in range(3):
            sum_chip(n, which).wait_send()

    class Gather:
        def __init__(self, i, src, buf):
            self.i, self.src, self.buf = i, src, buf

        def rows(self, o_, x_, c_):
            return self.buf.at[span(((o_ * 2 + x_) * 2 + c_) * RP, RP, RP), :]

        def place(self, step):
            return lax.rem(o - step + O, O)

        def send(self, step):
            return remote(
                self.src, self.rows(o, x, c), s_gz.at[self.i, step], r_gz.at[self.i, step],
                at(lax.rem(o + step, O), q, y),
            )

        def over(self, step):
            rows = self.rows(self.place(step), x, c)
            src = self.src if step == 0 else rows
            return remote(src, rows, s_gx.at[self.i, step], r_gx.at[self.i, step], over_x)

        def across(self, step, far_x):
            rows = self.rows(self.place(step), (1 - x) if far_x else x, c)
            src = self.src if step == 0 and not far_x else rows
            return remote(
                src, rows, s_gc.at[self.i, far_x, step], r_gc.at[self.i, far_x, step], core,
            )

        def own(self):
            return local(self.src, self.rows(o, x, c), s_gz.at[self.i, 0])

        def start(self):
            for step in range(1, O):
                self.send(step).start()
            self.over(0).start()
            self.across(0, 0).start()
            self.own().start()

        def pass_on(self):
            for step in range(1, O):
                self.send(step).wait_recv()
                self.over(step).start()
                self.across(step, 0).start()
                self.pass_over(step - 1)

        def pass_over(self, step):
            self.over(step).wait_recv()
            self.across(step, 1).start()

        def wait(self):
            for far_x in range(2):
                for step in range(O):
                    self.across(step, far_x).wait_recv()
            self.own().wait()

        def sent(self):
            for step in range(1, O):
                self.send(step).wait_send()
            for step in range(O):
                self.over(step).wait_send()
                self.across(step, 0).wait_send()
                self.across(step, 1).wait_send()

    def fetch(parts, sem):
        if sz.whole:
            copies = [local(buf.at[:, cols], dst, loc.at[sem + i]) for i, (buf, cols, dst) in enumerate(parts)]
            for copy in copies:
                copy.start()

            def wait():
                for copy in copies:
                    copy.wait()

            return wait
        for buf, cols, dst in parts:
            n = dst.shape[-1]

            def step(b):
                rows = span(b * QUADS * RP, QUADS * RP, QUADS * RP)
                move(buf.at[rows, cols], stage.at[:, pl.ds(0, n)], loc.at[sem])
                part = [stage[i * RP : i * RP + RP, :n].astype(F32)[:R] for i in range(QUADS)]
                dst[span(b * R4, R4, R4), :] = jnp.concatenate(part, axis=0).astype(BF)

            loop(O, step)
        return lambda: None

    def y_copy(src, dst, i):
        return remote(src, dst, s_y.at[i], r_y.at[i], over_y)

    QUERY, KEY, VALUE = pl.ds(0, QW), pl.ds(QW, sz.key), pl.ds(QW + sz.key, sz.key)
    REST = pl.ds(QW, 2 * sz.key)
    TT = 2 * T
    seq = TT // 2

    def head_cols(h):
        return pl.ds(h * HEAD_SIZE, HEAD_SIZE)

    def turn(u, sign, rows):
        return u * rope[0, rows, :] + sign * pltpu.roll(u, HEAD_SIZE // 2, 1) * rope[1, rows, :]

    gather_q = Gather(0, wq_ref, gq)
    gather_o = Gather(1, wo_ref, go)
    head = Chunk(None)

    gather_q.start()
    local(tok_ref, tk, loc.at[1]).start()
    head.a2a_start()
    Chunk(0).a2a_start()
    local(tok_ref, tk, loc.at[1]).wait()

    def norm_first(i):
        a = span(i * 32, 32, 32)
        values = tk[a, :].astype(F32)
        scale = lax.rsqrt(jnp.mean(values * values, axis=-1, keepdims=True) + norm_eps)
        xa[span(y * T + i * 32, 32, 32), :] = (values * scale * vec[0:1, :]).astype(BF)

    loop(T // 32, norm_first)
    own_half, other_half = span(y * T, T, T), span((1 - y) * T, T, T)
    y_copy(xa.at[own_half, :], xa.at[own_half, :], 0).start()
    sv[...] = jnp.zeros_like(sv)
    head.gather_own()
    gather_q.pass_on()
    gather_o.start()
    gather_q.pass_over(O - 1)
    Chunk(0).gather_own()
    head.gather_half()
    gather_q.wait()
    wq_v, wr_v, wo_v = pb.at[0], pb.at[1, :, pl.ds(0, 2 * sz.key)], pb.at[2]
    ready = fetch([(gq, QUERY, wq_v), (gq, REST, wr_v)], 1)
    Chunk(1).a2a_start()
    tok_start(cot_ref, cb, 1)
    local(cot_ref, cb.at[mine, :], loc.at[3]).start()
    y_copy(xa.at[own_half, :], xa.at[other_half, :], 0).wait_recv()
    ready()

    def project(i):
        rows = span(i * seq, seq, seq)
        lin = dot_rows(xa[rows, :], wq_v[...]) + vec[2:3, :QW]
        for h in range(HEADS):
            qkv[rows, head_cols(h)] = turn(lin[:, h * HEAD_SIZE : (h + 1) * HEAD_SIZE], 1.0, rows).astype(BF)
        lin = dot_rows(xa[rows, :], wr_v[...]) + vec[2:3, QW:GW]
        for h in range(sz.key // HEAD_SIZE):
            cut = slice(h * HEAD_SIZE, (h + 1) * HEAD_SIZE)
            qkv[rows, head_cols(HEADS + h)] = turn(lin[:, cut], 1.0, rows).astype(BF)
        qkv[rows, VALUE] = lin[:, sz.key :].astype(BF)

    loop(2, project)
    gather_o.pass_on()
    head.gather_far()
    Chunk(0).gather_half()
    SHARE = QW // sz.key

    def chances(h, part, queries):
        keys = slice(0, (part + 1) * seq)
        kcol = span(QW + (h // SHARE) * HEAD_SIZE, HEAD_SIZE, HEAD_SIZE)
        scores = dot_right(queries, qkv[keys, kcol]) * FACTOR
        row = lax.broadcasted_iota(jnp.int32, scores.shape, 0) + part * seq
        col = lax.broadcasted_iota(jnp.int32, scores.shape, 1)
        scores = jnp.where(row >= col, scores, -1e30)
        exponent = jnp.exp(scores - jnp.max(scores, axis=-1, keepdims=True))
        return exponent / jnp.sum(exponent, axis=-1, keepdims=True)

    def attend(h):
        qcol = span(h * HEAD_SIZE, HEAD_SIZE, HEAD_SIZE)
        vcol = span(QW + sz.key + (h // SHARE) * HEAD_SIZE, HEAD_SIZE, HEAD_SIZE)
        for part in range(2):
            rows = slice(part * seq, (part + 1) * seq)
            probs = chances(h, part, qkv[rows, qcol]).astype(BF)
            mh[rows, qcol] = dot_rows(probs, qkv[0 : (part + 1) * seq, vcol]).astype(BF)

    loop(HEADS, attend)
    gather_o.pass_over(O - 1)
    Chunk(1).gather_own()
    gather_o.wait()
    ready = fetch([(go, pl.ds(0, QW), wo_v)], 1)
    tok_next(cot_ref, cb, 1)
    ready()
    st[...] = dot_right(mh[other_half, :], wo_v[...]).astype(BF)
    y_copy(st, ar.at[0], 1).start()
    mid[...] = dot_right(mh[own_half, :], wo_v[...]) + tk[...].astype(F32)
    Chunk(2).a2a_start()
    Chunk(0).gather_far()
    Chunk(1).gather_half()
    tok_across(cb, 1)
    y_copy(st, ar.at[0], 1).wait_recv()

    def norm_second(i):
        a = span(i * 32, 32, 32)
        values = mid[a, :] + ar[0, a, :].astype(F32)
        mid[a, :] = values
        scale = lax.rsqrt(jnp.mean(values * values, axis=-1, keepdims=True) + norm_eps)
        xb[span(((x * 2 + y) * 2 + c) * T + i * 32, 32, 32), :] = (values * scale * vec[1:2, :]).astype(BF)

    loop(T // 32, norm_second)

    xsrc = xb.at[mine, :]
    tok_start(xsrc, xb, 0)
    local(cot_ref, cb.at[mine, :], loc.at[3]).wait()
    tok(cot_ref, cb, 1, 3).wait_recv()
    for n in range(3):
        tok_pass(cb, 1, n).wait_recv()
    head.gather_wait()
    head.load().start()
    Chunk(2).gather_own()
    head.load().wait()

    def tile(ch, rows, first):
        fk = ch.fk
        both = dot_rows(xb[rows, :], ch.wv[:, : 2 * fk])
        back = dot_rows(cb[rows, :], ch.wv[:, 2 * fk :])
        gate, upper = both[:, :fk], both[:, fk:]
        sigma = jax.nn.sigmoid(gate)
        silu = gate * sigma
        ch.hid[rows, :] = (silu * upper).astype(BF)
        gu[rows, :fk] = (back * upper * (sigma * (1.0 + gate * (1.0 - sigma)))).astype(BF)
        gu[rows, fk : 2 * fk] = (back * silu).astype(BF)
        for j in range(0, W, 512):
            cols = slice(j, j + 512)
            total = dot_right(gu[rows, : 2 * fk], ch.wv[cols, : 2 * fk])
            if first:
                nacc[rows, cols] = total
            else:
                nacc[rows, cols] = nacc[rows, cols] + total

    TD = 512 if W % 512 == 0 else 256

    def products(ch):
        fk = ch.fk

        def step(i):
            cols = span(i * TD, TD, TD)
            ch.pb[cols, : 2 * fk] = dot_left(xb[:, cols], gu[:, : 2 * fk]).astype(BF)
            ch.pb[cols, 2 * fk :] = dot_left(cb[:, cols], ch.hid[...]).astype(BF)

        loop(W // TD, step)

    tok(xsrc, xb, 0, 3).wait_recv()
    tile(head, chip_rows(*order[3]), True)
    tok_next(xsrc, xb, 0)
    tok_pass(xb, 0, 2).wait_recv()
    tile(head, chip_rows(*order[2]), True)
    Chunk(1).gather_far()
    Chunk(2).gather_half()
    tok_pass(xb, 0, 1).wait_recv()
    tile(head, chip_rows(*order[1]), True)
    tok_across(xb, 0)
    for kk in range(3, NF):
        Chunk(kk).a2a_start()
    Chunk(0).gather_wait()
    tok_pass(xb, 0, 0).wait_recv()
    tile(head, chip_rows(*order[0]), True)
    Chunk(0).load().start()
    products(head)
    head.line.first()

    def body(kk):
        ch, nxt = Chunk(kk), Chunk(lax.min(kk + 1, NF - 1))
        two, three = Chunk(lax.max(kk - 2, 0)), Chunk(lax.max(kk - 3, 0))
        last = kk == NF - 1
        later = Chunk(lax.min(kk + 3, NF - 1))
        pl.when(kk + 3 < NF)(later.gather_own)
        ch.load().wait()

        def visit(p):
            for n in range(3):
                pl.when(last & (p == n + 1))(lambda: sum_take(n, 0))
            pl.when((kk == 1) & (p == 1))(head.line.far_take)
            pl.when((kk == 2) & (p == 0))(head.line.cross_take)
            pl.when((kk >= 2) & (kk < NF - 1) & (p == 2))(two.line.far_take)
            pl.when((kk == 3) & (p == 0))(head.line.last_take)
            xx = jnp.where(p < 2, 1 - x, x)
            yy = jnp.where(p % 2 == 0, 1 - y, y)
            tile(ch, chip_rows(xx, yy), False)
            for n in range(4):
                pl.when(last & (p == n))(lambda: sum_pair(n, 0).start())
            for n in range(3):
                pl.when(last & (p == n + 1))(lambda: sum_give(n, 0))

            pl.when((kk == 1) & (p == 1))(head.line.far_give)
            pl.when((kk == 2) & (p == 0))(head.line.cross_give)
            pl.when((kk >= 2) & (kk < NF - 1) & (p == 2))(two.line.far_give)
            pl.when((kk == 3) & (p == 0))(head.finish_give)
            pl.when((kk + 3 < NF) & (p == 2))(later.gather_half)

        loop(4, visit)
        pl.when(last)(lambda: sum_take(3, 0))

        @pl.when(kk < NF - 1)
        def _():
            pl.when(kk == 0)(Chunk(1).gather_wait)
            pl.when(kk > 1)(nxt.gather_far)
            pl.when(kk > 0)(nxt.gather_wait)
            nxt.load().start()

        pl.when(kk >= 3)(three.line.cross_take)
        products(ch)
        ch.line.first()
        pl.when(kk >= 3)(three.line.cross_give)
        pl.when(last)(lambda: sum_give(3, 0))
        pl.when(kk == 0)(Chunk(2).gather_far)

    loop(NF, body)

    y_copy(st, ar.at[0], 1).wait_send()
    local(cot_ref, st, loc.at[1]).start()
    wo_b, wq_b = cb.at[pl.ds(0, W), pl.ds(0, QW)], xb.at[pl.ds(0, W), pl.ds(0, GW)]
    tok_sent(cot_ref, cb, 1)
    tok_sent(xsrc, xb, 0)
    ready = fetch([(go, pl.ds(0, QW), wo_b), (gq, pl.ds(0, GW), wq_b)], 2)
    local(cot_ref, st, loc.at[1]).wait()

    def back_second(a, grad):
        values = mid[a, :]
        scale = lax.rsqrt(jnp.mean(values * values, axis=-1, keepdims=True) + norm_eps)
        scaled = grad * vec[1:2, :]
        mean = jnp.mean(scaled * values, axis=-1, keepdims=True)
        total = st[a, :].astype(F32) + (scale * scaled - values * (scale * scale * scale) * mean)
        own[a, :] = total
        tk[a, :] = total.astype(BF)
        sv[1:2, :] = sv[1:2, :] + jnp.sum(grad * values * scale, axis=0, keepdims=True)

    def m_load(kk):
        return local(
            wagf.at[kk, :, pl.ds(2 * WIDE, WIDE)], wv.at[:, span(lax.rem(kk, 2) * WIDE, WIDE, WIDE)], loc.at[8],
        )

    move(wagh.at[:, pl.ds(2 * HK, HK)], wv.at[:, pl.ds(2 * WIDE, HK)], loc.at[0])
    m_load(0).start()

    def m_first(p):
        rows = span(p * TT, TT, TT)
        nacc[rows, :] = dot_right(hh[rows, :], wv[:, 2 * WIDE : 2 * WIDE + HK])

    loop(4, m_first)

    def m_chunk(kk):
        m_load(kk).wait()
        pl.when(kk + 1 < NF)(lambda: m_load(lax.min(kk + 1, NF - 1)).start())
        cut = span(lax.rem(kk, 2) * WIDE, WIDE, WIDE)

        def m_tile(p):
            rows = span(p * TT, TT, TT)
            for j in range(0, W, 512):
                cols = slice(j, j + 512)
                nacc[rows, cols] = nacc[rows, cols] + dot_right(hf[kk, rows, :], wv[cols, cut])

        loop(4, m_tile)

    loop(NF, m_chunk)
    for n in range(4):
        sum_pair(n, 1).start()
    Chunk(NF - 3).line.far_take()
    sum_close(0, back_second)
    ga[own_half, :] = tk[...]
    y_copy(ga.at[own_half, :], ga.at[own_half, :], 2).start()
    Chunk(NF - 3).line.far_give()
    for n in range(4):
        sum_take(n, 1)
    for n in range(4):
        sum_give(n, 1)
    ready()
    y_copy(ga.at[own_half, :], ga.at[other_half, :], 2).wait_recv()

    PER = 2 * WIDE // HEAD_SIZE

    def cell(h, level):
        return (level * 2 + h // PER) * TT, span(h % PER * HEAD_SIZE, HEAD_SIZE, HEAD_SIZE)

    grad_mixed = dot_rows(ga[...], wo_b[...]).astype(BF)
    for h in range(HEADS):
        row, cut = cell(h, 1)
        gu[pl.ds(row, TT), cut] = grad_mixed[:, h * HEAD_SIZE : (h + 1) * HEAD_SIZE]

    HR = 2 * LR
    tile_rows = R4 * 128 // math.gcd(R4, 128)
    quads = tile_rows // R4

    def spread_rows(i, values, store):
        for b in range(quads):
            for q_ in range(QUADS):
                rows = values[(b * QUADS + q_) * R : (b * QUADS + q_ + 1) * R]
                if not sz.whole:
                    rows = jnp.concatenate([rows, jnp.zeros((RP - R, rows.shape[1]), F32)], axis=0)
                where = ((q_ % 2) * 2 + q_ // 2) * O + i * quads + b
                store(span(where * RP, RP, RP), rows.astype(BF))

    out_cols = pl.ds(QW, QW)

    def out_products(i):
        cols = span(i * tile_rows, tile_rows, 128)
        values = dot_left(ga[:, cols], mh[...])

        def store(rows, part):
            cb[rows, out_cols] = part

        spread_rows(i, values, store)

    loop(W // tile_rows, out_products)

    class Part:
        def __init__(self, i, pieces, temps, cores, overs, col, near, out):
            self.i, self.pieces, self.temps, self.cores, self.overs = i, pieces, temps, cores, overs
            first = (c * 2 + x) * LR
            self.line = Line(
                NF + 1 + i, RP, [p.at[span(first, LR, RP), :] for p in pieces], col, near, out, temps
            )

        def to_core(self, k):
            rows = span((1 - c) * HR, HR, RP)
            return remote(
                self.pieces[k].at[rows, :], self.cores[k], s_pc.at[self.i + k], r_pc.at[self.i + k], core
            )

        def to_x(self, k):
            rows = span((c * 2 + 1 - x) * LR, LR, RP)
            return remote(
                self.pieces[k].at[rows, :], self.overs[k], s_px.at[self.i + k], r_px.at[self.i + k], over_x
            )

        def send_core(self):
            for k in range(len(self.pieces)):
                self.to_core(k).start()

        def take(self, copies, bufs, start, n):
            for k, p in enumerate(self.pieces):
                copies(k).wait_recv()
                local(bufs[k], self.temps[k].at[pl.ds(0, n), :], loc.at[4 + k]).start()
            for k, p in enumerate(self.pieces):
                local(bufs[k], self.temps[k].at[pl.ds(0, n), :], loc.at[4 + k]).wait()
                add_into(p.at[span(start, n, RP), :], self.temps[k], n)

        def send_x(self):
            self.take(self.to_core, self.cores, c * HR, HR)
            for k in range(len(self.pieces)):
                self.to_x(k).start()

        def send_along(self):
            self.take(self.to_x, self.overs, (c * 2 + x) * LR, LR)
            self.line.first()

        def sent(self):
            for k in range(len(self.pieces)):
                self.to_core(k).wait_send()
                self.to_x(k).wait_send()
            self.line.sent()

    NQ = GW // WIDE

    def side_part(side):
        ks = range(side * NQ // 2, (side + 1) * NQ // 2)
        temps = [xb.at[pl.ds((k // 2) * HR, HR), pl.ds(GW + (k % 2) * WIDE, WIDE)] for k in ks]

        def each(ref):
            return [ref.at[k] for k in ks]

        return Part(
            ks[0], each(hf), temps, each(rcq), each(rxq), each(colq), each(nearq), each(outq)
        )

    part_a, part_b = side_part(0), side_part(1)
    part_o = Part(
        NQ, [cb.at[:, out_cols]], [rt.at[:, pl.ds(0, QW)]], [rco], [rxo], [colo], [nearo], [outo]
    )
    part_o.send_core()
    Chunk(NF - 2).line.far_take()

    kv_sums = nacc.at[rows_of(*order[1], c), :]
    kv_sums[:, : 4 * HEAD_SIZE] = jnp.zeros((T, 4 * HEAD_SIZE), F32)

    def attend_back(h):
        qcol = span(h * HEAD_SIZE, HEAD_SIZE, HEAD_SIZE)
        row, cut = cell(h, 1)
        to_row, to_cut = cell(h, 0)
        for part in range(2):
            rows = slice(part * seq, (part + 1) * seq)
            keys = slice(0, (part + 1) * seq)
            queries = qkv[rows, qcol]
            probs = chances(h, part, queries)
            upstream = gu[span(row + part * seq, seq, seq), cut]
            grad_probs = dot_right(upstream, qkv[keys, VALUE])
            inner = jnp.sum(grad_probs * probs, axis=-1, keepdims=True)
            grad_scores = (probs * (grad_probs - inner)).astype(BF)
            grad_queries = dot_rows(grad_scores, qkv[keys, KEY]) * FACTOR
            gu[span(to_row + part * seq, seq, seq), to_cut] = turn(grad_queries, -1.0, rows).astype(BF)
            grad_keys = dot_left(grad_scores, queries) * FACTOR
            grad_values = dot_left(probs.astype(BF), upstream)
            for i in range(part + 1):
                kcut, vcut = head_cols(i), head_cols(2 + i)
                piece = slice(i * seq, (i + 1) * seq)
                kv_sums[:, kcut] = kv_sums[:, kcut] + grad_keys[piece]
                kv_sums[:, vcut] = kv_sums[:, vcut] + grad_values[piece]

    half_cols = 2 * WIDE

    def lin_products(side):
        def step(i):
            cols = span(i * tile_rows, tile_rows, 128)
            values = dot_left(xa[:, cols], gu[side * TT : (side + 1) * TT, :])

            def store(rows, part):
                hf[2 * side, rows, :] = part[:, :WIDE]
                hf[2 * side + 1, rows, :] = part[:, WIDE:]

            spread_rows(i, values, store)

        loop(W // tile_rows, step)

    def lin_back(start):
        return dot_right(
            gu[span(start, T, T), :], wq_b[:, :half_cols]
        ) + dot_right(gu[span(TT + start, T, T), :], wq_b[:, half_cols:])

    def heads_back(first, n):
        loop(n, lambda h: attend_back(first + h))

    heads_back(0, PER)
    Chunk(NF - 2).line.far_give()
    lin_products(0)
    part_a.send_core()
    part_o.send_x()
    heads_back(PER, HEADS - PER)
    for i in range(2):
        rows = slice(i * seq, (i + 1) * seq)
        row, cut = cell(HEADS, 0)
        gu[pl.ds(row + i * seq, seq), cut] = turn(kv_sums[:, head_cols(i)], -1.0, rows).astype(BF)
        row, cut = cell(HEADS + 1, 0)
        gu[pl.ds(row + i * seq, seq), cut] = kv_sums[:, head_cols(2 + i)].astype(BF)
    lin_products(1)
    part_b.send_core()
    part_a.send_x()
    Chunk(NF - 3).line.cross_take()
    st[...] = lin_back((1 - y) * T).astype(BF)
    y_copy(st, ar.at[1], 3).start()
    Chunk(NF - 3).line.cross_give()
    part_o.send_along()
    part_b.send_x()
    Chunk(NF - 4).line.last_take()
    grad_lin = nacc.at[rows_of(*order[0], c), :]
    grad_lin[...] = lin_back(y * T)
    for side in range(2):
        cut = slice(side * half_cols, (side + 1) * half_cols)
        sums = jnp.sum(gu[side * TT : (side + 1) * TT, :].astype(F32), axis=0, keepdims=True)
        sv[2:3, cut] = sums
    Chunk(NF - 4).finish_give()
    part_a.send_along()
    Chunk(NF - 2).line.cross_take()
    tokens_again = ga.at[other_half, :]
    y_copy(ga.at[own_half, :], ga.at[own_half, :], 2).wait_send()
    local(tok_ref, tokens_again, loc.at[1]).start()
    Chunk(NF - 2).line.cross_give()
    part_b.send_along()
    Chunk(NF - 3).finish()
    Chunk(NF - 1).line.far_take()
    Chunk(NF - 1).line.far_give()
    part_o.line.far_take()
    part_o.line.far_give()
    part_a.line.far_take()
    part_a.line.far_give()
    local(tok_ref, tokens_again, loc.at[1]).wait()
    y_copy(st, ar.at[1], 3).wait()

    def back_first(i):
        a = span(i * 32, 32, 32)
        values = tokens_again[a, :].astype(F32)
        grad = grad_lin[a, :] + ar[1, a, :].astype(F32)
        scale = lax.rsqrt(jnp.mean(values * values, axis=-1, keepdims=True) + norm_eps)
        scaled = grad * vec[0:1, :]
        mean = jnp.mean(scaled * values, axis=-1, keepdims=True)
        own[a, :] = own[a, :] + (scale * scaled - values * (scale * scale * scale) * mean)
        sv[0:1, :] = sv[0:1, :] + jnp.sum(grad * values * scale, axis=0, keepdims=True)

    loop(T // 32, back_first)
    local(own, gtok_ref, loc.at[1]).start()

    def small(dq, dy):
        to_q, to_y = lax.rem(q + dq, QUADS), lax.rem(y + dy, 2)
        return remote(
            sv, svr.at[q * 2 + y], s_v.at[dq * 2 + dy], r_v.at[q * 2 + y], at(o, to_q, to_y)
        )

    def small_from(dq, dy):
        from_q, from_y = lax.rem(q + dq, QUADS), lax.rem(y + dy, 2)
        return remote(
            sv, svr.at[from_q * 2 + from_y], s_v.at[dq * 2 + dy],
            r_v.at[from_q * 2 + from_y], at(o, from_q, from_y),
        )

    def small_along(step):
        return remote(sv, svz.at[o], s_vz.at[step], r_vz.at[o], at(lax.rem(o + step, O), q, y))

    def small_along_from(step):
        place = lax.rem(o + step, O)
        return remote(sv, svz.at[place], s_vz.at[step], r_vz.at[place], at(place, q, y))

    peers = [(dq, dy) for dq in range(QUADS) for dy in range(2) if dq or dy]
    for dq, dy in peers:
        small(dq, dy).start()
    svr[q * 2 + y] = sv[...]

    part_b.line.far_take()
    part_b.line.far_give()
    Chunk(NF - 2).finish()

    def layer_out(a, total):
        tk[a, :] = (mid[a, :] + total).astype(BF)

    Chunk(NF - 1).line.cross_take()
    Chunk(NF - 1).line.cross_give()
    for dq, dy in peers:
        small_from(dq, dy).wait_recv()
        small(dq, dy).wait_send()
    gains = svr[0]
    for i in range(1, 2 * QUADS):
        gains = gains + svr[i]
    biases = svr[y]
    for i in range(1, QUADS):
        biases = biases + svr[i * 2 + y]
    sv[...] = gains
    sv[2:3, :] = biases[2:3, :]
    for step in range(1, O):
        small_along(step).start()
    svz[o] = sv[...]
    for part in (part_o, part_a, part_b):
        part.line.cross_take()
        part.line.cross_give()
    sum_close(1, layer_out)
    local(tk, mixed_ref, loc.at[2]).start()
    head.collect()
    loop(NF - 1, lambda kk: Chunk(kk).collect())
    Chunk(NF - 1).finish()
    for step in range(1, O):
        small_along_from(step).wait_recv()
        small_along(step).wait_send()
    total = svz[0]
    for i in range(1, O):
        total = total + svz[i]
    sv[...] = total
    local(sv, sums_ref, loc.at[8]).start()
    low = span(3 * PIECES * RP, RP, RP)
    lower = span((3 * PIECES + 1) * RP, RP, RP)
    for part in (part_o, part_a, part_b):
        part.line.last_take()
        part.line.last_give()
    nacc[low, :QW] = part_o.line.block(0, o)[...].astype(F32)
    for side, part in enumerate((part_a, part_b)):
        for k in range(NQ // 2):
            cut = slice((side * NQ // 2 + k) * WIDE, (side * NQ // 2 + k + 1) * WIDE)
            nacc[lower, cut] = part.line.block(k, o)[...].astype(F32)
    outputs = [
        local(nacc.at[low, pl.ds(0, QW)], gao_ref, loc.at[3]),
        local(nacc.at[lower, QUERY], gwq_ref, loc.at[4]),
        local(nacc.at[lower, KEY], gwk_ref, loc.at[5]),
        local(nacc.at[lower, VALUE], gwv_ref, loc.at[6]),
    ]
    for copy in outputs:
        copy.start()
    Chunk(NF - 1).collect()
    for m in range(3):
        for j in range(PIECES):
            n = min(W, sz.hidden - j * W)
            here = nacc.at[pl.ds((m * PIECES + j) * RP, RP), pl.ds(0, n)]
            outputs.append(local(here, gw_refs[m].at[:, pl.ds(j * W, n)], loc.at[20 + m * PIECES + j]))
            outputs[-1].start()

    for copy in outputs:
        copy.wait()
    gather_q.sent()
    gather_o.sent()
    y_copy(xa.at[own_half, :], xa.at[own_half, :], 0).wait_send()
    part_o.sent()
    part_a.sent()
    part_b.sent()
    head.finished()
    loop(NF, lambda kk: Chunk(kk).finished())
    local(own, gtok_ref, loc.at[1]).wait()
    local(tk, mixed_ref, loc.at[2]).wait()
    local(sv, sums_ref, loc.at[8]).wait()


def layer(sz, tokens, cotangent, wq, wo, wh, wg, wu, wd, vec, rope):
    O, NF, T = sz.outer, sz.full, sz.tokens
    H = O // 2
    HK, W, RP = sz.head, sz.wide, sz.pad
    R4, LR = QUADS * sz.rows, O * sz.pad
    HR = 2 * LR
    QW, GW = sz.query, sz.query + 2 * sz.key
    NQ = GW // WIDE
    PT = 2 * QUADS * T
    NL = NF + 1 + NQ + 1
    A, B = 3 * HK, 3 * WIDE
    PIECES = -(-sz.hidden // W)
    out = jax.ShapeDtypeStruct
    outs = [
        out((RP, sz.hidden), F32),
        out((RP, sz.hidden), F32),
        out((RP, sz.hidden), F32),
        out((RP, QW), F32),
        out((RP, sz.key), F32),
        out((RP, sz.key), F32),
        out((RP, QW), F32),
        out((T, W), BF),
        out((T, W), F32),
        out((8, W), F32),
        out((QUADS, RP, A), BF),
        out((NF, QUADS, RP, B), BF),
        out((W, A), BF),
        out((NF, W, B), BF),
        out((H, H * R4, A), BF),
        out((NF, H, H * R4, B), BF),
        out((H, R4, A), BF),
        out((NF, H, R4, B), BF),
        out((H * R4, A), BF),
        out((NF, H * R4, B), BF),
        out((2, 4, T, W), F32),
        out((2, 3, T, W), BF),
        out((sz.dp * RP, GW), BF),
        out((sz.dp * RP, QW), BF),
        out((NQ, HR, WIDE), BF),
        out((HR, QW), BF),
        out((NQ, LR, WIDE), BF),
        out((LR, QW), BF),
        out((NQ, H, H * RP, WIDE), BF),
        out((H, H * RP, QW), BF),
        out((NQ, H, RP, WIDE), BF),
        out((H, RP, QW), BF),
        out((NQ, H * RP, WIDE), BF),
        out((H * RP, QW), BF),
    ]
    if not sz.whole:
        outs += [out((QUADS, RP, A), BF), out((NF, QUADS, RP, B), BF)]
    dma = pltpu.SemaphoreType.DMA
    vm = pltpu.VMEM
    scratch = [
        vm((PT, W), BF),
        vm((PT, W), BF),
        vm((PT, W), F32),
        vm((W, B), BF),
        vm((W, A), BF),
        vm((NF, W, B), BF),
        vm((PT, HK), BF),
        vm((NF, PT, WIDE), BF),
        vm((PT, 2 * WIDE), BF),
        vm((3, T, W), BF),
        vm((T, W), BF),
        vm((max(W // 2, HR), B), BF),
        vm((T, W), F32),
        vm((2 * T, W), BF),
        vm((2 * T, GW), BF),
        vm((2 * T, QW), BF),
        vm((2, T, W), BF),
        vm((T, W), BF),
        vm((T, W), F32),
        vm((2 * T, W), BF),
        vm((8, W), F32),
        vm((2 * QUADS, 8, W), F32),
        vm((O, 8, W), F32),
        dma((NF + 1, 3, 4)),
        dma((NF + 1, 3, 3)),
        dma((NF + 1, H)),
        dma((NF + 1, H)),
        dma((NF + 1,)),
        dma((NF + 1,)),
        dma((NF + 1, H)),
        dma((NF + 1,)),
        dma((NL,)),
        dma((NL, H)),
        dma((NL, H)),
        dma((NL, H)),
        dma((NL,)),
        dma((NL,)),
        dma((NF + 1, 4)),
        dma((NF + 1, 3)),
        dma((2, 9)),
        dma((2, 9)),
        dma((2, 7)),
        dma((2, 7)),
        dma((4,)),
        dma((4,)),
        dma((2, O)),
        dma((2, O)),
        dma((2, O)),
        dma((2, O)),
        dma((2, 2, O)),
        dma((2, 2, O)),
        dma((NQ + 1,)),
        dma((NQ + 1,)),
        dma((NQ + 1,)),
        dma((NQ + 1,)),
        dma((2 * QUADS,)),
        dma((2 * QUADS,)),
        dma((O,)),
        dma((O,)),
        dma((20 + 3 * PIECES,)),
    ]
    if not sz.whole:
        scratch += [vm((QUADS * RP, max(B, GW)), BF), vm((R4, B), BF)]
    any_spec = pl.BlockSpec(memory_space=pl.ANY)
    vmem_spec = pl.BlockSpec(memory_space=pltpu.VMEM)
    results = pl.pallas_call(
        lambda *refs: layer_kernel(sz, *refs),
        out_shape=outs,
        in_specs=[any_spec] * 8 + [vmem_spec] * 2,
        out_specs=[any_spec] * len(outs),
        scratch_shapes=scratch,
        compiler_params=pltpu.CompilerParams(
            collective_id=0, has_side_effects=True, vmem_limit_bytes=64 << 20
        ),
        name="layer",
    )(tokens, cotangent, wq, wo, wh, wg, wu, wd, vec, rope)
    return results[:10]


def per_device(
    sz,
    tokens,
    w_query,
    key_weight,
    value_weight,
    b_query,
    key_bias,
    value_bias,
    w_out,
    gain_attn,
    gain_mlp,
    w_gate,
    w_up,
    w_down,
    cotangent,
):
    rows = sz.rows
    more = sz.pad - sz.rows

    def fill(values):
        return jnp.pad(values, ((0, more), (0, 0))) if more else values

    wg, wu, wd = fill(w_gate), fill(w_up), fill(w_down.T)
    start = sz.hidden - sz.rest
    wh = jnp.stack([wg[:, start:], wu[:, start:], wd[:, start:]], axis=1)
    wh = jnp.pad(wh, ((0, 0), (0, 0), (0, QUADS * sz.head - sz.rest)))
    wh = wh.reshape(sz.pad, 3, QUADS, sz.head).transpose(2, 0, 1, 3)
    wh = wh.reshape(QUADS, sz.pad, 3 * sz.head)
    wq = jnp.concatenate([w_query, key_weight, value_weight], axis=1)
    wq, wo = fill(wq), fill(w_out.T)
    bias = jnp.concatenate([b_query, key_bias, value_bias]).astype(F32)
    bias = jnp.pad(bias, (0, sz.wide - bias.shape[0]))
    vec = jnp.stack([gain_attn.astype(F32), gain_mlp.astype(F32), bias])
    vec = jnp.pad(vec, ((0, 5), (0, 0)))
    rope = jnp.asarray(rope_tables(SEQUENCE_TOKENS, HEAD_SIZE))

    grad_gate, grad_up, grad_down, grad_q, grad_k, grad_v, grad_o, mixed, grad_tokens, sums = layer(
        sz, tokens, cotangent, wq, wo, wh, wg, wu, wd, vec, rope
    )
    cuts = (sz.query, sz.query + sz.key, sz.query + 2 * sz.key)
    return (
        mixed,
        grad_tokens,
        grad_q[:rows],
        grad_k[:rows],
        grad_v[:rows],
        sums[2, : cuts[0]],
        sums[2, cuts[0] : cuts[1]],
        sums[2, cuts[1] : cuts[2]],
        grad_o[:rows].T,
        sums[0],
        sums[1],
        grad_gate[:rows],
        grad_up[:rows],
        grad_down[:rows].T,
    )


def solution(mesh):
    dp = mesh.shape["dp"]

    def whole(*args):
        def shard(*blocks):
            tokens, w_query, key_weight, w_gate = blocks[0], blocks[1], blocks[2], blocks[10]
            sz = Sizes(dp, w_gate.shape, tokens.shape[0], w_query.shape[1], key_weight.shape[1])
            return per_device(sz, *blocks)

        return jax.shard_map(
            shard, mesh=mesh, in_specs=in_specs, out_specs=out_specs, check_vma=False
        )(*args)

    in_specs = (
        P(("dp", "tensor"), None),
        P("dp", "tensor"),
        P("dp", "tensor"),
        P("dp", "tensor"),
        P("tensor"),
        P("tensor"),
        P("tensor"),
        P("tensor", "dp"),
        P(),
        P(),
        P("dp", "tensor"),
        P("dp", "tensor"),
        P("tensor", "dp"),
        P(("dp", "tensor"), None),
    )
    out_specs = (
        P(("dp", "tensor"), None),
        P(("dp", "tensor"), None),
        P("dp", "tensor"),
        P("dp", "tensor"),
        P("dp", "tensor"),
        P("tensor"),
        P("tensor"),
        P("tensor"),
        P("tensor", "dp"),
        P(),
        P(),
        P("dp", "tensor"),
        P("dp", "tensor"),
        P("tensor", "dp"),
    )
    return whole
```
